512 devices in a mesh: tm: 8 (over y, core), utt: 64 (over x, z).
Axes of the slice: x: 4, y: 4, z: 16, core: 2. Of those that a mesh axis runs over, the one named last changes fastest.
Arguments:
- encoder: bfloat16 [128, 512, 512], P('utt', 'tm'), may hold values from -16 to 16
- predictor: bfloat16 [128, 65, 512], P('utt'), may hold values from -6 to 6
- starts: int32 [128, 512], P('utt', 'tm'), may hold values from 0 to 49, as said below
- frame_lengths: int32 [128], P('utt'), may hold values from 256 to 512, as said below
- label_lengths: int32 [128], P('utt'), may hold values from 32 to 64, as said below
- labels: int32 [128, 64], P('utt'), may hold values from 1 to 499
- w_out: bfloat16 [512, 500], P('utt'), may hold values from -7 to 7
Outputs:
- losses: float32 [128], P('utt')
- grad_encoder: bfloat16 [128, 512, 512], P('utt', 'tm')
- grad_predictor: float32 [128, 65, 512], P('utt')
- grad_w_out: float32 [512, 500], P('utt')
The draws below stay inside these ranges and needn't reach their ends.
Inputs may be any that keep to these rules, and one draw needn't show every extreme that they name: `frame_lengths`: some utterance has all 512 frames. `label_lengths`: some utterance has 64 labels. starts[b, 0] = 0; starts never falls along frames and rises by at most 15 from one frame to the next; the ranges hold a complete path of blanks and emissions from label 0 at frame 0 to label label_lengths[b] after the last frame, and every range from frame frame_lengths[b] - 1 on contains label_lengths[b].
All inputs are finite; a program needn't handle non-finite values.
Results may differ from the reference program's by a relative error of at most 0.012.
Values may be sent and summed in bfloat16 or wider, within the bound.
No kernel may reach another device: no remote copies, remote signals or barrier semaphores. Data moves between devices by JAX's collectives and lax.ppermute only.
A program may use at most 64 MiB of HBM per device.

```python
import jax
import jax.numpy as jnp
from jax import lax

J = 512
V = 500
S = 16
UMAX = 64
B = 128
NT = 512
UP = 65


def shared_lengths(key):
    frame_counts = jax.random.randint(jax.random.fold_in(key, 101), (B,), NT // 2, NT + 1)
    longest_frames = jax.random.randint(jax.random.fold_in(key, 103), (), 0, B)
    frame_counts = jnp.where(jnp.arange(B) == longest_frames, NT, frame_counts)
    label_counts = jax.random.randint(jax.random.fold_in(key, 102), (B,), UMAX // 2, UMAX + 1)
    longest_labels = jax.random.randint(jax.random.fold_in(key, 104), (), 0, B)
    label_counts = jnp.where(jnp.arange(B) == longest_labels, UMAX, label_counts)
    return (frame_counts.astype(jnp.int32), label_counts.astype(jnp.int32))


def draw_frame_lengths(key, part):
    frame_counts, label_counts = shared_lengths(key)
    return frame_counts


def draw_label_lengths(key, part):
    frame_counts, label_counts = shared_lengths(key)
    return label_counts


def draw_starts(key, part):
    frame_counts, label_counts = shared_lengths(key)
    key = jax.random.fold_in(key, 3)
    jitter_key, slack_key = jax.random.split(key)
    frame_ids = jnp.arange(NT, dtype=jnp.int32)[None, :]
    baseline = label_counts[:, None] * (frame_ids + 1) // frame_counts[:, None]
    jitter = jax.random.randint(jitter_key, (B, NT), -3, 4)
    aligned = jnp.clip(baseline + jitter, 0, label_counts[:, None])
    aligned = lax.cummax(aligned, axis=1)
    aligned = jnp.where(frame_ids >= frame_counts[:, None] - 1, label_counts[:, None], aligned)
    previous = jnp.concatenate([jnp.zeros((B, 1), jnp.int32), aligned[:, :-1]], axis=1)
    rises = aligned - previous
    slack = jax.random.randint(slack_key, (B, NT), 0, S - rises)
    lowest = lax.cummax(jnp.maximum(aligned - rises - slack, 0), axis=1)
    return jnp.minimum(lowest, UP - S).astype(jnp.int32)


def draw_w_out(key, part):
    key = jax.random.fold_in(key, 7)
    base_key = jax.random.fold_in(key, 0)
    values = jax.random.normal(base_key, (J, V), jnp.float32) * 0.2
    return jnp.clip(values, -7.0, 7.0).astype(jnp.bfloat16)


def with_ends(result, own_key, low, high):
    index_at = [jax.random.randint(jax.random.fold_in(own_key, axis), (), 0, length) for axis, length in enumerate(result.shape)]
    longest = result.shape.index(max(result.shape))
    next_to = index_at[:longest] + [(index_at[longest] + 1) % result.shape[longest]] + index_at[longest + 1:]
    return result.at[tuple(index_at)].set(low).at[tuple(next_to)].set(high)


def raised(result, stream_key, source, target, blocks, factor):
    owner, partner = [(jnp.arange(result.shape[position]) // (result.shape[position] // blocks)).reshape([-1 if axis == position else 1 for axis in range(result.ndim)]) for position in (source, target)]
    chosen = jax.random.permutation(stream_key, blocks)[partner]
    strong = (owner == chosen) | (owner == (partner + blocks // 2) % blocks)
    return jnp.where(strong, factor * result, result)


def block_levels(key, shape, shards, low, high):
    loudness, own = 1.0, jax.random.fold_in(key, 6)
    for dim, shards_of in shards:
        draws = jnp.exp(jax.random.uniform(jax.random.fold_in(own, dim), (shards_of,), jnp.float32, low / len(shards), high / len(shards)))
        loudness = loudness * jnp.repeat(draws, shape[dim] // shards_of).reshape([-1 if axis == dim else 1 for axis in range(len(shape))])
    return loudness


def bell_draw(own_key, dims, spread, limit, cuts=(), kind=jnp.bfloat16):
    values = spread * jax.random.normal(own_key, dims, jnp.float32)
    if cuts:
        values = values * block_levels(own_key, dims, cuts, -0.22, 0.18)
    return jnp.clip(values, -limit, limit).astype(kind)


def heavy_noise(rng, shape, width, limit, shards, heavy, held_as=jnp.bfloat16):
    values = width * jax.random.normal(rng, shape, jnp.float32)
    if shards:
        values = values * block_levels(rng, shape, shards, -0.22, 0.18)
    return jnp.clip(raised(values, jax.random.fold_in(rng, 3), *heavy), -limit, limit).astype(held_as)


def setup_inputs(seed: int = 0) -> dict:
    streams_of = jax.random.split(jax.random.key(seed), 8)
    encoder = heavy_noise(streams_of[0], (B, NT, J), 1.0, 16.0, ((0, 64), (1, 8)), (0, 2, 64, 4.0))
    predictor = bell_draw(streams_of[1], (B, UP, J), 1.0, 6.0, ((0, 64),))
    starts = draw_starts(jax.random.fold_in(streams_of[7], 71), 0)
    frame_lengths = draw_frame_lengths(jax.random.fold_in(streams_of[7], 71), 0)
    label_lengths = draw_label_lengths(jax.random.fold_in(streams_of[7], 71), 0)
    labels = with_ends(jax.random.randint(streams_of[5], (B, UMAX), 1, V), jax.random.fold_in(streams_of[5], 1), 1, V - 1).astype(jnp.int32)
    w_out = draw_w_out(jax.random.fold_in(streams_of[7], 71), 0)
    return {"encoder": encoder, "predictor": predictor, "starts": starts, "frame_lengths": frame_lengths, "label_lengths": label_lengths, "labels": labels, "w_out": w_out}


masked_log = -1e+30

def log_identity(size):
    diagonal = jnp.arange(size)[:, None] == jnp.arange(size)[None, :]
    return jnp.where(diagonal, jnp.float32(0.0), jnp.float32(masked_log))

def log_product(former, latter):
    return jax.nn.logsumexp(former[..., :, :, None] + latter[..., None, :, :], axis=-2)

def frame_matrices(blank_lp, emit_lp, shifts):
    size = blank_lp.shape[-1]
    places = jnp.arange(size, dtype=jnp.int32)
    entries = places - shifts[..., None]
    inside = (entries[..., :, None, None] <= places) & (places < places[:, None])
    spans = lax.optimization_barrier(jnp.sum(jnp.where(inside, emit_lp[..., None, None, :], jnp.float32(0.0)), axis=-1))
    usable = (entries[..., :, None] >= 0) & (entries[..., :, None] <= places)
    return jnp.where(usable, spans + blank_lp[..., None, :], jnp.float32(masked_log))

def chain_product(matrices):
    while matrices.shape[-3] > 1:
        if matrices.shape[-3] % 2:
            padding = jnp.broadcast_to(log_identity(matrices.shape[-1]), matrices[..., :1, :, :].shape)
            matrices = jnp.concatenate([matrices, padding], axis=-3)
        matrices = log_product(matrices[..., 0::2, :, :], matrices[..., 1::2, :, :])
    return matrices[..., 0, :, :]

def select_entry(values, index):
    places = jnp.arange(values.shape[-1], dtype=jnp.int32)
    return lax.optimization_barrier(jnp.sum(jnp.where(places == index[..., None], values, jnp.float32(0.0)), axis=-1))

def reference(encoder, predictor, starts, frame_lengths, label_lengths, labels, w_out):
    offsets = jnp.arange(S, dtype=jnp.int32)
    vocab_ids = jnp.arange(V, dtype=jnp.int32)

    def one_utterance(weight_total, inputs):
        enc_rows, pred_rows, start_row, frame_len, label_len, label_row = inputs
        window_rows = start_row[:, None] + offsets
        picked = jnp.take(pred_rows, window_rows, axis=0)
        summed = enc_rows[:, None, :].astype(jnp.float32) + picked.astype(jnp.float32)
        hidden = jnp.tanh(summed).astype(jnp.bfloat16).reshape(NT * S, J)
        logits = jnp.dot(hidden, w_out, preferred_element_type=jnp.float32)
        log_probs = jax.nn.log_softmax(logits, axis=-1)
        label_ids = jnp.take(label_row, jnp.minimum(window_rows, UMAX - 1), axis=0).reshape(-1)
        is_label = vocab_ids == label_ids[:, None]
        blank_lp = log_probs[:, 0].reshape(NT, S)
        emit_lp = lax.optimization_barrier(jnp.sum(jnp.where(is_label, log_probs, jnp.float32(0.0)), axis=-1)).reshape(NT, S)
        live = jnp.arange(NT, dtype=jnp.int32)[:, None] < frame_len
        blank_lp = jnp.where(live, blank_lp, jnp.float32(0.0))
        emit_lp = jnp.where(live & (window_rows < label_len), emit_lp, jnp.float32(masked_log))
        previous = jnp.concatenate([jnp.zeros((1,), jnp.int32), start_row[:-1]])
        shifts = start_row - previous
        final_place = label_len - start_row[-1]

        def whole_chain(blanks, emits):
            product = chain_product(frame_matrices(blanks, emits, shifts))
            return select_entry(product[0], final_place)
        log_total, pull_back = jax.vjp(whole_chain, blank_lp, emit_lp)
        grad_blank, grad_emit = pull_back(-jnp.ones_like(log_total))
        coeff = jnp.where(is_label, grad_emit.reshape(-1)[:, None], jnp.float32(0.0))
        coeff = coeff + jnp.where(vocab_ids == 0, grad_blank.reshape(-1)[:, None], jnp.float32(0.0))
        probs = jnp.exp(log_probs)
        grad_logits = (coeff - probs * lax.optimization_barrier(jnp.sum(coeff, axis=-1, keepdims=True))).astype(jnp.bfloat16)
        grad_hidden = jnp.einsum('rv,jv->rj', grad_logits, w_out, preferred_element_type=jnp.float32)
        hidden_wide = hidden.astype(jnp.float32)
        grad_summed = grad_hidden * (1.0 - hidden_wide * hidden_wide)
        grad_enc = lax.optimization_barrier(jnp.sum(grad_summed.reshape(NT, S, J), axis=1)).astype(jnp.bfloat16)
        grad_pred = jax.ops.segment_sum(grad_summed, window_rows.reshape(-1), num_segments=UP)
        weight_term = jnp.einsum('rj,rv->jv', hidden, grad_logits, preferred_element_type=jnp.float32)
        losses_one = -log_total / frame_len.astype(jnp.float32)
        return (weight_total + weight_term, (losses_one, grad_enc, grad_pred))
    weight_total, outputs = lax.scan(one_utterance, jnp.zeros((J, V), jnp.float32), (encoder, predictor, starts, frame_lengths, label_lengths, labels))
    losses, grad_encoder, grad_predictor = outputs
    return (losses, grad_encoder, grad_predictor, weight_total)
```

```python
import functools

import jax
import jax.numpy as jnp
from jax import lax
from jax.experimental import pallas as pl
from jax.experimental.pallas import tpu as pltpu
from jax.sharding import PartitionSpec as P

S = 16
LANES = 128
GROUP = 4
STEPS = S // GROUP
WIDE = GROUP * LANES
PRED_PAD = 80
PRED_SHARE = 17
PRED_SLOT = 32
VMEM_BYTES = 40 * 2**20

masked_log = -1e30

F32 = jnp.float32
BF16 = jnp.bfloat16

NT_DIMS = (((1,), (1,)), ((), ()))


def lane_ids(shape=(1, LANES)):
    return lax.broadcasted_iota(jnp.int32, shape, 1)


def row_ids(shape):
    return lax.broadcasted_iota(jnp.int32, shape, 0)


def per_lane(half, low, high):
    return jnp.where(lane_ids() < half, low, high)


def rows_to_lanes(pair):
    return jnp.concatenate([pair[0:1, :], pair[1:2, :]], axis=1)


def rowwise_logsumexp(terms):
    top = functools.reduce(jnp.maximum, terms)
    total = functools.reduce(lambda a, b: a + b, [jnp.exp(t - top) for t in terms])
    return top + jnp.log(total)


def vector_times(vector, matrix):
    return rowwise_logsumexp([vector[i : i + 1, :] + matrix[i] for i in range(S)])


def times_vector(matrix, vector, rows_ref):
    for i in range(S):
        terms = matrix[i] + vector
        top = jnp.max(terms, axis=0, keepdims=True)
        total = jnp.sum(jnp.exp(terms - top), axis=0, keepdims=True)
        rows_ref[i : i + 1, :] = top + jnp.log(total)
    return rows_ref[...]


def span_rows(blank, emit):
    places = row_ids((S, LANES))
    spans = jnp.zeros((S, LANES), F32)
    rows = [None] * S
    for e in reversed(range(S)):
        spans = jnp.where(places > e, spans + emit[e : e + 1, :], 0.0)
        rows[e] = jnp.where(places >= e, spans + blank, masked_log)
    return rows


def hidden_kernel(starts_ref, labels_ref, enc_ref, pred_ref, hidden_ref, label_ref, enc_t, pred_t, stack):
    step = pl.program_id(0)
    half = starts_ref.shape[1]
    starts = rows_to_lanes(starts_ref[...])

    @pl.when(step == 0)
    def _():
        enc_t[...] = jnp.transpose(enc_ref[...].astype(F32))
        stack[...] = jnp.zeros_like(stack)
        rows = pred_ref.shape[1]
        stack[0:rows, :] = pred_ref[0].astype(F32)
        stack[PRED_PAD : PRED_PAD + rows, :] = pred_ref[1].astype(F32)
        pred_t[...] = jnp.transpose(stack[...]).astype(BF16)
        cap = labels_ref.shape[1]
        labels = labels_ref[...].astype(F32)
        table = [jnp.transpose(jnp.broadcast_to(labels[b : b + 1, :], (LANES, cap))) for b in range(2)]
        table = jnp.where(lane_ids((cap, LANES)) < half, table[0], table[1])
        places = row_ids((cap, LANES))
        for k in range(S):
            wanted = jnp.minimum(starts + k, cap - 1)
            label_ref[k : k + 1, :] = jnp.sum(
                jnp.where(places == wanted, table, 0.0), axis=0, keepdims=True
            ).astype(jnp.int32)

    base = starts + per_lane(half, 0, PRED_PAD) + step * GROUP
    wanted = jnp.concatenate([base + k for k in range(GROUP)], axis=1)
    match = (row_ids((2 * PRED_PAD, WIDE)) == wanted).astype(BF16)
    picked = jnp.dot(pred_t[...], match, preferred_element_type=F32)
    for k in range(GROUP):
        part = slice(k * LANES, (k + 1) * LANES)
        hidden_ref[:, part] = jnp.tanh(enc_t[...] + picked[:, part]).astype(BF16)


def forward_kernel(
    piece,
    vocab,
    starts_ref,
    prior_ref,
    frames_ref,
    labels_len_ref,
    block_ref,
    label_ref,
    gathered_ref,
    hidden_ref,
    exps_ref,
    weights_ref,
    lps_ref,
    tree_ref,
    payload_ref,
    weights_t,
    root,
):
    step = pl.program_id(0)
    width = gathered_ref.shape[0]

    @pl.when(step == 0)
    def _():
        own = row_ids((width, width))
        got = lane_ids((width, width))
        share = width // 8
        source = (got % share) // piece * (8 * piece) + got // share * piece + got % piece
        turn = (own == source).astype(BF16)
        weights = jnp.dot(turn, gathered_ref[...], preferred_element_type=F32)
        weights_ref[...] = weights.astype(BF16)
        weights_t[...] = jnp.transpose(weights).astype(BF16)

    logits = jnp.dot(weights_t[...], hidden_ref[...], preferred_element_type=F32)
    padded = logits.shape[0]
    edge = padded - 16
    tail = jnp.where(row_ids((16, WIDE)) < vocab - edge, logits[edge:], masked_log)
    logits = jnp.concatenate([logits[:edge], tail], axis=0)
    top = jnp.max(logits, axis=0, keepdims=True)
    exps = jnp.exp(logits - top)
    exps_ref[...] = exps
    total = jnp.sum(exps, axis=0, keepdims=True)
    norm = top + jnp.log(total)
    scale = 1.0 / total
    names = jnp.concatenate([label_ref[pl.ds(step * GROUP + k, 1), :] for k in range(GROUP)], axis=1)
    emit = jnp.sum(jnp.where(row_ids((padded, WIDE)) == names, logits, 0.0), axis=0, keepdims=True) - norm
    blank = logits[0:1, :] - norm
    for k in range(GROUP):
        part = slice(k * LANES, (k + 1) * LANES)
        row = pl.ds(step * GROUP + k, 1)
        lps_ref[0, row, :] = blank[:, part]
        lps_ref[1, row, :] = emit[:, part]
        lps_ref[2, row, :] = scale[:, part]

    @pl.when(step == STEPS - 1)
    def _():
        half = starts_ref.shape[1]
        lanes = lane_ids()
        starts = rows_to_lanes(starts_ref[...])
        frame = block_ref[0] * half + lanes % half
        live = frame < per_lane(half, frames_ref[0], frames_ref[1])
        limit = per_lane(half, labels_len_ref[0], labels_len_ref[1])
        allowed = live & (row_ids((S, LANES)) + starts < limit)
        blank = jnp.where(live, lps_ref[0], 0.0)
        emit = jnp.where(allowed, lps_ref[1], masked_log)
        lps_ref[0] = blank
        lps_ref[1] = emit
        before = pltpu.roll(starts, 1, 1)
        before = jnp.where(lanes == 0, prior_ref[0], jnp.where(lanes == half, prior_ref[1], before))
        shift = starts - before
        rows = span_rows(blank, emit)
        for bit in (1, 2, 4, 8):
            moved = (shift & bit) != 0
            rows = [
                jnp.where(moved, rows[i - bit] if i >= bit else masked_log, rows[i]) for i in range(S)
            ]
        for i in range(S):
            tree_ref[0, i] = rows[i]
        levels = half.bit_length() - 1
        for level in range(levels):
            reach = 1 << level
            latter = [pltpu.roll(tree_ref[level, m], LANES - reach, 1) for m in range(S)]

            def product(i, carry, level=level, latter=latter):
                former = tree_ref[level, i]
                row = rowwise_logsumexp([former[m : m + 1, :] + latter[m] for m in range(S)])
                if level + 1 < levels:
                    tree_ref[level + 1, i] = row
                else:
                    root[i] = row
                return carry

            lax.fori_loop(0, S, product, 0)
        flat = jnp.transpose(root[...].reshape(S * S, LANES))
        payload_ref[...] = jnp.zeros_like(payload_ref)
        for b in range(2):
            line = flat[b * half : b * half + 1, :]
            payload_ref[4 * b : 4 * b + 1, :] = line[:, :LANES]
            payload_ref[4 * b + 1 : 4 * b + 2, :] = line[:, LANES:]
            last = starts_ref[b : b + 1, half - 1 : half].astype(F32)
            payload_ref[4 * b + 2 : 4 * b + 3, :] = jnp.broadcast_to(last, (1, LANES))


def backward_kernel(
    piece,
    vocab,
    starts_ref,
    prior_ref,
    frames_ref,
    labels_len_ref,
    block_ref,
    blocks_ref,
    lps_ref,
    tree_ref,
    label_ref,
    weights_ref,
    hidden_ref,
    exps_ref,
    losses_ref,
    grad_enc_ref,
    send_ref,
    chain,
    line_up,
    rows_ref,
    grads,
    enc_sum,
    pred_sum,
    weight_sum,
):
    step = pl.program_id(0)
    half = starts_ref.shape[1]
    width = weights_ref.shape[0]
    count = blocks_ref.shape[0]
    lanes = lane_ids()

    @pl.when(step == 0)
    def _():
        places = row_ids((S, LANES))
        line_up[...] = jnp.zeros_like(line_up)
        for r in range(count):
            for b in range(2):
                at = 2 * r + b
                line_up[at : at + 1, :LANES] = blocks_ref[r, 4 * b : 4 * b + 1, :]
                line_up[at : at + 1, LANES:] = blocks_ref[r, 4 * b + 1 : 4 * b + 2, :]
        chain[...] = jnp.transpose(line_up[...]).reshape(S, S, LANES)
        odd = lanes % 2 == 1
        last_start = [blocks_ref[count - 1, 4 * b + 2 : 4 * b + 3, :].astype(jnp.int32) for b in range(2)]
        final_place = jnp.where(odd, labels_len_ref[1] - last_start[1], labels_len_ref[0] - last_start[0])
        forward = jnp.where(places == 0, 0.0, masked_log) + jnp.zeros((S, LANES), F32)
        closing = jnp.where(places == final_place, 0.0, masked_log)
        backward = closing
        owner = lanes // 2
        for turn in range(count - 1):
            ahead = pltpu.roll(vector_times(forward, chain), 2, 1)
            forward = jnp.where(owner == turn + 1, ahead, forward)
            behind = pltpu.roll(times_vector(chain, backward, rows_ref), LANES - 2, 1)
            backward = jnp.where(owner == count - 2 - turn, behind, backward)
        leaving = vector_times(forward, chain) + closing
        best = jnp.max(leaving, axis=0, keepdims=True)
        log_total = best + jnp.log(jnp.sum(jnp.exp(leaving - best), axis=0, keepdims=True))
        for b in range(2):
            own_total = jnp.sum(jnp.where(lanes == 2 * (count - 1) + b, log_total, 0.0))
            losses_ref[b] = -own_total / frames_ref[b].astype(F32)

        def own_boundary(vectors):
            columns = [
                jnp.sum(jnp.where(lanes == 2 * block_ref[0] + b, vectors, 0.0), axis=1, keepdims=True)
                for b in range(2)
            ]
            spread = jnp.where(lanes < half, columns[0], columns[1])
            return spread - jnp.max(spread, axis=0, keepdims=True)

        alpha = own_boundary(forward)
        beta = own_boundary(backward)
        levels = half.bit_length() - 1
        for level in reversed(range(levels)):
            reach = 1 << level
            later = lanes % (2 * reach) == reach
            ahead = pltpu.roll(vector_times(alpha, tree_ref.at[level]), reach, 1)
            alpha = jnp.where(later, ahead, alpha)
            beta_late = pltpu.roll(beta, reach, 1)
            behind = times_vector(tree_ref.at[level], beta_late, rows_ref)
            beta = jnp.where(later, beta_late, pltpu.roll(behind, LANES - reach, 1))
        starts = rows_to_lanes(starts_ref[...])
        before = pltpu.roll(starts, 1, 1)
        before = jnp.where(lanes == 0, prior_ref[0], jnp.where(lanes == half, prior_ref[1], before))
        shift = starts - before
        for bit in (1, 2, 4, 8):
            moved = jnp.where(places < S - bit, pltpu.roll(alpha, S - bit, 0), masked_log)
            alpha = jnp.where((shift & bit) != 0, moved, alpha)
        spans = span_rows(lps_ref[0], lps_ref[1])
        scores = [spans[e] + alpha[e : e + 1, :] + beta for e in range(S)]
        best = jnp.max(functools.reduce(jnp.maximum, scores), axis=0, keepdims=True)
        weights = [jnp.exp(score - best) for score in scores]
        for e in range(1, S):
            weights[e] = weights[e] + weights[e - 1]
        total = jnp.sum(weights[S - 1], axis=0, keepdims=True)
        negative = -1.0 / total
        grads[0] = weights[S - 1] * negative
        for m in range(S):
            crossing = jnp.sum(jnp.where(places > m, weights[m], 0.0), axis=0, keepdims=True)
            grads[1, m : m + 1, :] = crossing * negative
        enc_sum[...] = jnp.zeros_like(enc_sum)
        pred_sum[...] = jnp.zeros_like(pred_sum)
        weight_sum[...] = jnp.zeros_like(weight_sum)

    def wide(ref, *lead):
        return jnp.concatenate([ref[(*lead, pl.ds(step * GROUP + k, 1), slice(None))] for k in range(GROUP)], axis=1)

    names = wide(label_ref)
    grad_blank = wide(grads, 0)
    grad_emit = wide(grads, 1)
    spread = (grad_blank + grad_emit) * wide(lps_ref, 2)
    padded = exps_ref.shape[0]
    ids = row_ids((padded, WIDE))
    coeff = jnp.where(ids == names, grad_emit, jnp.where(ids == 0, grad_blank, 0.0))
    grad_logits = (coeff - exps_ref[...] * spread).astype(BF16)
    grad_hidden = jnp.dot(weights_ref[...], grad_logits, preferred_element_type=F32)
    hidden = hidden_ref[...]
    hidden_wide = hidden.astype(F32)
    grad_summed = grad_hidden * (1.0 - hidden_wide * hidden_wide)
    enc_sum[...] += functools.reduce(
        lambda a, b: a + b, [grad_summed[:, k * LANES : (k + 1) * LANES] for k in range(GROUP)]
    )
    starts = rows_to_lanes(starts_ref[...])
    base = starts + step * GROUP
    rows = jnp.concatenate([base + k for k in range(GROUP)], axis=1)
    second = jnp.concatenate([per_lane(half, 0, 65)] * GROUP, axis=1)
    slot = row_ids((8 * PRED_SLOT, WIDE))
    wanted = rows + second
    match = (slot // PRED_SLOT * PRED_SHARE + slot % PRED_SLOT == wanted) & (slot % PRED_SLOT < PRED_SHARE)
    pred_sum[...] += lax.dot_general(
        match.astype(BF16), grad_summed.astype(BF16), NT_DIMS, preferred_element_type=F32
    )
    weight_sum[...] += lax.dot_general(hidden, grad_logits, NT_DIMS, preferred_element_type=F32)

    @pl.when(step == STEPS - 1)
    def _():
        grad_enc_ref[...] = jnp.transpose(enc_sum[...]).astype(BF16)
        share = width // 8
        got = row_ids((width, width))
        source = (got % share) // piece * (8 * piece) + got // share * piece + got % piece
        turn = (lane_ids((width, width)) == source).astype(BF16)
        turned = jnp.dot(turn, weight_sum[...].astype(BF16), preferred_element_type=F32).astype(BF16)
        for p in range(8):
            send_ref[p, 0:share, :] = turned[p * share : (p + 1) * share, :]
            send_ref[p, share : share + PRED_SLOT, :] = pred_sum[p * PRED_SLOT : (p + 1) * PRED_SLOT, :].astype(BF16)


def params():
    return pltpu.CompilerParams(dimension_semantics=("arbitrary",), vmem_limit_bytes=VMEM_BYTES)


def whole(shape):
    return pl.BlockSpec(shape, lambda i: (0,) * len(shape))


smem = pl.BlockSpec(memory_space=pltpu.SMEM)


def from_behind(block, axis, distance):
    devices = range(lax.axis_size(axis))
    route = [(i - distance, i) for i in devices if i - distance in devices]
    return lax.ppermute(block, axis, route)


def per_device(encoder, predictor, starts, frame_lengths, label_lengths, labels, w_out):
    utt_count, frame_count, width = encoder.shape
    own_rows, vocab = w_out.shape
    tm_index = lax.axis_index("tm")
    tm_count = lax.axis_size("tm")
    utt_size = lax.axis_size("utt")
    piece = own_rows // tm_count
    padded = -(-vocab // LANES) * LANES
    share = width // tm_count
    rows = S * utt_count * frame_count
    shape = jax.ShapeDtypeStruct

    mine = lax.dynamic_slice_in_dim(w_out, tm_index * piece, piece, axis=0)
    mine = jnp.pad(mine, ((0, 0), (0, padded - vocab)))
    across = lax.all_to_all(
        jnp.broadcast_to(mine.reshape(1, piece * padded // LANES, LANES), (utt_size, piece * padded // LANES, LANES)),
        "utt", 0, 0, tiled=True,
    )
    gathered = lax.all_gather(across.reshape(share, padded), "tm", axis=0, tiled=True)
    prior = from_behind(starts[:, -1], "tm", 1)
    block = tm_index.reshape(1).astype(jnp.int32)

    hidden, label_ids = pl.pallas_call(
        hidden_kernel,
        grid=(STEPS,),
        in_specs=[
            whole(starts.shape),
            whole(labels.shape),
            whole((utt_count * frame_count, width)),
            whole(predictor.shape),
        ],
        out_specs=[pl.BlockSpec((width, WIDE), lambda i: (0, i)), whole((S, LANES))],
        out_shape=[shape((width, rows), BF16), shape((S, LANES), jnp.int32)],
        scratch_shapes=[
            pltpu.VMEM((width, LANES), F32),
            pltpu.VMEM((width, 2 * PRED_PAD), BF16),
            pltpu.VMEM((2 * PRED_PAD, width), F32),
        ],
        compiler_params=params(),
        cost_estimate=pl.CostEstimate(
            flops=2 * 2 * PRED_PAD * width * rows, bytes_accessed=3 * 2**20, transcendentals=width * rows
        ),
    )(starts, labels, encoder.reshape(-1, width), predictor)

    levels = frame_count.bit_length() - 1
    exps, weights, lps, tree, payload = pl.pallas_call(
        functools.partial(forward_kernel, piece, vocab),
        grid=(STEPS,),
        in_specs=[
            whole(starts.shape),
            smem,
            smem,
            smem,
            smem,
            whole((S, LANES)),
            whole((width, padded)),
            pl.BlockSpec((width, WIDE), lambda i: (0, i)),
        ],
        out_specs=[
            pl.BlockSpec((padded, WIDE), lambda i: (0, i)),
            whole((width, padded)),
            whole((3, S, LANES)),
            whole((levels, S, S, LANES)),
            whole((8, LANES)),
        ],
        out_shape=[
            shape((padded, rows), F32),
            shape((width, padded), BF16),
            shape((3, S, LANES), F32),
            shape((levels, S, S, LANES), F32),
            shape((8, LANES), F32),
        ],
        scratch_shapes=[pltpu.VMEM((padded, width), BF16), pltpu.VMEM((S, S, LANES), F32)],
        compiler_params=params(),
        cost_estimate=pl.CostEstimate(
            flops=2 * padded * width * rows, bytes_accessed=8 * 2**20, transcendentals=padded * rows
        ),
    )(starts, prior, frame_lengths, label_lengths, block, label_ids, gathered, hidden)

    blocks = lax.all_gather(payload, "tm", axis=0)

    losses, grad_encoder, send = pl.pallas_call(
        functools.partial(backward_kernel, piece, vocab),
        grid=(STEPS,),
        in_specs=[
            whole(starts.shape),
            smem,
            smem,
            smem,
            smem,
            whole((tm_count, 8, LANES)),
            whole((3, S, LANES)),
            whole((levels, S, S, LANES)),
            whole((S, LANES)),
            whole((width, padded)),
            pl.BlockSpec((width, WIDE), lambda i: (0, i)),
            pl.BlockSpec((padded, WIDE), lambda i: (0, i)),
        ],
        out_specs=[smem, whole((utt_count * frame_count, width)), whole((tm_count, share + PRED_SLOT, padded))],
        out_shape=[
            shape((utt_count,), F32),
            shape((utt_count * frame_count, width), BF16),
            shape((tm_count, share + PRED_SLOT, padded), BF16),
        ],
        scratch_shapes=[
            pltpu.VMEM((S, S, LANES), F32),
            pltpu.VMEM((LANES, S * S), F32),
            pltpu.VMEM((S, LANES), F32),
            pltpu.VMEM((2, S, LANES), F32),
            pltpu.VMEM((width, LANES), F32),
            pltpu.VMEM((8 * PRED_SLOT, width), F32),
            pltpu.VMEM((width, padded), F32),
        ],
        compiler_params=params(),
        cost_estimate=pl.CostEstimate(
            flops=6 * padded * width * rows, bytes_accessed=8 * 2**20, transcendentals=2**16
        ),
    )(starts, prior, frame_lengths, label_lengths, block, blocks, lps, tree, label_ids, weights, hidden, exps)

    came = lax.all_to_all(send, "tm", 0, 0, tiled=True)
    block_sum = jnp.sum(came.astype(F32), axis=0)
    weight_rows = block_sum[:share].reshape(utt_size, piece * padded // LANES, LANES)
    pred_rows = block_sum[share : share + PRED_SHARE]
    across = lax.all_to_all(weight_rows, "utt", 0, 0, tiled=True)
    own_weight = jnp.sum(across, axis=0).reshape(piece, padded)
    final = lax.all_gather(jnp.concatenate([pred_rows, own_weight], axis=0), "tm", axis=0)
    label_rows = predictor.shape[1]
    grad_predictor = final[:, :PRED_SHARE].reshape(-1, width)[: utt_count * label_rows]
    grad_predictor = grad_predictor.reshape(utt_count, label_rows, width)
    grad_w_out = final[:, PRED_SHARE:, :vocab].reshape(own_rows, vocab)
    return (losses, grad_encoder.reshape(encoder.shape), grad_predictor, grad_w_out)


def solution(mesh):
    return jax.shard_map(
        per_device,
        mesh=mesh,
        in_specs=(
            P("utt", "tm", None),
            P("utt", None, None),
            P("utt", "tm"),
            P("utt"),
            P("utt"),
            P("utt", None),
            P("utt", None),
        ),
        out_specs=(P("utt"), P("utt", "tm", None), P("utt", None, None), P("utt", None)),
        check_vma=False,
    )
```

```python
import functools

import jax
import jax.numpy as jnp
from jax import lax
from jax.experimental import pallas as pl
from jax.experimental.pallas import tpu as pltpu
from jax.sharding import PartitionSpec as P

S = 16
LANES = 128
GROUP = 4
STEPS = S // GROUP
WIDE = GROUP * LANES
PRED_PAD = 80
VMEM_BYTES = 40 * 2**20

masked_log = -1e30

F32 = jnp.float32
BF16 = jnp.bfloat16

OFFSETS = (0, 1, 2, -1)
RINGS = {64: (4, 16), 1: (1, 1)}

NT_DIMS = (((1,), (1,)), ((), ()))


def lane_ids(shape=(1, LANES)):
    return lax.broadcasted_iota(jnp.int32, shape, 1)


def row_ids(shape):
    return lax.broadcasted_iota(jnp.int32, shape, 0)


def per_lane(half, low, high):
    return jnp.where(lane_ids() < half, low, high)


def rows_to_lanes(pair):
    return jnp.concatenate([pair[0:1, :], pair[1:2, :]], axis=1)


def rowwise_logsumexp(terms):
    top = functools.reduce(jnp.maximum, terms)
    total = functools.reduce(lambda a, b: a + b, [jnp.exp(t - top) for t in terms])
    return top + jnp.log(total)


def vector_times(vector, matrix):
    return rowwise_logsumexp([vector[i : i + 1, :] + matrix[i] for i in range(S)])


def times_vector(matrix, vector, rows_ref):
    for i in range(S):
        terms = matrix[i] + vector
        top = jnp.max(terms, axis=0, keepdims=True)
        total = jnp.sum(jnp.exp(terms - top), axis=0, keepdims=True)
        rows_ref[i : i + 1, :] = top + jnp.log(total)
    return rows_ref[...]


def window_down(vector, distance):
    places = row_ids((S, LANES))
    for bit in (1, 2, 4, 8):
        moved = jnp.where(places < S - bit, pltpu.roll(vector, S - bit, 0), masked_log)
        vector = jnp.where((distance & bit) != 0, moved, vector)
    return vector


def window_up(vector, distance):
    places = row_ids((S, LANES))
    for bit in (1, 2, 4, 8):
        moved = jnp.where(places >= bit, pltpu.roll(vector, bit, 0), masked_log)
        vector = jnp.where((distance & bit) != 0, moved, vector)
    return vector


def slot_row(slot, utt_index, own_rows, x_size, z_size):
    if x_size * z_size == 1:
        return slot
    unit = slot // own_rows
    s4, s1, sx = unit % 4, unit // 4 % 4, unit // 16
    near = lambda s: jnp.where(s == 3, -1, s)
    x = (utt_index // z_size + near(sx) + x_size) % x_size
    z = (utt_index % z_size + near(s1) + 4 * s4 + z_size) % z_size
    return (x * z_size + z) * own_rows + slot % own_rows


def frame_shifts(starts, half):
    lanes = lane_ids()
    first = (lanes == 0) | (lanes == half)
    return jnp.where(first, 0, starts - pltpu.roll(starts, 1, 1))


def span_rows(blank, emit):
    places = row_ids((S, LANES))
    spans = jnp.zeros((S, LANES), F32)
    rows = [None] * S
    for e in reversed(range(S)):
        spans = jnp.where(places > e, spans + emit[e : e + 1, :], 0.0)
        rows[e] = jnp.where(places >= e, spans + blank, masked_log)
    return rows


def hidden_kernel(starts_ref, labels_ref, enc_ref, pred_ref, hidden_ref, label_ref, enc_t, pred_t, stack):
    step = pl.program_id(0)
    half = starts_ref.shape[1]
    starts = rows_to_lanes(starts_ref[...])

    @pl.when(step == 0)
    def _():
        enc_t[...] = jnp.transpose(enc_ref[...].astype(F32))
        stack[...] = jnp.zeros_like(stack)
        rows = pred_ref.shape[1]
        stack[0:rows, :] = pred_ref[0].astype(F32)
        stack[PRED_PAD : PRED_PAD + rows, :] = pred_ref[1].astype(F32)
        pred_t[...] = jnp.transpose(stack[...]).astype(BF16)
        cap = labels_ref.shape[1]
        labels = labels_ref[...].astype(F32)
        table = [jnp.transpose(jnp.broadcast_to(labels[b : b + 1, :], (LANES, cap))) for b in range(2)]
        table = jnp.where(lane_ids((cap, LANES)) < half, table[0], table[1])
        places = row_ids((cap, LANES))
        for k in range(S):
            wanted = jnp.minimum(starts + k, cap - 1)
            label_ref[k : k + 1, :] = jnp.sum(
                jnp.where(places == wanted, table, 0.0), axis=0, keepdims=True
            ).astype(jnp.int32)

    base = starts + per_lane(half, 0, PRED_PAD) + step * GROUP
    wanted = jnp.concatenate([base + k for k in range(GROUP)], axis=1)
    match = (row_ids((2 * PRED_PAD, WIDE)) == wanted).astype(BF16)
    picked = jnp.dot(pred_t[...], match, preferred_element_type=F32)
    for k in range(GROUP):
        part = slice(k * LANES, (k + 1) * LANES)
        hidden_ref[:, part] = jnp.tanh(enc_t[...] + picked[:, part]).astype(BF16)


def forward_kernel(
    own_rows,
    rings,
    starts_ref,
    frames_ref,
    labels_len_ref,
    block_ref,
    label_ref,
    parts_0,
    parts_1,
    parts_2,
    parts_3,
    hidden_ref,
    exps_ref,
    weights_ref,
    lps_ref,
    tree_ref,
    payload_ref,
    gathered,
    weights_t,
    root,
):
    step = pl.program_id(0)
    width = gathered.shape[0]
    vocab = parts_0.shape[1]

    @pl.when(step == 0)
    def _():
        gathered[...] = jnp.zeros_like(gathered)
        part = width // 4
        for i, parts in enumerate((parts_0, parts_1, parts_2, parts_3)):
            gathered[i * part : (i + 1) * part, :vocab] = parts[...]
        source = slot_row(lane_ids((width, width)), block_ref[1], own_rows, *rings)
        turn = (row_ids((width, width)) == source).astype(BF16)
        weights = jnp.dot(turn, gathered[...], preferred_element_type=F32)
        weights_ref[...] = weights.astype(BF16)
        weights_t[...] = jnp.transpose(weights).astype(BF16)

    logits = jnp.dot(weights_t[...], hidden_ref[...], preferred_element_type=F32)
    padded = logits.shape[0]
    edge = padded - 16
    tail = jnp.where(row_ids((16, WIDE)) < vocab - edge, logits[edge:], masked_log)
    logits = jnp.concatenate([logits[:edge], tail], axis=0)
    top = jnp.max(logits, axis=0, keepdims=True)
    exps = jnp.exp(logits - top)
    exps_ref[...] = exps
    total = jnp.sum(exps, axis=0, keepdims=True)
    norm = top + jnp.log(total)
    scale = 1.0 / total
    names = jnp.concatenate([label_ref[pl.ds(step * GROUP + k, 1), :] for k in range(GROUP)], axis=1)
    emit = jnp.sum(jnp.where(row_ids((padded, WIDE)) == names, logits, 0.0), axis=0, keepdims=True) - norm
    blank = logits[0:1, :] - norm
    for k in range(GROUP):
        part = slice(k * LANES, (k + 1) * LANES)
        row = pl.ds(step * GROUP + k, 1)
        lps_ref[0, row, :] = blank[:, part]
        lps_ref[1, row, :] = emit[:, part]
        lps_ref[2, row, :] = scale[:, part]

    @pl.when(step == STEPS - 1)
    def _():
        half = starts_ref.shape[1]
        lanes = lane_ids()
        starts = rows_to_lanes(starts_ref[...])
        frame = block_ref[0] * half + lanes % half
        live = frame < per_lane(half, frames_ref[0], frames_ref[1])
        limit = per_lane(half, labels_len_ref[0], labels_len_ref[1])
        allowed = live & (row_ids((S, LANES)) + starts < limit)
        blank = jnp.where(live, lps_ref[0], 0.0)
        emit = jnp.where(allowed, lps_ref[1], masked_log)
        lps_ref[0] = blank
        lps_ref[1] = emit
        shift = frame_shifts(starts, half)
        rows = span_rows(blank, emit)
        for bit in (1, 2, 4, 8):
            moved = (shift & bit) != 0
            rows = [
                jnp.where(moved, rows[i - bit] if i >= bit else masked_log, rows[i]) for i in range(S)
            ]
        for i in range(S):
            tree_ref[0, i] = rows[i]
        levels = half.bit_length() - 1
        for level in range(levels):
            reach = 1 << level
            latter = [pltpu.roll(tree_ref[level, m], LANES - reach, 1) for m in range(S)]

            def product(i, carry, level=level, latter=latter):
                former = tree_ref[level, i]
                row = rowwise_logsumexp([former[m : m + 1, :] + latter[m] for m in range(S)])
                if level + 1 < levels:
                    tree_ref[level + 1, i] = row
                else:
                    root[i] = row
                return carry

            lax.fori_loop(0, S, product, 0)
        flat = jnp.transpose(root[...].reshape(S * S, LANES))
        payload_ref[...] = jnp.zeros_like(payload_ref)
        for b in range(2):
            line = flat[b * half : b * half + 1, :]
            payload_ref[4 * b : 4 * b + 1, :] = line[:, :LANES]
            payload_ref[4 * b + 1 : 4 * b + 2, :] = line[:, LANES:]
            for end, at in ((2, half - 1), (3, 0)):
                edge_start = starts_ref[b : b + 1, at : at + 1].astype(F32)
                payload_ref[4 * b + end : 4 * b + end + 1, :] = jnp.broadcast_to(edge_start, (1, LANES))


def backward_kernel(
    own_rows,
    rings,
    label_rows,
    starts_ref,
    frames_ref,
    labels_len_ref,
    block_ref,
    *refs,
):
    blocks_refs, refs = refs[:8], refs[8:]
    lps_ref, tree_ref, label_ref, weights_ref, hidden_ref, exps_ref = refs[:6]
    losses_ref, grad_enc_ref, send_0, send_1, send_2, send_3, pred_own, pred_other = refs[6:14]
    chain, line_up, rows_ref, grads, enc_sum, pred_sum, weight_sum = refs[14:]
    step = pl.program_id(0)
    half = starts_ref.shape[1]
    width = weights_ref.shape[0]
    count = len(blocks_refs)
    lanes = lane_ids()
    core = block_ref[0] % 2

    @pl.when(step == 0)
    def _():
        places = row_ids((S, LANES))
        line_up[...] = jnp.zeros_like(line_up)
        final = [jnp.zeros((1, LANES), F32)] * 2
        ends = jnp.zeros((1, LANES), F32)
        begins = jnp.zeros((1, LANES), F32)
        for turn, blocks_ref in enumerate(blocks_refs):
            r = block_ref[0] ^ turn
            for b in range(2):
                at = 2 * r + b
                end = blocks_ref[4 * b + 2 : 4 * b + 3, :]
                line_up[0, pl.ds(at, 1), :] = blocks_ref[4 * b : 4 * b + 1, :]
                line_up[1, pl.ds(at, 1), :] = blocks_ref[4 * b + 1 : 4 * b + 2, :]
                ends = jnp.where(lanes == at, end, ends)
                begins = jnp.where(lanes == at, blocks_ref[4 * b + 3 : 4 * b + 4, :], begins)
                final[b] = jnp.where(r == count - 1, end, final[b])
        for h in range(2):
            chain[h * S // 2 : (h + 1) * S // 2] = jnp.transpose(line_up[h]).reshape(S // 2, S, LANES)
        odd = lanes % 2 == 1
        last_start = [row.astype(jnp.int32) for row in final]
        final_place = jnp.where(odd, labels_len_ref[1] - last_start[1], labels_len_ref[0] - last_start[0])
        gap = (begins - pltpu.roll(ends, 2, 1)).astype(jnp.int32)
        gap = jnp.where((lanes >= 2) & (lanes < 2 * count), gap, 0)
        forward = jnp.where(places == 0, 0.0, masked_log) + jnp.zeros((S, LANES), F32)
        closing = jnp.where(places == final_place, 0.0, masked_log)
        backward = closing
        owner = lanes // 2
        for turn in range(count - 1):
            ahead = window_down(pltpu.roll(vector_times(forward, chain), 2, 1), gap)
            forward = jnp.where(owner == turn + 1, ahead, forward)
            behind = pltpu.roll(window_up(times_vector(chain, backward, rows_ref), gap), LANES - 2, 1)
            backward = jnp.where(owner == count - 2 - turn, behind, backward)
        leaving = vector_times(forward, chain) + closing
        best = jnp.max(leaving, axis=0, keepdims=True)
        log_total = best + jnp.log(jnp.sum(jnp.exp(leaving - best), axis=0, keepdims=True))
        for b in range(2):
            own_total = jnp.sum(jnp.where(lanes == 2 * (count - 1) + b, log_total, 0.0))
            losses_ref[b] = -own_total / frames_ref[b].astype(F32)

        def own_boundary(vectors):
            columns = [
                jnp.sum(jnp.where(lanes == 2 * block_ref[0] + b, vectors, 0.0), axis=1, keepdims=True)
                for b in range(2)
            ]
            spread = jnp.where(lanes < half, columns[0], columns[1])
            return spread - jnp.max(spread, axis=0, keepdims=True)

        alpha = own_boundary(forward)
        beta = own_boundary(backward)
        levels = half.bit_length() - 1
        for level in reversed(range(levels)):
            reach = 1 << level
            later = lanes % (2 * reach) == reach
            ahead = pltpu.roll(vector_times(alpha, tree_ref.at[level]), reach, 1)
            alpha = jnp.where(later, ahead, alpha)
            beta_late = pltpu.roll(beta, reach, 1)
            behind = times_vector(tree_ref.at[level], beta_late, rows_ref)
            beta = jnp.where(later, beta_late, pltpu.roll(behind, LANES - reach, 1))
        starts = rows_to_lanes(starts_ref[...])
        alpha = window_down(alpha, frame_shifts(starts, half))
        spans = span_rows(lps_ref[0], lps_ref[1])
        scores = [spans[e] + alpha[e : e + 1, :] + beta for e in range(S)]
        best = jnp.max(functools.reduce(jnp.maximum, scores), axis=0, keepdims=True)
        weights = [jnp.exp(score - best) for score in scores]
        for e in range(1, S):
            weights[e] = weights[e] + weights[e - 1]
        total = jnp.sum(weights[S - 1], axis=0, keepdims=True)
        negative = -1.0 / total
        grads[0] = weights[S - 1] * negative
        for m in range(S):
            crossing = jnp.sum(jnp.where(places > m, weights[m], 0.0), axis=0, keepdims=True)
            grads[1, m : m + 1, :] = crossing * negative
        enc_sum[...] = jnp.zeros_like(enc_sum)
        pred_sum[...] = jnp.zeros_like(pred_sum)
        weight_sum[...] = jnp.zeros_like(weight_sum)

    def wide(ref, *lead):
        return jnp.concatenate([ref[(*lead, pl.ds(step * GROUP + k, 1), slice(None))] for k in range(GROUP)], axis=1)

    names = wide(label_ref)
    grad_blank = wide(grads, 0)
    grad_emit = wide(grads, 1)
    spread = (grad_blank + grad_emit) * wide(lps_ref, 2)
    padded = exps_ref.shape[0]
    ids = row_ids((padded, WIDE))
    coeff = jnp.where(ids == names, grad_emit, jnp.where(ids == 0, grad_blank, 0.0))
    grad_logits = (coeff - exps_ref[...] * spread).astype(BF16)
    grad_hidden = jnp.dot(weights_ref[...], grad_logits, preferred_element_type=F32)
    hidden = hidden_ref[...]
    hidden_wide = hidden.astype(F32)
    grad_summed = grad_hidden * (1.0 - hidden_wide * hidden_wide)
    enc_sum[...] += functools.reduce(
        lambda a, b: a + b, [grad_summed[:, k * LANES : (k + 1) * LANES] for k in range(GROUP)]
    )
    starts = rows_to_lanes(starts_ref[...])
    base = starts + step * GROUP
    rows = jnp.concatenate([base + k for k in range(GROUP)], axis=1)
    second = jnp.concatenate([per_lane(half, 0, 1)] * GROUP, axis=1)
    slot = row_ids((2 * PRED_PAD, WIDE))
    match = (slot % PRED_PAD == rows) & ((slot // PRED_PAD ^ core) == second)
    pred_sum[...] += lax.dot_general(
        match.astype(BF16), grad_summed.astype(BF16), NT_DIMS, preferred_element_type=F32
    )
    weight_sum[...] += lax.dot_general(hidden, grad_logits, NT_DIMS, preferred_element_type=F32)

    @pl.when(step == STEPS - 1)
    def _():
        grad_enc_ref[...] = jnp.transpose(enc_sum[...]).astype(BF16)
        source = slot_row(row_ids((width, width)), block_ref[1], own_rows, *rings)
        turn = (lane_ids((width, width)) == source).astype(BF16)
        turned = jnp.dot(turn, weight_sum[...].astype(BF16), preferred_element_type=F32).astype(BF16)
        part = width // 4
        for i, send_ref in enumerate((send_0, send_1, send_2, send_3)):
            send_ref[...] = turned[i * part : (i + 1) * part, :]
        pred_own[...] = pred_sum[0:PRED_PAD, :]
        pred_other[...] = pred_sum[PRED_PAD:, :].astype(BF16)


def sum_kernel(*refs):
    ins, outs = refs[:4], refs[4:]
    total = functools.reduce(lambda a, b: a + b, [r[...].astype(F32) for r in ins])
    part = total.shape[0] // len(outs)
    for i, out in enumerate(outs):
        out[...] = total[i * part : (i + 1) * part].astype(out.dtype)


def sum_and_split(arrays, kinds):
    rows, width = arrays[0].shape
    vmem = pl.BlockSpec(memory_space=pltpu.VMEM)
    return pl.pallas_call(
        sum_kernel,
        in_specs=[vmem] * 4,
        out_specs=[vmem] * len(kinds),
        out_shape=[jax.ShapeDtypeStruct((rows // len(kinds), width), kind) for kind in kinds],
    )(*arrays)


def params():
    return pltpu.CompilerParams(dimension_semantics=("arbitrary",), vmem_limit_bytes=VMEM_BYTES)


def whole(shape):
    return pl.BlockSpec(shape, lambda i: (0,) * len(shape))


smem = pl.BlockSpec(memory_space=pltpu.SMEM)


def from_offset(block, axis, source):
    size = lax.axis_size(axis)
    return lax.ppermute(block, axis, [(source(i) % size, i) for i in range(size)])


def x_source(offset, x_size, z_size):
    return lambda i: (i // z_size + offset) % x_size * z_size + i % z_size


def z_source(offset, x_size, z_size):
    return lambda i: i // z_size * z_size + (i % z_size + offset) % z_size


def per_device(encoder, predictor, starts, frame_lengths, label_lengths, labels, w_out):
    utt_count, frame_count, width = encoder.shape
    own_rows, vocab = w_out.shape
    label_rows = predictor.shape[1]
    tm_index = lax.axis_index("tm")
    tm_count = lax.axis_size("tm")
    utt_index = lax.axis_index("utt")
    utt_size = lax.axis_size("utt")
    rings = RINGS[utt_size]
    padded = -(-vocab // LANES) * LANES
    rows = S * utt_count * frame_count
    shape = jax.ShapeDtypeStruct

    if utt_size > 1:
        held = [w_out] + [from_offset(w_out, "utt", z_source(4 * s, *rings)) for s in (1, 2, 3)]
        held = jnp.concatenate(held, axis=0)
        held = [held] + [from_offset(held, "utt", z_source(o, *rings)) for o in OFFSETS[1:]]
        held = jnp.concatenate(held, axis=0)
        parts = [held] + [from_offset(held, "utt", x_source(o, *rings)) for o in OFFSETS[1:]]
    else:
        parts = [w_out[i * width // 4 : (i + 1) * width // 4] for i in range(4)]
    block = jnp.stack([tm_index, utt_index]).astype(jnp.int32)

    hidden, label_ids = pl.pallas_call(
        hidden_kernel,
        grid=(STEPS,),
        in_specs=[
            whole(starts.shape),
            whole(labels.shape),
            whole((utt_count * frame_count, width)),
            whole(predictor.shape),
        ],
        out_specs=[pl.BlockSpec((width, WIDE), lambda i: (0, i)), whole((S, LANES))],
        out_shape=[shape((width, rows), BF16), shape((S, LANES), jnp.int32)],
        scratch_shapes=[
            pltpu.VMEM((width, LANES), F32),
            pltpu.VMEM((width, 2 * PRED_PAD), BF16),
            pltpu.VMEM((2 * PRED_PAD, width), F32),
        ],
        compiler_params=params(),
        cost_estimate=pl.CostEstimate(
            flops=2 * 2 * PRED_PAD * width * rows, bytes_accessed=3 * 2**20, transcendentals=width * rows
        ),
    )(starts, labels, encoder.reshape(-1, width), predictor)

    levels = frame_count.bit_length() - 1
    exps, weights, lps, tree, payload = pl.pallas_call(
        functools.partial(forward_kernel, own_rows, rings),
        grid=(STEPS,),
        in_specs=[
            whole(starts.shape),
            smem,
            smem,
            smem,
            whole((S, LANES)),
            *[whole((width // 4, vocab))] * 4,
            pl.BlockSpec((width, WIDE), lambda i: (0, i)),
        ],
        out_specs=[
            pl.BlockSpec((padded, WIDE), lambda i: (0, i)),
            whole((width, padded)),
            whole((3, S, LANES)),
            whole((levels, S, S, LANES)),
            whole((8, LANES)),
        ],
        out_shape=[
            shape((padded, rows), F32),
            shape((width, padded), BF16),
            shape((3, S, LANES), F32),
            shape((levels, S, S, LANES), F32),
            shape((8, LANES), F32),
        ],
        scratch_shapes=[
            pltpu.VMEM((width, padded), BF16),
            pltpu.VMEM((padded, width), BF16),
            pltpu.VMEM((S, S, LANES), F32),
        ],
        compiler_params=params(),
        cost_estimate=pl.CostEstimate(
            flops=2 * padded * width * rows, bytes_accessed=8 * 2**20, transcendentals=padded * rows
        ),
    )(starts, frame_lengths, label_lengths, block, label_ids, *parts, hidden)

    def tm_flip(block, turn):
        return from_offset(block, "tm", lambda i: i ^ turn)

    blocks = [payload] + [tm_flip(payload, turn) for turn in range(1, tm_count)]

    losses, grad_encoder, *sends = pl.pallas_call(
        functools.partial(backward_kernel, own_rows, rings, label_rows),
        grid=(STEPS,),
        in_specs=[
            whole(starts.shape),
            smem,
            smem,
            smem,
            *[whole((8, LANES))] * tm_count,
            whole((3, S, LANES)),
            whole((levels, S, S, LANES)),
            whole((S, LANES)),
            whole((width, padded)),
            pl.BlockSpec((width, WIDE), lambda i: (0, i)),
            pl.BlockSpec((padded, WIDE), lambda i: (0, i)),
        ],
        out_specs=[
            smem,
            whole((utt_count * frame_count, width)),
            *[whole((width // 4, padded))] * 4,
            *[whole((PRED_PAD, width))] * 2,
        ],
        out_shape=[
            shape((utt_count,), F32),
            shape((utt_count * frame_count, width), BF16),
            *[shape((width // 4, padded), BF16)] * 4,
            shape((PRED_PAD, width), F32),
            shape((PRED_PAD, width), BF16),
        ],
        scratch_shapes=[
            pltpu.VMEM((S, S, LANES), F32),
            pltpu.VMEM((2, LANES, LANES), F32),
            pltpu.VMEM((S, LANES), F32),
            pltpu.VMEM((2, S, LANES), F32),
            pltpu.VMEM((width, LANES), F32),
            pltpu.VMEM((2 * PRED_PAD, width), F32),
            pltpu.VMEM((width, padded), F32),
        ],
        compiler_params=params(),
        cost_estimate=pl.CostEstimate(
            flops=6 * padded * width * rows, bytes_accessed=8 * 2**20, transcendentals=2**16
        ),
    )(starts, frame_lengths, label_lengths, block, *blocks, lps, tree, label_ids, weights, hidden, exps)

    terms, (pred_own, pred_other) = sends[:4], sends[4:]
    pred_own = pred_own + tm_flip(pred_other, 1).astype(F32)
    pred_sent = pred_own.astype(BF16)
    for turn in (2, 4, 6):
        pred_own = pred_own + tm_flip(pred_sent, turn).astype(F32)
    pred_own = pred_own[:label_rows]
    pred_far = tm_flip(pred_own, 1)
    is_odd = tm_index % 2 == 1
    grad_predictor = jnp.stack([jnp.where(is_odd, pred_far, pred_own), jnp.where(is_odd, pred_own, pred_far)])

    if utt_size > 1:
        arrived = [terms[0]] + [from_offset(t, "utt", x_source(-o, *rings)) for t, o in zip(terms[1:], OFFSETS[1:])]
        terms = sum_and_split(arrived, [F32, BF16, BF16, BF16])
        arrived = [terms[0]] + [from_offset(t, "utt", z_source(-o, *rings)) for t, o in zip(terms[1:], OFFSETS[1:])]
        terms = sum_and_split(arrived, [F32] * 4)
        arrived = [terms[0]] + [from_offset(t, "utt", z_source(-4 * s, *rings)) for t, s in zip(terms[1:], (1, 2, 3))]
        own = arrived[0] + arrived[1] + arrived[2] + arrived[3]
    else:
        own = jnp.concatenate(terms, axis=0).astype(F32)
    own = own + tm_flip(own, 1)
    own = own + tm_flip(own, 2) + tm_flip(own, 4) + tm_flip(own, 6)
    return (losses, grad_encoder.reshape(encoder.shape), grad_predictor, own[:, :vocab])


def solution(mesh):
    return jax.shard_map(
        per_device,
        mesh=mesh,
        in_specs=(
            P("utt", "tm", None),
            P("utt", None, None),
            P("utt", "tm"),
            P("utt"),
            P("utt"),
            P("utt", None),
            P("utt", None),
        ),
        out_specs=(P("utt"), P("utt", "tm", None), P("utt", None, None), P("utt", None)),
        check_vma=False,
    )
```

```python
import functools

import jax
import jax.numpy as jnp
from jax import lax
from jax.experimental import pallas as pl
from jax.experimental.pallas import tpu as pltpu
from jax.sharding import PartitionSpec as P

S = 16
LANES = 128
GROUP = 4
STEPS = S // GROUP
WIDE = GROUP * LANES
PRED_PAD = 80
VMEM_BYTES = 40 * 2**20

masked_log = -1e30

F32 = jnp.float32
BF16 = jnp.bfloat16

PRED_SHARE = 17
PRED_SLOT = 32
TM = ("y", "core")
NEAR = ("x", "zl")
FAR = "zh"

NT_DIMS = (((1,), (1,)), ((), ()))


def lane_ids(shape=(1, LANES)):
    return lax.broadcasted_iota(jnp.int32, shape, 1)


def row_ids(shape):
    return lax.broadcasted_iota(jnp.int32, shape, 0)


def per_lane(half, low, high):
    return jnp.where(lane_ids() < half, low, high)


def rows_to_lanes(pair):
    return jnp.concatenate([pair[0:1, :], pair[1:2, :]], axis=1)


def balanced(combine, terms):
    while len(terms) > 1:
        terms = [combine(a, b) for a, b in zip(terms[0::2], terms[1::2])]
    return terms[0]


def rowwise_logsumexp(terms):
    top = balanced(jnp.maximum, terms)
    total = balanced(jnp.add, [jnp.exp(t - top) for t in terms])
    return top + jnp.log(total)


def vector_times(vector, matrix):
    return rowwise_logsumexp([vector[i : i + 1, :] + matrix[i] for i in range(S)])


def times_vector(matrix, vector, rows_ref):
    for i in range(S):
        terms = matrix[i] + vector
        top = jnp.max(terms, axis=0, keepdims=True)
        total = jnp.sum(jnp.exp(terms - top), axis=0, keepdims=True)
        rows_ref[i : i + 1, :] = top + jnp.log(total)
    return rows_ref[...]


def window_down(vector, distance):
    places = row_ids((S, LANES))
    for bit in (1, 2, 4, 8):
        moved = jnp.where(places < S - bit, pltpu.roll(vector, S - bit, 0), masked_log)
        vector = jnp.where((distance & bit) != 0, moved, vector)
    return vector


def window_up(vector, distance):
    places = row_ids((S, LANES))
    for bit in (1, 2, 4, 8):
        moved = jnp.where(places >= bit, pltpu.roll(vector, bit, 0), masked_log)
        vector = jnp.where((distance & bit) != 0, moved, vector)
    return vector


def slot_row(slot, own_rows, width):
    if own_rows != 8:
        return slot
    share = width // 8
    tm, x, zl, zh = slot // share, slot // 16 % 4, slot // 8 % 2, slot % 8
    return (x * 16 + zh * 2 + zl) * own_rows + tm


def frame_shifts(starts, half):
    lanes = lane_ids()
    first = (lanes == 0) | (lanes == half)
    return jnp.where(first, 0, starts - pltpu.roll(starts, 1, 1))


def span_rows(blank, emit):
    places = row_ids((S, LANES))
    spans = jnp.zeros((S, LANES), F32)
    rows = [None] * S
    for e in reversed(range(S)):
        spans = jnp.where(places > e, spans + emit[e : e + 1, :], 0.0)
        rows[e] = jnp.where(places >= e, spans + blank, masked_log)
    return rows


def hidden_kernel(starts_ref, labels_ref, enc_ref, pred_ref, hidden_ref, label_ref, enc_t, pred_t, stack):
    step = pl.program_id(0)
    half = starts_ref.shape[1]
    starts = rows_to_lanes(starts_ref[...])

    @pl.when(step == 0)
    def _():
        enc_t[...] = jnp.transpose(enc_ref[...].astype(F32))
        stack[...] = jnp.zeros_like(stack)
        rows = pred_ref.shape[1]
        stack[0:rows, :] = pred_ref[0].astype(F32)
        stack[PRED_PAD : PRED_PAD + rows, :] = pred_ref[1].astype(F32)
        pred_t[...] = jnp.transpose(stack[...]).astype(BF16)
        cap = labels_ref.shape[1]
        labels = labels_ref[...].astype(F32)
        table = [jnp.transpose(jnp.broadcast_to(labels[b : b + 1, :], (LANES, cap))) for b in range(2)]
        table = jnp.where(lane_ids((cap, LANES)) < half, table[0], table[1])
        places = row_ids((cap, LANES))
        for k in range(S):
            wanted = jnp.minimum(starts + k, cap - 1)
            label_ref[k : k + 1, :] = jnp.sum(
                jnp.where(places == wanted, table, 0.0), axis=0, keepdims=True
            ).astype(jnp.int32)

    base = starts + per_lane(half, 0, PRED_PAD) + step * GROUP
    wanted = jnp.concatenate([base + k for k in range(GROUP)], axis=1)
    match = (row_ids((2 * PRED_PAD, WIDE)) == wanted).astype(BF16)
    picked = jnp.dot(pred_t[...], match, preferred_element_type=F32)
    for k in range(GROUP):
        part = slice(k * LANES, (k + 1) * LANES)
        hidden_ref[:, part] = jnp.tanh(enc_t[...] + picked[:, part]).astype(BF16)


def forward_kernel(
    own_rows,
    vocab,
    starts_ref,
    frames_ref,
    labels_len_ref,
    block_ref,
    label_ref,
    gathered_ref,
    hidden_ref,
    exps_ref,
    weights_ref,
    lps_ref,
    tree_ref,
    payload_ref,
    weights_t,
    root,
):
    step = pl.program_id(0)
    width = gathered_ref.shape[0]

    @pl.when(step == 0)
    def _():
        source = slot_row(lane_ids((width, width)), own_rows, width)
        turn = (row_ids((width, width)) == source).astype(BF16)
        weights = jnp.dot(turn, gathered_ref[...], preferred_element_type=F32)
        weights_ref[...] = weights.astype(BF16)
        weights_t[...] = jnp.transpose(weights).astype(BF16)

    logits = jnp.dot(weights_t[...], hidden_ref[...], preferred_element_type=F32)
    padded = logits.shape[0]
    edge = padded - 16
    tail = jnp.where(row_ids((16, WIDE)) < vocab - edge, logits[edge:], masked_log)
    logits = jnp.concatenate([logits[:edge], tail], axis=0)
    top = jnp.max(logits, axis=0, keepdims=True)
    exps = jnp.exp(logits - top)
    exps_ref[...] = exps
    total = jnp.sum(exps, axis=0, keepdims=True)
    norm = top + jnp.log(total)
    scale = 1.0 / total
    names = jnp.concatenate([label_ref[pl.ds(step * GROUP + k, 1), :] for k in range(GROUP)], axis=1)
    emit = jnp.sum(jnp.where(row_ids((padded, WIDE)) == names, logits, 0.0), axis=0, keepdims=True) - norm
    blank = logits[0:1, :] - norm
    for k in range(GROUP):
        part = slice(k * LANES, (k + 1) * LANES)
        row = pl.ds(step * GROUP + k, 1)
        lps_ref[0, row, :] = blank[:, part]
        lps_ref[1, row, :] = emit[:, part]
        lps_ref[2, row, :] = scale[:, part]

    @pl.when(step == STEPS - 1)
    def _():
        half = starts_ref.shape[1]
        lanes = lane_ids()
        starts = rows_to_lanes(starts_ref[...])
        frame = block_ref[0] * half + lanes % half
        live = frame < per_lane(half, frames_ref[0], frames_ref[1])
        limit = per_lane(half, labels_len_ref[0], labels_len_ref[1])
        allowed = live & (row_ids((S, LANES)) + starts < limit)
        blank = jnp.where(live, lps_ref[0], 0.0)
        emit = jnp.where(allowed, lps_ref[1], masked_log)
        lps_ref[0] = blank
        lps_ref[1] = emit
        shift = frame_shifts(starts, half)
        rows = span_rows(blank, emit)
        for bit in (1, 2, 4, 8):
            moved = (shift & bit) != 0
            rows = [
                jnp.where(moved, rows[i - bit] if i >= bit else masked_log, rows[i]) for i in range(S)
            ]
        for i in range(S):
            tree_ref[0, i] = rows[i]
        levels = half.bit_length() - 1
        for level in range(levels):
            reach = 1 << level
            latter = [pltpu.roll(tree_ref[level, m], LANES - reach, 1) for m in range(S)]

            def product(i, carry, level=level, latter=latter):
                former = tree_ref[level, i]
                row = rowwise_logsumexp([former[m : m + 1, :] + latter[m] for m in range(S)])
                if level + 1 < levels:
                    tree_ref[level + 1, i] = row
                else:
                    root[i] = row
                return carry

            lax.fori_loop(0, S, product, 0, unroll=4)
        flat = jnp.transpose(root[...].reshape(S * S, LANES))
        payload_ref[...] = jnp.zeros_like(payload_ref)
        for b in range(2):
            line = flat[b * half : b * half + 1, :]
            payload_ref[4 * b : 4 * b + 1, :] = line[:, :LANES]
            payload_ref[4 * b + 1 : 4 * b + 2, :] = line[:, LANES:]
            for end, at in ((2, half - 1), (3, 0)):
                edge_start = starts_ref[b : b + 1, at : at + 1].astype(F32)
                payload_ref[4 * b + end : 4 * b + end + 1, :] = jnp.broadcast_to(edge_start, (1, LANES))


def backward_kernel(
    own_rows,
    label_rows,
    starts_ref,
    frames_ref,
    labels_len_ref,
    block_ref,
    blocks_ref,
    lps_ref,
    tree_ref,
    label_ref,
    weights_ref,
    hidden_ref,
    exps_ref,
    losses_ref,
    grad_enc_ref,
    send_ref,
    chain,
    line_up,
    rows_ref,
    grads,
    enc_sum,
    pred_sum,
    weight_sum,
):
    step = pl.program_id(0)
    half = starts_ref.shape[1]
    width = weights_ref.shape[0]
    count = blocks_ref.shape[0]
    lanes = lane_ids()

    @pl.when(step == 0)
    def _():
        places = row_ids((S, LANES))
        line_up[...] = jnp.zeros_like(line_up)
        ends = jnp.zeros((1, LANES), F32)
        begins = jnp.zeros((1, LANES), F32)
        for r in range(count):
            for b in range(2):
                at = 2 * r + b
                line_up[0, at : at + 1, :] = blocks_ref[r, 4 * b : 4 * b + 1, :]
                line_up[1, at : at + 1, :] = blocks_ref[r, 4 * b + 1 : 4 * b + 2, :]
                ends = jnp.where(lanes == at, blocks_ref[r, 4 * b + 2 : 4 * b + 3, :], ends)
                begins = jnp.where(lanes == at, blocks_ref[r, 4 * b + 3 : 4 * b + 4, :], begins)
        for h in range(2):
            chain[h * S // 2 : (h + 1) * S // 2] = jnp.transpose(line_up[h]).reshape(S // 2, S, LANES)
        odd = lanes % 2 == 1
        last_start = [blocks_ref[count - 1, 4 * b + 2 : 4 * b + 3, :].astype(jnp.int32) for b in range(2)]
        final_place = jnp.where(odd, labels_len_ref[1] - last_start[1], labels_len_ref[0] - last_start[0])
        gap = (begins - pltpu.roll(ends, 2, 1)).astype(jnp.int32)
        gap = jnp.where((lanes >= 2) & (lanes < 2 * count), gap, 0)
        forward = jnp.where(places == 0, 0.0, masked_log) + jnp.zeros((S, LANES), F32)
        closing = jnp.where(places == final_place, 0.0, masked_log)
        backward = closing
        owner = lanes // 2
        for turn in range(count - 1):
            ahead = window_down(pltpu.roll(vector_times(forward, chain), 2, 1), gap)
            forward = jnp.where(owner == turn + 1, ahead, forward)
            behind = pltpu.roll(window_up(times_vector(chain, backward, rows_ref), gap), LANES - 2, 1)
            backward = jnp.where(owner == count - 2 - turn, behind, backward)
        leaving = vector_times(forward, chain) + closing
        best = jnp.max(leaving, axis=0, keepdims=True)
        log_total = best + jnp.log(jnp.sum(jnp.exp(leaving - best), axis=0, keepdims=True))
        for b in range(2):
            own_total = jnp.sum(jnp.where(lanes == 2 * (count - 1) + b, log_total, 0.0))
            losses_ref[b] = -own_total / frames_ref[b].astype(F32)

        def own_boundary(vectors):
            columns = [
                jnp.sum(jnp.where(lanes == 2 * block_ref[0] + b, vectors, 0.0), axis=1, keepdims=True)
                for b in range(2)
            ]
            spread = jnp.where(lanes < half, columns[0], columns[1])
            return spread - jnp.max(spread, axis=0, keepdims=True)

        alpha = own_boundary(forward)
        beta = own_boundary(backward)
        levels = half.bit_length() - 1
        for level in reversed(range(levels)):
            reach = 1 << level
            later = lanes % (2 * reach) == reach
            ahead = pltpu.roll(vector_times(alpha, tree_ref.at[level]), reach, 1)
            alpha = jnp.where(later, ahead, alpha)
            beta_late = pltpu.roll(beta, reach, 1)
            behind = times_vector(tree_ref.at[level], beta_late, rows_ref)
            beta = jnp.where(later, beta_late, pltpu.roll(behind, LANES - reach, 1))
        starts = rows_to_lanes(starts_ref[...])
        alpha = window_down(alpha, frame_shifts(starts, half))
        spans = span_rows(lps_ref[0], lps_ref[1])
        scores = [spans[e] + alpha[e : e + 1, :] + beta for e in range(S)]
        best = jnp.max(functools.reduce(jnp.maximum, scores), axis=0, keepdims=True)
        weights = [jnp.exp(score - best) for score in scores]
        for e in range(1, S):
            weights[e] = weights[e] + weights[e - 1]
        total = jnp.sum(weights[S - 1], axis=0, keepdims=True)
        negative = -1.0 / total
        grads[0] = weights[S - 1] * negative
        for m in range(S):
            crossing = jnp.sum(jnp.where(places > m, weights[m], 0.0), axis=0, keepdims=True)
            grads[1, m : m + 1, :] = crossing * negative
        enc_sum[...] = jnp.zeros_like(enc_sum)
        pred_sum[...] = jnp.zeros_like(pred_sum)
        weight_sum[...] = jnp.zeros_like(weight_sum)

    def wide(ref, *lead):
        return jnp.concatenate([ref[(*lead, pl.ds(step * GROUP + k, 1), slice(None))] for k in range(GROUP)], axis=1)

    names = wide(label_ref)
    grad_blank = wide(grads, 0)
    grad_emit = wide(grads, 1)
    spread = (grad_blank + grad_emit) * wide(lps_ref, 2)
    padded = exps_ref.shape[0]
    ids = row_ids((padded, WIDE))
    coeff = jnp.where(ids == names, grad_emit, jnp.where(ids == 0, grad_blank, 0.0))
    grad_logits = (coeff - exps_ref[...] * spread).astype(BF16)
    grad_hidden = jnp.dot(weights_ref[...], grad_logits, preferred_element_type=F32)
    hidden = hidden_ref[...]
    hidden_wide = hidden.astype(F32)
    grad_summed = grad_hidden * (1.0 - hidden_wide * hidden_wide)
    enc_sum[...] += functools.reduce(
        lambda a, b: a + b, [grad_summed[:, k * LANES : (k + 1) * LANES] for k in range(GROUP)]
    )
    starts = rows_to_lanes(starts_ref[...])
    base = starts + step * GROUP
    rows = jnp.concatenate([base + k for k in range(GROUP)], axis=1)
    wanted = rows + jnp.concatenate([per_lane(half, 0, label_rows)] * GROUP, axis=1)
    slot = row_ids((8 * PRED_SLOT, WIDE))
    match = (slot // PRED_SLOT * PRED_SHARE + slot % PRED_SLOT == wanted) & (slot % PRED_SLOT < PRED_SHARE)
    pred_sum[...] += lax.dot_general(
        match.astype(BF16), grad_summed.astype(BF16), NT_DIMS, preferred_element_type=F32
    )
    weight_sum[...] += lax.dot_general(hidden, grad_logits, NT_DIMS, preferred_element_type=F32)

    @pl.when(step == STEPS - 1)
    def _():
        grad_enc_ref[...] = jnp.transpose(enc_sum[...]).astype(BF16)
        share = width // 8
        source = slot_row(row_ids((width, width)), own_rows, width)
        turn = (lane_ids((width, width)) == source).astype(BF16)
        turned = jnp.dot(turn, weight_sum[...].astype(BF16), preferred_element_type=F32).astype(BF16)
        for p in range(8):
            send_ref[p, 0:share, :] = turned[p * share : (p + 1) * share, :]
            send_ref[p, share : share + PRED_SLOT, :] = pred_sum[p * PRED_SLOT : (p + 1) * PRED_SLOT, :].astype(BF16)


def params():
    return pltpu.CompilerParams(dimension_semantics=("arbitrary",), vmem_limit_bytes=VMEM_BYTES)


def whole(shape):
    return pl.BlockSpec(shape, lambda i: (0,) * len(shape))


smem = pl.BlockSpec(memory_space=pltpu.SMEM)


def exchange(blocks, axes):
    return lax.all_to_all(blocks, axes, 0, 0, tiled=True)


def share_copies(block, axes):
    count = lax.axis_size(axes)
    return exchange(jnp.broadcast_to(block[None], (count, *block.shape)), axes)


def per_device(encoder, predictor, starts, frame_lengths, label_lengths, labels, w_out):
    utt_count, frame_count, width = encoder.shape
    own_rows, vocab = w_out.shape
    label_rows = predictor.shape[1]
    tm_index = lax.axis_index(TM)
    tm_count = lax.axis_size(TM)
    near, far = lax.axis_size(NEAR), lax.axis_size(FAR)
    piece = own_rows // tm_count
    padded = -(-vocab // LANES) * LANES
    fold = piece * padded // LANES
    share = width // tm_count
    rows = S * utt_count * frame_count
    shape = jax.ShapeDtypeStruct

    mine = lax.dynamic_slice_in_dim(w_out, tm_index * piece, piece, axis=0)
    mine = jnp.pad(mine, ((0, 0), (0, padded - vocab))).reshape(fold, LANES)
    held = share_copies(mine, FAR).reshape(far * piece, padded)
    held = share_copies(held, NEAR).reshape(share, padded)
    gathered = share_copies(held, TM).reshape(width, padded)
    block = tm_index.reshape(1).astype(jnp.int32)

    hidden, label_ids = pl.pallas_call(
        hidden_kernel,
        grid=(STEPS,),
        in_specs=[
            whole(starts.shape),
            whole(labels.shape),
            whole((utt_count * frame_count, width)),
            whole(predictor.shape),
        ],
        out_specs=[pl.BlockSpec((width, WIDE), lambda i: (0, i)), whole((S, LANES))],
        out_shape=[shape((width, rows), BF16), shape((S, LANES), jnp.int32)],
        scratch_shapes=[
            pltpu.VMEM((width, LANES), F32),
            pltpu.VMEM((width, 2 * PRED_PAD), BF16),
            pltpu.VMEM((2 * PRED_PAD, width), F32),
        ],
        compiler_params=params(),
        cost_estimate=pl.CostEstimate(
            flops=2 * 2 * PRED_PAD * width * rows, bytes_accessed=3 * 2**20, transcendentals=width * rows
        ),
    )(starts, labels, encoder.reshape(-1, width), predictor)

    levels = frame_count.bit_length() - 1
    exps, weights, lps, tree, payload = pl.pallas_call(
        functools.partial(forward_kernel, own_rows, vocab),
        grid=(STEPS,),
        in_specs=[
            whole(starts.shape),
            smem,
            smem,
            smem,
            whole((S, LANES)),
            whole((width, padded)),
            pl.BlockSpec((width, WIDE), lambda i: (0, i)),
        ],
        out_specs=[
            pl.BlockSpec((padded, WIDE), lambda i: (0, i)),
            whole((width, padded)),
            whole((3, S, LANES)),
            whole((levels, S, S, LANES)),
            whole((8, LANES)),
        ],
        out_shape=[
            shape((padded, rows), F32),
            shape((width, padded), BF16),
            shape((3, S, LANES), F32),
            shape((levels, S, S, LANES), F32),
            shape((8, LANES), F32),
        ],
        scratch_shapes=[
            pltpu.VMEM((padded, width), BF16),
            pltpu.VMEM((S, S, LANES), F32),
        ],
        compiler_params=params(),
        cost_estimate=pl.CostEstimate(
            flops=2 * padded * width * rows, bytes_accessed=8 * 2**20, transcendentals=padded * rows
        ),
    )(starts, frame_lengths, label_lengths, block, label_ids, gathered, hidden)

    blocks = share_copies(payload, TM)

    losses, grad_encoder, send = pl.pallas_call(
        functools.partial(backward_kernel, own_rows, label_rows),
        grid=(STEPS,),
        in_specs=[
            whole(starts.shape),
            smem,
            smem,
            smem,
            whole((tm_count, 8, LANES)),
            whole((3, S, LANES)),
            whole((levels, S, S, LANES)),
            whole((S, LANES)),
            whole((width, padded)),
            pl.BlockSpec((width, WIDE), lambda i: (0, i)),
            pl.BlockSpec((padded, WIDE), lambda i: (0, i)),
        ],
        out_specs=[
            smem,
            whole((utt_count * frame_count, width)),
            whole((tm_count, share + PRED_SLOT, padded)),
        ],
        out_shape=[
            shape((utt_count,), F32),
            shape((utt_count * frame_count, width), BF16),
            shape((tm_count, share + PRED_SLOT, padded), BF16),
        ],
        scratch_shapes=[
            pltpu.VMEM((S, S, LANES), F32),
            pltpu.VMEM((2, LANES, LANES), F32),
            pltpu.VMEM((S, LANES), F32),
            pltpu.VMEM((2, S, LANES), F32),
            pltpu.VMEM((width, LANES), F32),
            pltpu.VMEM((8 * PRED_SLOT, width), F32),
            pltpu.VMEM((width, padded), F32),
        ],
        compiler_params=params(),
        cost_estimate=pl.CostEstimate(
            flops=6 * padded * width * rows, bytes_accessed=8 * 2**20, transcendentals=2**16
        ),
    )(starts, frame_lengths, label_lengths, block, blocks, lps, tree, label_ids, weights, hidden, exps)

    block_sum = jnp.sum(exchange(send, TM).astype(F32), axis=0)
    pred_rows = block_sum[share : share + PRED_SHARE]
    near_sum = jnp.sum(exchange(block_sum[:share].reshape(near, share // near, padded), NEAR), axis=0)
    own_weight = jnp.sum(exchange(near_sum.reshape(far, fold, LANES), FAR), axis=0).reshape(piece, padded)
    final = share_copies(jnp.concatenate([pred_rows, own_weight], axis=0), TM)
    grad_predictor = final[:, :PRED_SHARE].reshape(-1, width)[: utt_count * label_rows]
    grad_predictor = grad_predictor.reshape(utt_count, label_rows, width)
    grad_w_out = final[:, PRED_SHARE:, :vocab].reshape(own_rows, vocab)
    return (losses, grad_encoder.reshape(encoder.shape), grad_predictor, grad_w_out)


def finer(mesh):
    sizes = (4, 2, 4, 8, 2) if mesh.shape["utt"] == 64 else (4, 2, 1, 1, 1)
    return jax.sharding.Mesh(mesh.devices.reshape(sizes), (*TM, "x", FAR, "zl"))


def solution(mesh):
    utt = ("x", FAR, "zl")
    return jax.shard_map(
        per_device,
        mesh=finer(mesh),
        in_specs=(
            P(utt, TM, None),
            P(utt, None, None),
            P(utt, TM),
            P(utt),
            P(utt),
            P(utt, None),
            P(utt, None),
        ),
        out_specs=(P(utt), P(utt, TM, None), P(utt, None, None), P(utt, None)),
        check_vma=False,
    )
```

```python
import functools

import jax
import jax.numpy as jnp
from jax import lax
from jax.experimental import pallas as pl
from jax.experimental.pallas import tpu as pltpu
from jax.sharding import PartitionSpec as P

S = 16
LANES = 128
GROUP = 4
STEPS = S // GROUP
WIDE = GROUP * LANES
PRED_PAD = 80
VMEM_BYTES = 40 * 2**20

masked_log = -1e30

F32 = jnp.float32
BF16 = jnp.bfloat16

PRED_SHARE = 17
PRED_SLOT = 32
TM = "tm"
UTT = "utt"

NT_DIMS = (((1,), (1,)), ((), ()))


def lane_ids(shape=(1, LANES)):
    return lax.broadcasted_iota(jnp.int32, shape, 1)


def row_ids(shape):
    return lax.broadcasted_iota(jnp.int32, shape, 0)


def per_lane(half, low, high):
    return jnp.where(lane_ids() < half, low, high)


def rows_to_lanes(pair):
    return jnp.concatenate([pair[0:1, :], pair[1:2, :]], axis=1)


def balanced(combine, terms):
    while len(terms) > 1:
        terms = [combine(a, b) for a, b in zip(terms[0::2], terms[1::2])]
    return terms[0]


def rowwise_logsumexp(terms):
    top = balanced(jnp.maximum, terms)
    total = balanced(jnp.add, [jnp.exp(t - top) for t in terms])
    return top + jnp.log(total)


def vector_times(vector, matrix):
    return rowwise_logsumexp([vector[i : i + 1, :] + matrix[i] for i in range(S)])


def times_vector(matrix, vector, rows_ref):
    for i in range(S):
        terms = matrix[i] + vector
        top = jnp.max(terms, axis=0, keepdims=True)
        total = jnp.sum(jnp.exp(terms - top), axis=0, keepdims=True)
        rows_ref[i : i + 1, :] = top + jnp.log(total)
    return rows_ref[...]


def window_down(vector, distance):
    places = row_ids((S, LANES))
    for bit in (1, 2, 4, 8):
        moved = jnp.where(places < S - bit, pltpu.roll(vector, S - bit, 0), masked_log)
        vector = jnp.where((distance & bit) != 0, moved, vector)
    return vector


def window_up(vector, distance):
    places = row_ids((S, LANES))
    for bit in (1, 2, 4, 8):
        moved = jnp.where(places >= bit, pltpu.roll(vector, bit, 0), masked_log)
        vector = jnp.where((distance & bit) != 0, moved, vector)
    return vector


def slot_row(slot, own_rows, width):
    if own_rows != 8:
        return slot
    share = width // 8
    return slot % share * own_rows + slot // share


def frame_shifts(starts, half):
    lanes = lane_ids()
    first = (lanes == 0) | (lanes == half)
    return jnp.where(first, 0, starts - pltpu.roll(starts, 1, 1))


def span_rows(blank, emit):
    places = row_ids((S, LANES))
    spans = jnp.zeros((S, LANES), F32)
    rows = [None] * S
    for e in reversed(range(S)):
        spans = jnp.where(places > e, spans + emit[e : e + 1, :], 0.0)
        rows[e] = jnp.where(places >= e, spans + blank, masked_log)
    return rows


def hidden_kernel(starts_ref, labels_ref, enc_ref, pred_ref, hidden_ref, label_ref, enc_t, pred_t, stack):
    step = pl.program_id(0)
    half = starts_ref.shape[1]
    starts = rows_to_lanes(starts_ref[...])

    @pl.when(step == 0)
    def _():
        enc_t[...] = jnp.transpose(enc_ref[...].astype(F32))
        stack[...] = jnp.zeros_like(stack)
        rows = pred_ref.shape[1]
        stack[0:rows, :] = pred_ref[0].astype(F32)
        stack[PRED_PAD : PRED_PAD + rows, :] = pred_ref[1].astype(F32)
        pred_t[...] = jnp.transpose(stack[...]).astype(BF16)
        cap = labels_ref.shape[1]
        labels = labels_ref[...].astype(F32)
        table = [jnp.transpose(jnp.broadcast_to(labels[b : b + 1, :], (LANES, cap))) for b in range(2)]
        table = jnp.where(lane_ids((cap, LANES)) < half, table[0], table[1])
        places = row_ids((cap, LANES))
        for k in range(S):
            wanted = jnp.minimum(starts + k, cap - 1)
            label_ref[k : k + 1, :] = jnp.sum(
                jnp.where(places == wanted, table, 0.0), axis=0, keepdims=True
            ).astype(jnp.int32)

    base = starts + per_lane(half, 0, PRED_PAD) + step * GROUP
    wanted = jnp.concatenate([base + k for k in range(GROUP)], axis=1)
    match = (row_ids((2 * PRED_PAD, WIDE)) == wanted).astype(BF16)
    picked = jnp.dot(pred_t[...], match, preferred_element_type=F32)
    for k in range(GROUP):
        part = slice(k * LANES, (k + 1) * LANES)
        hidden_ref[:, part] = jnp.tanh(enc_t[...] + picked[:, part]).astype(BF16)


def forward_kernel(
    own_rows,
    vocab,
    starts_ref,
    frames_ref,
    labels_len_ref,
    block_ref,
    label_ref,
    gathered_ref,
    hidden_ref,
    exps_ref,
    weights_ref,
    lps_ref,
    tree_ref,
    payload_ref,
    weights_t,
    root,
):
    step = pl.program_id(0)
    width = gathered_ref.shape[0]

    @pl.when(step == 0)
    def _():
        source = slot_row(lane_ids((width, width)), own_rows, width)
        turn = (row_ids((width, width)) == source).astype(BF16)
        weights = jnp.dot(turn, gathered_ref[...], preferred_element_type=F32)
        weights_ref[...] = weights.astype(BF16)
        weights_t[...] = jnp.transpose(weights).astype(BF16)

    logits = jnp.dot(weights_t[...], hidden_ref[...], preferred_element_type=F32)
    padded = logits.shape[0]
    edge = padded - 16
    tail = jnp.where(row_ids((16, WIDE)) < vocab - edge, logits[edge:], masked_log)
    logits = jnp.concatenate([logits[:edge], tail], axis=0)
    top = jnp.max(logits, axis=0, keepdims=True)
    exps = jnp.exp(logits - top)
    exps_ref[...] = exps
    total = jnp.sum(exps, axis=0, keepdims=True)
    norm = top + jnp.log(total)
    scale = 1.0 / total
    names = jnp.concatenate([label_ref[pl.ds(step * GROUP + k, 1), :] for k in range(GROUP)], axis=1)
    emit = jnp.sum(jnp.where(row_ids((padded, WIDE)) == names, logits, 0.0), axis=0, keepdims=True) - norm
    blank = logits[0:1, :] - norm
    for k in range(GROUP):
        part = slice(k * LANES, (k + 1) * LANES)
        row = pl.ds(step * GROUP + k, 1)
        lps_ref[0, row, :] = blank[:, part]
        lps_ref[1, row, :] = emit[:, part]
        lps_ref[2, row, :] = scale[:, part]

    @pl.when(step == STEPS - 1)
    def _():
        half = starts_ref.shape[1]
        lanes = lane_ids()
        starts = rows_to_lanes(starts_ref[...])
        frame = block_ref[0] * half + lanes % half
        live = frame < per_lane(half, frames_ref[0], frames_ref[1])
        limit = per_lane(half, labels_len_ref[0], labels_len_ref[1])
        allowed = live & (row_ids((S, LANES)) + starts < limit)
        blank = jnp.where(live, lps_ref[0], 0.0)
        emit = jnp.where(allowed, lps_ref[1], masked_log)
        lps_ref[0] = blank
        lps_ref[1] = emit
        shift = frame_shifts(starts, half)
        rows = span_rows(blank, emit)
        for bit in (1, 2, 4, 8):
            moved = (shift & bit) != 0
            rows = [
                jnp.where(moved, rows[i - bit] if i >= bit else masked_log, rows[i]) for i in range(S)
            ]
        for i in range(S):
            tree_ref[0, i] = rows[i]
        levels = half.bit_length() - 1
        for level in range(levels):
            reach = 1 << level
            late = lanes % (2 * reach) == reach
            back = LANES - reach
            latter = [tree_ref[level, m] for m in range(S)]
            latter = [jnp.where(late, one, pltpu.roll(one, back, 1)) for one in latter]

            def product(i, carry, level=level, reach=reach, late=late, back=back, latter=latter):
                former = jnp.where(late, pltpu.roll(tree_ref[level, i + S // 2], reach, 1), tree_ref[level, i])
                row = rowwise_logsumexp([former[m : m + 1, :] + latter[m] for m in range(S)])
                if level + 1 < levels:
                    tree_ref[level + 1, i] = row
                    tree_ref[level + 1, i + S // 2] = pltpu.roll(row, back, 1)
                else:
                    root[i] = row
                    root[i + S // 2] = pltpu.roll(row, back, 1)
                return carry

            lax.fori_loop(0, S // 2, product, 0, unroll=4)
        flat = jnp.transpose(root[...].reshape(S * S, LANES))
        payload_ref[...] = jnp.zeros_like(payload_ref)
        for b in range(2):
            line = flat[b * half : b * half + 1, :]
            payload_ref[4 * b : 4 * b + 1, :] = line[:, :LANES]
            payload_ref[4 * b + 1 : 4 * b + 2, :] = line[:, LANES:]
            for end, at in ((2, half - 1), (3, 0)):
                edge_start = starts_ref[b : b + 1, at : at + 1].astype(F32)
                payload_ref[4 * b + end : 4 * b + end + 1, :] = jnp.broadcast_to(edge_start, (1, LANES))


def backward_kernel(
    own_rows,
    label_rows,
    starts_ref,
    frames_ref,
    labels_len_ref,
    block_ref,
    blocks_ref,
    lps_ref,
    tree_ref,
    label_ref,
    weights_ref,
    hidden_ref,
    exps_ref,
    losses_ref,
    grad_enc_ref,
    send_ref,
    chain,
    line_up,
    rows_ref,
    grads,
    enc_sum,
    pred_sum,
    weight_sum,
):
    step = pl.program_id(0)
    half = starts_ref.shape[1]
    width = weights_ref.shape[0]
    count = blocks_ref.shape[0]
    lanes = lane_ids()

    @pl.when(step == 0)
    def _():
        places = row_ids((S, LANES))
        line_up[...] = jnp.zeros_like(line_up)
        ends = jnp.zeros((1, LANES), F32)
        begins = jnp.zeros((1, LANES), F32)
        for r in range(count):
            for b in range(2):
                at = 2 * r + b
                line_up[0, at : at + 1, :] = blocks_ref[r, 4 * b : 4 * b + 1, :]
                line_up[1, at : at + 1, :] = blocks_ref[r, 4 * b + 1 : 4 * b + 2, :]
                ends = jnp.where(lanes == at, blocks_ref[r, 4 * b + 2 : 4 * b + 3, :], ends)
                begins = jnp.where(lanes == at, blocks_ref[r, 4 * b + 3 : 4 * b + 4, :], begins)
        for h in range(2):
            chain[h * S // 2 : (h + 1) * S // 2] = jnp.transpose(line_up[h]).reshape(S // 2, S, LANES)
        odd = lanes % 2 == 1
        last_start = [blocks_ref[count - 1, 4 * b + 2 : 4 * b + 3, :].astype(jnp.int32) for b in range(2)]
        final_place = jnp.where(odd, labels_len_ref[1] - last_start[1], labels_len_ref[0] - last_start[0])
        gap = (begins - pltpu.roll(ends, 2, 1)).astype(jnp.int32)
        gap = jnp.where((lanes >= 2) & (lanes < 2 * count), gap, 0)
        forward = jnp.where(places == 0, 0.0, masked_log) + jnp.zeros((S, LANES), F32)
        closing = jnp.where(places == final_place, 0.0, masked_log)
        backward = closing
        owner = lanes // 2
        for turn in range(count - 1):
            ahead = window_down(pltpu.roll(vector_times(forward, chain), 2, 1), gap)
            forward = jnp.where(owner == turn + 1, ahead, forward)
            behind = pltpu.roll(window_up(times_vector(chain, backward, rows_ref), gap), LANES - 2, 1)
            backward = jnp.where(owner == count - 2 - turn, behind, backward)
        leaving = vector_times(forward, chain) + closing
        best = jnp.max(leaving, axis=0, keepdims=True)
        log_total = best + jnp.log(jnp.sum(jnp.exp(leaving - best), axis=0, keepdims=True))
        for b in range(2):
            own_total = jnp.sum(jnp.where(lanes == 2 * (count - 1) + b, log_total, 0.0))
            losses_ref[b] = -own_total / frames_ref[b].astype(F32)

        def own_boundary(vectors):
            columns = [
                jnp.sum(jnp.where(lanes == 2 * block_ref[0] + b, vectors, 0.0), axis=1, keepdims=True)
                for b in range(2)
            ]
            spread = jnp.where(lanes < half, columns[0], columns[1])
            return spread - jnp.max(spread, axis=0, keepdims=True)

        alpha = own_boundary(forward)
        beta = own_boundary(backward)
        levels = half.bit_length() - 1
        for level in reversed(range(levels)):
            reach = 1 << level
            later = lanes % (2 * reach) == reach
            ahead = pltpu.roll(vector_times(alpha, tree_ref.at[level]), reach, 1)
            alpha = jnp.where(later, ahead, alpha)
            beta_late = pltpu.roll(beta, reach, 1)
            behind = times_vector(tree_ref.at[level], beta_late, rows_ref)
            beta = jnp.where(later, beta_late, pltpu.roll(behind, LANES - reach, 1))
        starts = rows_to_lanes(starts_ref[...])
        alpha = window_down(alpha, frame_shifts(starts, half))
        spans = span_rows(lps_ref[0], lps_ref[1])
        scores = [spans[e] + alpha[e : e + 1, :] + beta for e in range(S)]
        best = jnp.max(functools.reduce(jnp.maximum, scores), axis=0, keepdims=True)
        weights = [jnp.exp(score - best) for score in scores]
        for e in range(1, S):
            weights[e] = weights[e] + weights[e - 1]
        total = jnp.sum(weights[S - 1], axis=0, keepdims=True)
        negative = -1.0 / total
        grads[0] = weights[S - 1] * negative
        for m in range(S):
            crossing = jnp.sum(jnp.where(places > m, weights[m], 0.0), axis=0, keepdims=True)
            grads[1, m : m + 1, :] = crossing * negative
        enc_sum[...] = jnp.zeros_like(enc_sum)
        pred_sum[...] = jnp.zeros_like(pred_sum)
        weight_sum[...] = jnp.zeros_like(weight_sum)

    def wide(ref, *lead):
        return jnp.concatenate([ref[(*lead, pl.ds(step * GROUP + k, 1), slice(None))] for k in range(GROUP)], axis=1)

    names = wide(label_ref)
    grad_blank = wide(grads, 0)
    grad_emit = wide(grads, 1)
    spread = (grad_blank + grad_emit) * wide(lps_ref, 2)
    padded = exps_ref.shape[0]
    ids = row_ids((padded, WIDE))
    coeff = jnp.where(ids == names, grad_emit, jnp.where(ids == 0, grad_blank, 0.0))
    grad_logits = (coeff - exps_ref[...] * spread).astype(BF16)
    grad_hidden = jnp.dot(weights_ref[...], grad_logits, preferred_element_type=F32)
    hidden = hidden_ref[...]
    hidden_wide = hidden.astype(F32)
    grad_summed = grad_hidden * (1.0 - hidden_wide * hidden_wide)
    enc_sum[...] += functools.reduce(
        lambda a, b: a + b, [grad_summed[:, k * LANES : (k + 1) * LANES] for k in range(GROUP)]
    )
    starts = rows_to_lanes(starts_ref[...])
    base = starts + step * GROUP
    rows = jnp.concatenate([base + k for k in range(GROUP)], axis=1)
    wanted = rows + jnp.concatenate([per_lane(half, 0, label_rows)] * GROUP, axis=1)
    slot = row_ids((8 * PRED_SLOT, WIDE))
    match = (slot // PRED_SLOT * PRED_SHARE + slot % PRED_SLOT == wanted) & (slot % PRED_SLOT < PRED_SHARE)
    pred_sum[...] += lax.dot_general(
        match.astype(BF16), grad_summed.astype(BF16), NT_DIMS, preferred_element_type=F32
    )
    weight_sum[...] += lax.dot_general(hidden, grad_logits, NT_DIMS, preferred_element_type=F32)

    @pl.when(step == STEPS - 1)
    def _():
        grad_enc_ref[...] = jnp.transpose(enc_sum[...]).astype(BF16)
        share = width // 8
        source = slot_row(row_ids((width, width)), own_rows, width)
        turn = (lane_ids((width, width)) == source).astype(BF16)
        turned = jnp.dot(turn, weight_sum[...].astype(BF16), preferred_element_type=F32).astype(BF16)
        for p in range(8):
            send_ref[p, 0:share, :] = turned[p * share : (p + 1) * share, :]
            send_ref[p, share : share + PRED_SLOT, :] = pred_sum[p * PRED_SLOT : (p + 1) * PRED_SLOT, :].astype(BF16)


def params():
    return pltpu.CompilerParams(dimension_semantics=("arbitrary",), vmem_limit_bytes=VMEM_BYTES)


def whole(shape):
    return pl.BlockSpec(shape, lambda i: (0,) * len(shape))


smem = pl.BlockSpec(memory_space=pltpu.SMEM)


def exchange(blocks, axes):
    return lax.all_to_all(blocks, axes, 0, 0, tiled=True)


def share_copies(block, axes):
    count = lax.axis_size(axes)
    return exchange(jnp.broadcast_to(block[None], (count, *block.shape)), axes)


def per_device(encoder, predictor, starts, frame_lengths, label_lengths, labels, w_out):
    utt_count, frame_count, width = encoder.shape
    own_rows, vocab = w_out.shape
    label_rows = predictor.shape[1]
    tm_index = lax.axis_index(TM)
    tm_count = lax.axis_size(TM)
    utt_size = lax.axis_size(UTT)
    piece = own_rows // tm_count
    padded = -(-vocab // LANES) * LANES
    fold = piece * padded // LANES
    share = width // tm_count
    rows = S * utt_count * frame_count
    shape = jax.ShapeDtypeStruct

    mine = lax.dynamic_slice_in_dim(w_out, tm_index * piece, piece, axis=0)
    mine = jnp.pad(mine, ((0, 0), (0, padded - vocab))).reshape(fold, LANES)
    held = share_copies(mine, UTT).reshape(share, padded)
    gathered = share_copies(held, TM).reshape(width, padded)
    block = tm_index.reshape(1).astype(jnp.int32)

    hidden, label_ids = pl.pallas_call(
        hidden_kernel,
        grid=(STEPS,),
        in_specs=[
            whole(starts.shape),
            whole(labels.shape),
            whole((utt_count * frame_count, width)),
            whole(predictor.shape),
        ],
        out_specs=[pl.BlockSpec((width, WIDE), lambda i: (0, i)), whole((S, LANES))],
        out_shape=[shape((width, rows), BF16), shape((S, LANES), jnp.int32)],
        scratch_shapes=[
            pltpu.VMEM((width, LANES), F32),
            pltpu.VMEM((width, 2 * PRED_PAD), BF16),
            pltpu.VMEM((2 * PRED_PAD, width), F32),
        ],
        compiler_params=params(),
        cost_estimate=pl.CostEstimate(
            flops=2 * 2 * PRED_PAD * width * rows, bytes_accessed=3 * 2**20, transcendentals=width * rows
        ),
    )(starts, labels, encoder.reshape(-1, width), predictor)

    levels = frame_count.bit_length() - 1
    exps, weights, lps, tree, payload = pl.pallas_call(
        functools.partial(forward_kernel, own_rows, vocab),
        grid=(STEPS,),
        in_specs=[
            whole(starts.shape),
            smem,
            smem,
            smem,
            whole((S, LANES)),
            whole((width, padded)),
            pl.BlockSpec((width, WIDE), lambda i: (0, i)),
        ],
        out_specs=[
            pl.BlockSpec((padded, WIDE), lambda i: (0, i)),
            whole((width, padded)),
            whole((3, S, LANES)),
            whole((levels, S, S, LANES)),
            whole((8, LANES)),
        ],
        out_shape=[
            shape((padded, rows), F32),
            shape((width, padded), BF16),
            shape((3, S, LANES), F32),
            shape((levels, S, S, LANES), F32),
            shape((8, LANES), F32),
        ],
        scratch_shapes=[
            pltpu.VMEM((padded, width), BF16),
            pltpu.VMEM((S, S, LANES), F32),
        ],
        compiler_params=params(),
        cost_estimate=pl.CostEstimate(
            flops=2 * padded * width * rows, bytes_accessed=8 * 2**20, transcendentals=padded * rows
        ),
    )(starts, frame_lengths, label_lengths, block, label_ids, gathered, hidden)

    blocks = share_copies(payload, TM)

    losses, grad_encoder, send = pl.pallas_call(
        functools.partial(backward_kernel, own_rows, label_rows),
        grid=(STEPS,),
        in_specs=[
            whole(starts.shape),
            smem,
            smem,
            smem,
            whole((tm_count, 8, LANES)),
            whole((3, S, LANES)),
            whole((levels, S, S, LANES)),
            whole((S, LANES)),
            whole((width, padded)),
            pl.BlockSpec((width, WIDE), lambda i: (0, i)),
            pl.BlockSpec((padded, WIDE), lambda i: (0, i)),
        ],
        out_specs=[
            smem,
            whole((utt_count * frame_count, width)),
            whole((tm_count, share + PRED_SLOT, padded)),
        ],
        out_shape=[
            shape((utt_count,), F32),
            shape((utt_count * frame_count, width), BF16),
            shape((tm_count, share + PRED_SLOT, padded), BF16),
        ],
        scratch_shapes=[
            pltpu.VMEM((S, S, LANES), F32),
            pltpu.VMEM((2, LANES, LANES), F32),
            pltpu.VMEM((S, LANES), F32),
            pltpu.VMEM((2, S, LANES), F32),
            pltpu.VMEM((width, LANES), F32),
            pltpu.VMEM((8 * PRED_SLOT, width), F32),
            pltpu.VMEM((width, padded), F32),
        ],
        compiler_params=params(),
        cost_estimate=pl.CostEstimate(
            flops=6 * padded * width * rows, bytes_accessed=8 * 2**20, transcendentals=2**16
        ),
    )(starts, frame_lengths, label_lengths, block, blocks, lps, tree, label_ids, weights, hidden, exps)

    block_sum = jnp.sum(exchange(send, TM).astype(F32), axis=0)
    pred_rows = share_copies(block_sum[share : share + PRED_SHARE], TM)
    weight_rows = exchange(block_sum[:share].reshape(utt_size, fold, LANES), UTT)
    pred_rows, weight_rows = lax.optimization_barrier((pred_rows, weight_rows))
    grad_w_out = share_copies(jnp.sum(weight_rows, axis=0), TM).reshape(own_rows, padded)
    grad_predictor = pred_rows.reshape(-1, width)[: utt_count * label_rows]
    grad_predictor = grad_predictor.reshape(utt_count, label_rows, width)
    return (losses, grad_encoder.reshape(encoder.shape), grad_predictor, grad_w_out[:, :vocab])


def solution(mesh):
    return jax.shard_map(
        per_device,
        mesh=mesh,
        in_specs=(
            P(UTT, TM, None),
            P(UTT, None, None),
            P(UTT, TM),
            P(UTT),
            P(UTT),
            P(UTT, None),
            P(UTT, None),
        ),
        out_specs=(P(UTT), P(UTT, TM, None), P(UTT, None, None), P(UTT, None)),
        check_vma=False,
    )
```

```python
import functools

import jax
import jax.numpy as jnp
from jax import lax
from jax.experimental import pallas as pl
from jax.experimental.pallas import tpu as pltpu
from jax.sharding import PartitionSpec as P

S = 16
LANES = 128
GROUP = 4
STEPS = S // GROUP
WIDE = GROUP * LANES
PRED_PAD = 80
VMEM_BYTES = 40 * 2**20

masked_log = -1e30

F32 = jnp.float32
BF16 = jnp.bfloat16

PRED_SHARE = 17
PRED_SLOT = 32
TM = "tm"
UTT = "utt"

NT_DIMS = (((1,), (1,)), ((), ()))


def lane_ids(shape=(1, LANES)):
    return lax.broadcasted_iota(jnp.int32, shape, 1)


def row_ids(shape):
    return lax.broadcasted_iota(jnp.int32, shape, 0)


def per_lane(half, low, high):
    return jnp.where(lane_ids() < half, low, high)


def rows_to_lanes(pair):
    return jnp.concatenate([pair[0:1, :], pair[1:2, :]], axis=1)


def balanced(combine, terms):
    while len(terms) > 1:
        terms = [combine(a, b) for a, b in zip(terms[0::2], terms[1::2])]
    return terms[0]


def rowwise_logsumexp(terms):
    top = balanced(jnp.maximum, terms)
    total = balanced(jnp.add, [jnp.exp(t - top) for t in terms])
    return top + jnp.log(total)


def vector_times(vector, matrix):
    return rowwise_logsumexp([vector[i : i + 1, :] + matrix[i] for i in range(S)])


def times_vector(matrix, vector, rows_ref):
    for i in range(S):
        terms = matrix[i] + vector
        top = jnp.max(terms, axis=0, keepdims=True)
        total = jnp.sum(jnp.exp(terms - top), axis=0, keepdims=True)
        rows_ref[i : i + 1, :] = top + jnp.log(total)
    return rows_ref[...]


def window_down(vector, distance):
    places = row_ids((S, LANES))
    for bit in (1, 2, 4, 8):
        moved = jnp.where(places < S - bit, pltpu.roll(vector, S - bit, 0), masked_log)
        vector = jnp.where((distance & bit) != 0, moved, vector)
    return vector


def window_up(vector, distance):
    places = row_ids((S, LANES))
    for bit in (1, 2, 4, 8):
        moved = jnp.where(places >= bit, pltpu.roll(vector, bit, 0), masked_log)
        vector = jnp.where((distance & bit) != 0, moved, vector)
    return vector


def slot_row(slot, own_rows, width):
    if own_rows != 8:
        return slot
    share = width // 8
    return slot % share * own_rows + slot // share


def frame_shifts(starts, half):
    lanes = lane_ids()
    first = (lanes == 0) | (lanes == half)
    return jnp.where(first, 0, starts - pltpu.roll(starts, 1, 1))


def span_rows(blank, emit):
    places = row_ids((S, LANES))
    spans = jnp.zeros((S, LANES), F32)
    rows = [None] * S
    for e in reversed(range(S)):
        spans = jnp.where(places > e, spans + emit[e : e + 1, :], 0.0)
        rows[e] = jnp.where(places >= e, spans + blank, masked_log)
    return rows


def reorder(own_rows, width):
    source = slot_row(row_ids((width, width)), own_rows, width)
    return (lane_ids((width, width)) == source).astype(BF16)


def hidden_kernel(own_rows, starts_ref, labels_ref, enc_ref, pred_ref, hidden_ref, label_ref, enc_t, pred_t, stack):
    step = pl.program_id(0)
    half = starts_ref.shape[1]
    starts = rows_to_lanes(starts_ref[...])

    @pl.when(step == 0)
    def _():
        turn = reorder(own_rows, enc_ref.shape[1])
        enc_t[...] = lax.dot_general(turn, enc_ref[...], NT_DIMS, preferred_element_type=F32)
        stack[...] = jnp.zeros_like(stack)
        rows = pred_ref.shape[1]
        stack[0:rows, :] = pred_ref[0].astype(F32)
        stack[PRED_PAD : PRED_PAD + rows, :] = pred_ref[1].astype(F32)
        pred_t[...] = lax.dot_general(
            turn, stack[...].astype(BF16), NT_DIMS, preferred_element_type=F32
        ).astype(BF16)
        cap = labels_ref.shape[1]
        labels = labels_ref[...].astype(F32)
        table = [jnp.transpose(jnp.broadcast_to(labels[b : b + 1, :], (LANES, cap))) for b in range(2)]
        table = jnp.where(lane_ids((cap, LANES)) < half, table[0], table[1])
        places = row_ids((cap, LANES))
        for k in range(S):
            wanted = jnp.minimum(starts + k, cap - 1)
            label_ref[k : k + 1, :] = jnp.sum(
                jnp.where(places == wanted, table, 0.0), axis=0, keepdims=True
            ).astype(jnp.int32)

    base = starts + per_lane(half, 0, PRED_PAD) + step * GROUP
    wanted = jnp.concatenate([base + k for k in range(GROUP)], axis=1)
    match = (row_ids((2 * PRED_PAD, WIDE)) == wanted).astype(BF16)
    picked = jnp.dot(pred_t[...], match, preferred_element_type=F32)
    for k in range(GROUP):
        part = slice(k * LANES, (k + 1) * LANES)
        hidden_ref[:, part] = jnp.tanh(enc_t[...] + picked[:, part]).astype(BF16)


def forward_kernel(
    vocab,
    starts_ref,
    frames_ref,
    labels_len_ref,
    block_ref,
    label_ref,
    gathered_ref,
    hidden_ref,
    exps_ref,
    lps_ref,
    tree_ref,
    payload_ref,
    weights_t,
    former,
    root,
):
    step = pl.program_id(0)

    @pl.when(step == 0)
    def _():
        weights_t[...] = jnp.transpose(gathered_ref[...])

    logits = jnp.dot(weights_t[...], hidden_ref[...], preferred_element_type=F32)
    padded = logits.shape[0]
    edge = padded - 16
    tail = jnp.where(row_ids((16, WIDE)) < vocab - edge, logits[edge:], masked_log)
    logits = jnp.concatenate([logits[:edge], tail], axis=0)
    top = jnp.max(logits, axis=0, keepdims=True)
    exps = jnp.exp(logits - top)
    exps_ref[...] = exps
    total = jnp.sum(exps, axis=0, keepdims=True)
    norm = top + jnp.log(total)
    scale = 1.0 / total
    names = jnp.concatenate([label_ref[pl.ds(step * GROUP + k, 1), :] for k in range(GROUP)], axis=1)
    emit = jnp.sum(jnp.where(row_ids((padded, WIDE)) == names, logits, 0.0), axis=0, keepdims=True) - norm
    blank = logits[0:1, :] - norm
    for k in range(GROUP):
        part = slice(k * LANES, (k + 1) * LANES)
        row = pl.ds(step * GROUP + k, 1)
        lps_ref[0, row, :] = blank[:, part]
        lps_ref[1, row, :] = emit[:, part]
        lps_ref[2, row, :] = scale[:, part]

    @pl.when(step == STEPS - 1)
    def _():
        half = starts_ref.shape[1]
        lanes = lane_ids()
        starts = rows_to_lanes(starts_ref[...])
        frame = block_ref[0] * half + lanes % half
        live = frame < per_lane(half, frames_ref[0], frames_ref[1])
        limit = per_lane(half, labels_len_ref[0], labels_len_ref[1])
        allowed = live & (row_ids((S, LANES)) + starts < limit)
        blank = jnp.where(live, lps_ref[0], 0.0)
        emit = jnp.where(allowed, lps_ref[1], masked_log)
        lps_ref[0] = blank
        lps_ref[1] = emit
        shift = frame_shifts(starts, half)
        rows = span_rows(blank, emit)
        for bit in (1, 2, 4, 8):
            moved = (shift & bit) != 0
            rows = [
                jnp.where(moved, rows[i - bit] if i >= bit else masked_log, rows[i]) for i in range(S)
            ]
        for i in range(S):
            tree_ref[0, i] = rows[i]
        levels = half.bit_length() - 1
        for level in range(levels):
            reach = 1 << level
            back = LANES - reach
            late = lanes % (2 * reach) == reach
            for i in range(S // 2):
                behind = pltpu.roll(tree_ref[level, i + S // 2], reach, 1)
                former[i] = jnp.where(late, behind, tree_ref[level, i])
            for cut in (slice(0, 8), slice(8, 16)):
                latter = [tree_ref[level, m, cut, :] for m in range(S)]
                latter = [jnp.where(late, one, pltpu.roll(one, back, 1)) for one in latter]

                def product(i, carry, level=level, back=back, latter=latter, cut=cut):
                    row = rowwise_logsumexp([former[i, m : m + 1, :] + latter[m] for m in range(S)])
                    moved = pltpu.roll(row, back, 1)
                    if level + 1 < levels:
                        tree_ref[level + 1, i, cut, :] = row
                        tree_ref[level + 1, i + S // 2, cut, :] = moved
                    else:
                        root[i, cut, :] = row
                        root[i + S // 2, cut, :] = moved
                    return carry

                lax.fori_loop(0, S // 2, product, 0, unroll=2)
        flat = jnp.transpose(root[...].reshape(S * S, LANES))
        payload_ref[...] = jnp.zeros_like(payload_ref)
        for b in range(2):
            line = flat[b * half : b * half + 1, :]
            payload_ref[4 * b : 4 * b + 1, :] = line[:, :LANES]
            payload_ref[4 * b + 1 : 4 * b + 2, :] = line[:, LANES:]
            for end, at in ((2, half - 1), (3, 0)):
                edge_start = starts_ref[b : b + 1, at : at + 1].astype(F32)
                payload_ref[4 * b + end : 4 * b + end + 1, :] = jnp.broadcast_to(edge_start, (1, LANES))


def backward_kernel(
    own_rows,
    label_rows,
    starts_ref,
    frames_ref,
    labels_len_ref,
    block_ref,
    blocks_ref,
    lps_ref,
    tree_ref,
    label_ref,
    weights_ref,
    hidden_ref,
    exps_ref,
    losses_ref,
    grad_enc_ref,
    send_ref,
    chain,
    line_up,
    rows_ref,
    grads,
    enc_sum,
    pred_sum,
    weight_sum,
):
    step = pl.program_id(0)
    half = starts_ref.shape[1]
    width = weights_ref.shape[0]
    count = blocks_ref.shape[0]
    lanes = lane_ids()

    @pl.when(step == 0)
    def _():
        places = row_ids((S, LANES))
        line_up[...] = jnp.zeros_like(line_up)
        ends = jnp.zeros((1, LANES), F32)
        begins = jnp.zeros((1, LANES), F32)
        for r in range(count):
            for b in range(2):
                at = 2 * r + b
                line_up[0, at : at + 1, :] = blocks_ref[r, 4 * b : 4 * b + 1, :]
                line_up[1, at : at + 1, :] = blocks_ref[r, 4 * b + 1 : 4 * b + 2, :]
                ends = jnp.where(lanes == at, blocks_ref[r, 4 * b + 2 : 4 * b + 3, :], ends)
                begins = jnp.where(lanes == at, blocks_ref[r, 4 * b + 3 : 4 * b + 4, :], begins)
        for h in range(2):
            chain[h * S // 2 : (h + 1) * S // 2] = jnp.transpose(line_up[h]).reshape(S // 2, S, LANES)
        odd = lanes % 2 == 1
        last_start = [blocks_ref[count - 1, 4 * b + 2 : 4 * b + 3, :].astype(jnp.int32) for b in range(2)]
        final_place = jnp.where(odd, labels_len_ref[1] - last_start[1], labels_len_ref[0] - last_start[0])
        gap = (begins - pltpu.roll(ends, 2, 1)).astype(jnp.int32)
        gap = jnp.where((lanes >= 2) & (lanes < 2 * count), gap, 0)
        forward = jnp.where(places == 0, 0.0, masked_log) + jnp.zeros((S, LANES), F32)
        closing = jnp.where(places == final_place, 0.0, masked_log)
        backward = closing
        owner = lanes // 2
        for turn in range(count - 1):
            ahead = window_down(pltpu.roll(vector_times(forward, chain), 2, 1), gap)
            forward = jnp.where(owner == turn + 1, ahead, forward)
            behind = pltpu.roll(window_up(times_vector(chain, backward, rows_ref), gap), LANES - 2, 1)
            backward = jnp.where(owner == count - 2 - turn, behind, backward)
        leaving = vector_times(forward, chain) + closing
        best = jnp.max(leaving, axis=0, keepdims=True)
        log_total = best + jnp.log(jnp.sum(jnp.exp(leaving - best), axis=0, keepdims=True))
        for b in range(2):
            own_total = jnp.sum(jnp.where(lanes == 2 * (count - 1) + b, log_total, 0.0))
            losses_ref[b] = -own_total / frames_ref[b].astype(F32)

        def own_boundary(vectors):
            columns = [
                jnp.sum(jnp.where(lanes == 2 * block_ref[0] + b, vectors, 0.0), axis=1, keepdims=True)
                for b in range(2)
            ]
            spread = jnp.where(lanes < half, columns[0], columns[1])
            return spread - jnp.max(spread, axis=0, keepdims=True)

        alpha = own_boundary(forward)
        beta = own_boundary(backward)
        levels = half.bit_length() - 1
        for level in reversed(range(levels)):
            reach = 1 << level
            later = lanes % (2 * reach) == reach
            ahead = pltpu.roll(vector_times(alpha, tree_ref.at[level]), reach, 1)
            alpha = jnp.where(later, ahead, alpha)
            beta_late = pltpu.roll(beta, reach, 1)
            behind = times_vector(tree_ref.at[level], beta_late, rows_ref)
            beta = jnp.where(later, beta_late, pltpu.roll(behind, LANES - reach, 1))
        starts = rows_to_lanes(starts_ref[...])
        alpha = window_down(alpha, frame_shifts(starts, half))
        spans = span_rows(lps_ref[0], lps_ref[1])
        scores = [spans[e] + alpha[e : e + 1, :] + beta for e in range(S)]
        best = jnp.max(functools.reduce(jnp.maximum, scores), axis=0, keepdims=True)
        weights = [jnp.exp(score - best) for score in scores]
        for e in range(1, S):
            weights[e] = weights[e] + weights[e - 1]
        total = jnp.sum(weights[S - 1], axis=0, keepdims=True)
        negative = -1.0 / total
        grads[0] = weights[S - 1] * negative
        for m in range(S):
            crossing = jnp.sum(jnp.where(places > m, weights[m], 0.0), axis=0, keepdims=True)
            grads[1, m : m + 1, :] = crossing * negative
        enc_sum[...] = jnp.zeros_like(enc_sum)
        pred_sum[...] = jnp.zeros_like(pred_sum)
        weight_sum[...] = jnp.zeros_like(weight_sum)

    def wide(ref, *lead):
        return jnp.concatenate([ref[(*lead, pl.ds(step * GROUP + k, 1), slice(None))] for k in range(GROUP)], axis=1)

    names = wide(label_ref)
    grad_blank = wide(grads, 0)
    grad_emit = wide(grads, 1)
    spread = (grad_blank + grad_emit) * wide(lps_ref, 2)
    padded = exps_ref.shape[0]
    ids = row_ids((padded, WIDE))
    coeff = jnp.where(ids == names, grad_emit, 0.0)
    head = coeff[:8] + jnp.where(row_ids((8, WIDE)) == 0, grad_blank, 0.0)
    coeff = jnp.concatenate([head, coeff[8:]], axis=0)
    grad_logits = (coeff - exps_ref[...] * spread).astype(BF16)
    grad_hidden = jnp.dot(weights_ref[...], grad_logits, preferred_element_type=F32)
    hidden = hidden_ref[...]
    hidden_wide = hidden.astype(F32)
    grad_summed = grad_hidden * (1.0 - hidden_wide * hidden_wide)
    enc_sum[...] += functools.reduce(
        lambda a, b: a + b, [grad_summed[:, k * LANES : (k + 1) * LANES] for k in range(GROUP)]
    )
    starts = rows_to_lanes(starts_ref[...])
    base = starts + step * GROUP
    rows = jnp.concatenate([base + k for k in range(GROUP)], axis=1)
    wanted = rows + jnp.concatenate([per_lane(half, 0, label_rows)] * GROUP, axis=1)
    slot = row_ids((8 * PRED_SLOT, WIDE))
    match = (slot // PRED_SLOT * PRED_SHARE + slot % PRED_SLOT == wanted) & (slot % PRED_SLOT < PRED_SHARE)
    pred_sum[...] += lax.dot_general(
        match.astype(BF16), grad_summed.astype(BF16), NT_DIMS, preferred_element_type=F32
    )
    weight_sum[...] += lax.dot_general(hidden, grad_logits, NT_DIMS, preferred_element_type=F32)

    @pl.when(step == STEPS - 1)
    def _():
        turn = reorder(own_rows, width)
        enc_rows = jnp.transpose(enc_sum[...]).astype(BF16)
        grad_enc_ref[...] = jnp.dot(enc_rows, turn, preferred_element_type=F32).astype(BF16)
        pred_rows = jnp.dot(pred_sum[...].astype(BF16), turn, preferred_element_type=F32).astype(BF16)
        share = width // 8
        for p in range(8):
            send_ref[p, 0:share, :] = weight_sum[p * share : (p + 1) * share, :].astype(BF16)
            send_ref[p, share : share + PRED_SLOT, :] = pred_rows[p * PRED_SLOT : (p + 1) * PRED_SLOT, :]


def params():
    return pltpu.CompilerParams(dimension_semantics=("arbitrary",), vmem_limit_bytes=VMEM_BYTES)


def whole(shape):
    return pl.BlockSpec(shape, lambda i: (0,) * len(shape))


smem = pl.BlockSpec(memory_space=pltpu.SMEM)


def exchange(blocks, axes):
    return lax.all_to_all(blocks, axes, 0, 0, tiled=True)


def share_copies(block, axes):
    count = lax.axis_size(axes)
    return exchange(jnp.broadcast_to(block[None], (count, *block.shape)), axes)


def per_device(encoder, predictor, starts, frame_lengths, label_lengths, labels, w_out):
    utt_count, frame_count, width = encoder.shape
    own_rows, vocab = w_out.shape
    label_rows = predictor.shape[1]
    tm_index = lax.axis_index(TM)
    tm_count = lax.axis_size(TM)
    utt_size = lax.axis_size(UTT)
    piece = own_rows // tm_count
    padded = -(-vocab // LANES) * LANES
    fold = piece * padded // LANES
    share = width // tm_count
    rows = S * utt_count * frame_count
    shape = jax.ShapeDtypeStruct

    mine = lax.dynamic_slice_in_dim(w_out, tm_index * piece, piece, axis=0)
    mine = jnp.pad(mine, ((0, 0), (0, padded - vocab))).reshape(fold, LANES)
    held = share_copies(mine, UTT).reshape(share, padded)
    block = tm_index.reshape(1).astype(jnp.int32)

    hidden, label_ids = pl.pallas_call(
        functools.partial(hidden_kernel, own_rows),
        grid=(STEPS,),
        in_specs=[
            whole(starts.shape),
            whole(labels.shape),
            whole((utt_count * frame_count, width)),
            whole(predictor.shape),
        ],
        out_specs=[pl.BlockSpec((width, WIDE), lambda i: (0, i)), whole((S, LANES))],
        out_shape=[shape((width, rows), BF16), shape((S, LANES), jnp.int32)],
        scratch_shapes=[
            pltpu.VMEM((width, LANES), F32),
            pltpu.VMEM((width, 2 * PRED_PAD), BF16),
            pltpu.VMEM((2 * PRED_PAD, width), F32),
        ],
        compiler_params=params(),
        cost_estimate=pl.CostEstimate(
            flops=2 * 2 * PRED_PAD * width * rows, bytes_accessed=3 * 2**20, transcendentals=width * rows
        ),
    )(starts, labels, encoder.reshape(-1, width), predictor)

    held, hidden = lax.optimization_barrier((held, hidden))
    gathered = share_copies(held, TM).reshape(width, padded)
    levels = frame_count.bit_length() - 1
    exps, lps, tree, payload = pl.pallas_call(
        functools.partial(forward_kernel, vocab),
        grid=(STEPS,),
        in_specs=[
            whole(starts.shape),
            smem,
            smem,
            smem,
            whole((S, LANES)),
            whole((width, padded)),
            pl.BlockSpec((width, WIDE), lambda i: (0, i)),
        ],
        out_specs=[
            pl.BlockSpec((padded, WIDE), lambda i: (0, i)),
            whole((3, S, LANES)),
            whole((levels, S, S, LANES)),
            whole((8, LANES)),
        ],
        out_shape=[
            shape((padded, rows), F32),
            shape((3, S, LANES), F32),
            shape((levels, S, S, LANES), F32),
            shape((8, LANES), F32),
        ],
        scratch_shapes=[
            pltpu.VMEM((padded, width), BF16),
            pltpu.VMEM((S // 2, S, LANES), F32),
            pltpu.VMEM((S, S, LANES), F32),
        ],
        compiler_params=params(),
        cost_estimate=pl.CostEstimate(
            flops=2 * padded * width * rows, bytes_accessed=8 * 2**20, transcendentals=padded * rows
        ),
    )(starts, frame_lengths, label_lengths, block, label_ids, gathered, hidden)

    blocks = share_copies(payload, TM)

    losses, grad_encoder, send = pl.pallas_call(
        functools.partial(backward_kernel, own_rows, label_rows),
        grid=(STEPS,),
        in_specs=[
            whole(starts.shape),
            smem,
            smem,
            smem,
            whole((tm_count, 8, LANES)),
            whole((3, S, LANES)),
            whole((levels, S, S, LANES)),
            whole((S, LANES)),
            whole((width, padded)),
            pl.BlockSpec((width, WIDE), lambda i: (0, i)),
            pl.BlockSpec((padded, WIDE), lambda i: (0, i)),
        ],
        out_specs=[
            smem,
            whole((utt_count * frame_count, width)),
            whole((tm_count, share + PRED_SLOT, padded)),
        ],
        out_shape=[
            shape((utt_count,), F32),
            shape((utt_count * frame_count, width), BF16),
            shape((tm_count, share + PRED_SLOT, padded), BF16),
        ],
        scratch_shapes=[
            pltpu.VMEM((S, S, LANES), F32),
            pltpu.VMEM((2, LANES, LANES), F32),
            pltpu.VMEM((S, LANES), F32),
            pltpu.VMEM((2, S, LANES), F32),
            pltpu.VMEM((width, LANES), F32),
            pltpu.VMEM((8 * PRED_SLOT, width), F32),
            pltpu.VMEM((width, padded), F32),
        ],
        compiler_params=params(),
        cost_estimate=pl.CostEstimate(
            flops=6 * padded * width * rows, bytes_accessed=8 * 2**20, transcendentals=2**16
        ),
    )(starts, frame_lengths, label_lengths, block, blocks, lps, tree, label_ids, gathered, hidden, exps)

    block_sum = jnp.sum(exchange(send, TM).astype(F32), axis=0)
    pred_rows = block_sum[share : share + PRED_SHARE]
    weight_rows = exchange(block_sum[:share].reshape(utt_size, fold, LANES), UTT)
    own_weight = jnp.sum(weight_rows, axis=0).reshape(piece, padded)
    final = share_copies(jnp.concatenate([pred_rows, own_weight], axis=0).astype(BF16), TM).astype(F32)
    grad_predictor = final[:, :PRED_SHARE].reshape(-1, width)[: utt_count * label_rows]
    grad_predictor = grad_predictor.reshape(utt_count, label_rows, width)
    grad_w_out = final[:, PRED_SHARE:, :vocab].reshape(own_rows, vocab)
    return (losses, grad_encoder.reshape(encoder.shape), grad_predictor, grad_w_out)


def solution(mesh):
    return jax.shard_map(
        per_device,
        mesh=mesh,
        in_specs=(
            P(UTT, TM, None),
            P(UTT, None, None),
            P(UTT, TM),
            P(UTT),
            P(UTT),
            P(UTT, None),
            P(UTT, None),
        ),
        out_specs=(P(UTT), P(UTT, TM, None), P(UTT, None, None), P(UTT, None)),
        check_vma=False,
    )
```

```python
import functools

import jax
import jax.numpy as jnp
from jax import lax
from jax.experimental import pallas as pl
from jax.experimental.pallas import tpu as pltpu
from jax.sharding import PartitionSpec as P

S = 16
LANES = 128
GROUP = 4
STEPS = S // GROUP
WIDE = GROUP * LANES
PRED_PAD = 80
VMEM_BYTES = 40 * 2**20

masked_log = -1e30

F32 = jnp.float32
BF16 = jnp.bfloat16

PRED_SHARE = 17
PRED_SLOT = 32
TM = "tm"
UTT = "utt"

NT_DIMS = (((1,), (1,)), ((), ()))


def lane_ids(shape=(1, LANES)):
    return lax.broadcasted_iota(jnp.int32, shape, 1)


def row_ids(shape):
    return lax.broadcasted_iota(jnp.int32, shape, 0)


def per_lane(half, low, high):
    return jnp.where(lane_ids() < half, low, high)


def rows_to_lanes(pair):
    return jnp.concatenate([pair[0:1, :], pair[1:2, :]], axis=1)


def balanced(combine, terms):
    while len(terms) > 1:
        terms = [combine(a, b) for a, b in zip(terms[0::2], terms[1::2])]
    return terms[0]


def rowwise_logsumexp(terms):
    top = balanced(jnp.maximum, terms)
    total = balanced(jnp.add, [jnp.exp(t - top) for t in terms])
    return top + jnp.log(total)


def vector_times(vector, matrix):
    return rowwise_logsumexp([vector[i : i + 1, :] + matrix[i] for i in range(S)])


def times_vector(matrix, vector, rows_ref):
    for i in range(S):
        terms = matrix[i] + vector
        top = jnp.max(terms, axis=0, keepdims=True)
        total = jnp.sum(jnp.exp(terms - top), axis=0, keepdims=True)
        rows_ref[i : i + 1, :] = top + jnp.log(total)
    return rows_ref[...]


def window_down(vector, distance):
    places = row_ids((S, LANES))
    for bit in (1, 2, 4, 8):
        moved = jnp.where(places < S - bit, pltpu.roll(vector, S - bit, 0), masked_log)
        vector = jnp.where((distance & bit) != 0, moved, vector)
    return vector


def window_up(vector, distance):
    places = row_ids((S, LANES))
    for bit in (1, 2, 4, 8):
        moved = jnp.where(places >= bit, pltpu.roll(vector, bit, 0), masked_log)
        vector = jnp.where((distance & bit) != 0, moved, vector)
    return vector


def slot_row(slot, own_rows, width):
    if own_rows != 8:
        return slot
    share = width // 8
    return slot % share * own_rows + slot // share


def frame_shifts(starts, half):
    lanes = lane_ids()
    first = (lanes == 0) | (lanes == half)
    return jnp.where(first, 0, starts - pltpu.roll(starts, 1, 1))


def span_rows(blank, emit):
    places = row_ids((S, LANES))
    spans = jnp.zeros((S, LANES), F32)
    rows = [None] * S
    for e in reversed(range(S)):
        spans = jnp.where(places > e, spans + emit[e : e + 1, :], 0.0)
        rows[e] = jnp.where(places >= e, spans + blank, masked_log)
    return rows


def reorder(own_rows, width):
    source = slot_row(row_ids((width, width)), own_rows, width)
    return (lane_ids((width, width)) == source).astype(BF16)


def hidden_kernel(own_rows, starts_ref, labels_ref, enc_ref, pred_ref, hidden_ref, label_ref, enc_t, pred_t, stack):
    step = pl.program_id(0)
    half = starts_ref.shape[1]
    starts = rows_to_lanes(starts_ref[...])

    @pl.when(step == 0)
    def _():
        turn = reorder(own_rows, enc_ref.shape[1])
        enc_t[...] = lax.dot_general(turn, enc_ref[...], NT_DIMS, preferred_element_type=F32)
        stack[...] = jnp.zeros_like(stack)
        rows = pred_ref.shape[1]
        stack[0:rows, :] = pred_ref[0].astype(F32)
        stack[PRED_PAD : PRED_PAD + rows, :] = pred_ref[1].astype(F32)
        pred_t[...] = lax.dot_general(
            turn, stack[...].astype(BF16), NT_DIMS, preferred_element_type=F32
        ).astype(BF16)
        cap = labels_ref.shape[1]
        labels = labels_ref[...].astype(F32)
        table = [jnp.transpose(jnp.broadcast_to(labels[b : b + 1, :], (LANES, cap))) for b in range(2)]
        table = jnp.where(lane_ids((cap, LANES)) < half, table[0], table[1])
        places = row_ids((cap, LANES))
        for k in range(S):
            wanted = jnp.minimum(starts + k, cap - 1)
            label_ref[k : k + 1, :] = jnp.sum(
                jnp.where(places == wanted, table, 0.0), axis=0, keepdims=True
            ).astype(jnp.int32)

    base = starts + per_lane(half, 0, PRED_PAD) + step * GROUP
    wanted = jnp.concatenate([base + k for k in range(GROUP)], axis=1)
    match = (row_ids((2 * PRED_PAD, WIDE)) == wanted).astype(BF16)
    picked = jnp.dot(pred_t[...], match, preferred_element_type=F32)
    for k in range(GROUP):
        part = slice(k * LANES, (k + 1) * LANES)
        hidden_ref[:, part] = jnp.tanh(enc_t[...] + picked[:, part]).astype(BF16)


def forward_kernel(
    vocab,
    starts_ref,
    frames_ref,
    labels_len_ref,
    block_ref,
    label_ref,
    gathered_ref,
    hidden_ref,
    exps_ref,
    lps_ref,
    tree_ref,
    payload_ref,
    weights_t,
    root,
):
    weights_t[...] = jnp.transpose(gathered_ref[...])
    for step in range(STEPS):
        joiner_step(step, vocab, weights_t, label_ref, hidden_ref, exps_ref, lps_ref)
    lattice_products(starts_ref, frames_ref, labels_len_ref, block_ref, lps_ref, tree_ref, payload_ref, root)


def joiner_step(step, vocab, weights_t, label_ref, hidden_ref, exps_ref, lps_ref):
    here = slice(step * WIDE, (step + 1) * WIDE)
    logits = jnp.dot(weights_t[...], hidden_ref[:, here], preferred_element_type=F32)
    padded = logits.shape[0]
    edge = padded - 16
    tail = jnp.where(row_ids((16, WIDE)) < vocab - edge, logits[edge:], masked_log)
    logits = jnp.concatenate([logits[:edge], tail], axis=0)
    top = jnp.max(logits, axis=0, keepdims=True)
    exps = jnp.exp(logits - top)
    exps_ref[:, here] = exps
    total = jnp.sum(exps, axis=0, keepdims=True)
    norm = top + jnp.log(total)
    scale = 1.0 / total
    names = jnp.concatenate([label_ref[step * GROUP + k : step * GROUP + k + 1, :] for k in range(GROUP)], axis=1)
    emit = jnp.sum(jnp.where(row_ids((padded, WIDE)) == names, logits, 0.0), axis=0, keepdims=True) - norm
    blank = logits[0:1, :] - norm
    for k in range(GROUP):
        part = slice(k * LANES, (k + 1) * LANES)
        row = slice(step * GROUP + k, step * GROUP + k + 1)
        lps_ref[0, row, :] = blank[:, part]
        lps_ref[1, row, :] = emit[:, part]
        lps_ref[2, row, :] = scale[:, part]


def lattice_products(starts_ref, frames_ref, labels_len_ref, block_ref, lps_ref, tree_ref, payload_ref, root):
    half = starts_ref.shape[1]
    lanes = lane_ids()
    starts = rows_to_lanes(starts_ref[...])
    frame = block_ref[0] * half + lanes % half
    live = frame < per_lane(half, frames_ref[0], frames_ref[1])
    limit = per_lane(half, labels_len_ref[0], labels_len_ref[1])
    allowed = live & (row_ids((S, LANES)) + starts < limit)
    blank = jnp.where(live, lps_ref[0], 0.0)
    emit = jnp.where(allowed, lps_ref[1], masked_log)
    lps_ref[0] = blank
    lps_ref[1] = emit
    shift = frame_shifts(starts, half)
    rows = span_rows(blank, emit)
    for bit in (1, 2, 4, 8):
        moved = (shift & bit) != 0
        rows = [
            jnp.where(moved, rows[i - bit] if i >= bit else masked_log, rows[i]) for i in range(S)
        ]
    for i in range(S):
        tree_ref[0, i] = rows[i]
    levels = half.bit_length() - 1
    for level in range(levels):
        reach = 1 << level
        back = LANES - reach
        late = lanes % (2 * reach) == reach
        latter = [tree_ref[level, m] for m in range(S)]
        latter = [jnp.where(late, one, pltpu.roll(one, back, 1)) for one in latter]
        for i in range(S // 2):
            former = jnp.where(late, pltpu.roll(tree_ref[level, i + S // 2], reach, 1), tree_ref[level, i])
            row = rowwise_logsumexp([former[m : m + 1, :] + latter[m] for m in range(S)])
            moved = pltpu.roll(row, back, 1)
            if level + 1 < levels:
                tree_ref[level + 1, i] = row
                tree_ref[level + 1, i + S // 2] = moved
            else:
                root[i] = row
                root[i + S // 2] = moved
    flat = jnp.transpose(root[...].reshape(S * S, LANES))
    payload_ref[...] = jnp.zeros_like(payload_ref)
    for b in range(2):
        line = flat[b * half : b * half + 1, :]
        payload_ref[4 * b : 4 * b + 1, :] = line[:, :LANES]
        payload_ref[4 * b + 1 : 4 * b + 2, :] = line[:, LANES:]
        for end, at in ((2, half - 1), (3, 0)):
            edge_start = starts_ref[b : b + 1, at : at + 1].astype(F32)
            payload_ref[4 * b + end : 4 * b + end + 1, :] = jnp.broadcast_to(edge_start, (1, LANES))


def backward_kernel(
    own_rows,
    label_rows,
    starts_ref,
    frames_ref,
    labels_len_ref,
    block_ref,
    blocks_ref,
    lps_ref,
    tree_ref,
    label_ref,
    weights_ref,
    hidden_ref,
    exps_ref,
    losses_ref,
    grad_enc_ref,
    send_ref,
    chain,
    line_up,
    rows_ref,
    grads,
    enc_sum,
    pred_sum,
    weight_sum,
):
    half = starts_ref.shape[1]
    width = weights_ref.shape[0]
    count = blocks_ref.shape[0]
    lanes = lane_ids()

    places = row_ids((S, LANES))
    line_up[...] = jnp.zeros_like(line_up)
    ends = jnp.zeros((1, LANES), F32)
    begins = jnp.zeros((1, LANES), F32)
    for r in range(count):
        for b in range(2):
            at = 2 * r + b
            line_up[0, at : at + 1, :] = blocks_ref[r, 4 * b : 4 * b + 1, :]
            line_up[1, at : at + 1, :] = blocks_ref[r, 4 * b + 1 : 4 * b + 2, :]
            ends = jnp.where(lanes == at, blocks_ref[r, 4 * b + 2 : 4 * b + 3, :], ends)
            begins = jnp.where(lanes == at, blocks_ref[r, 4 * b + 3 : 4 * b + 4, :], begins)
    for h in range(2):
        chain[h * S // 2 : (h + 1) * S // 2] = jnp.transpose(line_up[h]).reshape(S // 2, S, LANES)
    odd = lanes % 2 == 1
    last_start = [blocks_ref[count - 1, 4 * b + 2 : 4 * b + 3, :].astype(jnp.int32) for b in range(2)]
    final_place = jnp.where(odd, labels_len_ref[1] - last_start[1], labels_len_ref[0] - last_start[0])
    gap = (begins - pltpu.roll(ends, 2, 1)).astype(jnp.int32)
    gap = jnp.where((lanes >= 2) & (lanes < 2 * count), gap, 0)
    forward = jnp.where(places == 0, 0.0, masked_log) + jnp.zeros((S, LANES), F32)
    closing = jnp.where(places == final_place, 0.0, masked_log)
    backward = closing
    owner = lanes // 2
    for turn in range(count - 1):
        ahead = window_down(pltpu.roll(vector_times(forward, chain), 2, 1), gap)
        forward = jnp.where(owner == turn + 1, ahead, forward)
        behind = pltpu.roll(window_up(times_vector(chain, backward, rows_ref), gap), LANES - 2, 1)
        backward = jnp.where(owner == count - 2 - turn, behind, backward)
    leaving = vector_times(forward, chain) + closing
    best = jnp.max(leaving, axis=0, keepdims=True)
    log_total = best + jnp.log(jnp.sum(jnp.exp(leaving - best), axis=0, keepdims=True))
    for b in range(2):
        own_total = jnp.sum(jnp.where(lanes == 2 * (count - 1) + b, log_total, 0.0))
        losses_ref[b] = -own_total / frames_ref[b].astype(F32)

    def own_boundary(vectors):
        columns = [
            jnp.sum(jnp.where(lanes == 2 * block_ref[0] + b, vectors, 0.0), axis=1, keepdims=True)
            for b in range(2)
        ]
        spread = jnp.where(lanes < half, columns[0], columns[1])
        return spread - jnp.max(spread, axis=0, keepdims=True)

    alpha = own_boundary(forward)
    beta = own_boundary(backward)
    levels = half.bit_length() - 1
    for level in reversed(range(levels)):
        reach = 1 << level
        later = lanes % (2 * reach) == reach
        ahead = pltpu.roll(vector_times(alpha, tree_ref.at[level]), reach, 1)
        alpha = jnp.where(later, ahead, alpha)
        beta_late = pltpu.roll(beta, reach, 1)
        behind = times_vector(tree_ref.at[level], beta_late, rows_ref)
        beta = jnp.where(later, beta_late, pltpu.roll(behind, LANES - reach, 1))
    starts = rows_to_lanes(starts_ref[...])
    alpha = window_down(alpha, frame_shifts(starts, half))
    spans = span_rows(lps_ref[0], lps_ref[1])
    scores = [spans[e] + alpha[e : e + 1, :] + beta for e in range(S)]
    best = jnp.max(functools.reduce(jnp.maximum, scores), axis=0, keepdims=True)
    weights = [jnp.exp(score - best) for score in scores]
    for e in range(1, S):
        weights[e] = weights[e] + weights[e - 1]
    total = jnp.sum(weights[S - 1], axis=0, keepdims=True)
    negative = -1.0 / total
    grads[0] = weights[S - 1] * negative
    for m in range(S):
        crossing = jnp.sum(jnp.where(places > m, weights[m], 0.0), axis=0, keepdims=True)
        grads[1, m : m + 1, :] = crossing * negative
    for step in range(STEPS):
        gradient_step(
            step, label_rows, starts_ref, lps_ref, label_ref, weights_ref, hidden_ref, exps_ref, grads,
            enc_sum, pred_sum, weight_sum,
        )
    turn = reorder(own_rows, width)
    enc_rows = jnp.transpose(enc_sum[...]).astype(BF16)
    grad_enc_ref[...] = jnp.dot(enc_rows, turn, preferred_element_type=F32).astype(BF16)
    pred_rows = jnp.dot(pred_sum[...].astype(BF16), turn, preferred_element_type=F32).astype(BF16)
    share = width // 8
    for p in range(8):
        send_ref[p, 0:share, :] = weight_sum[p * share : (p + 1) * share, :].astype(BF16)
        send_ref[p, share : share + PRED_SLOT, :] = pred_rows[p * PRED_SLOT : (p + 1) * PRED_SLOT, :]


def gradient_step(
    step, label_rows, starts_ref, lps_ref, label_ref, weights_ref, hidden_ref, exps_ref, grads,
    enc_sum, pred_sum, weight_sum,
):
    half = starts_ref.shape[1]
    here = slice(step * WIDE, (step + 1) * WIDE)

    def wide(ref, *lead):
        return jnp.concatenate(
            [ref[(*lead, slice(step * GROUP + k, step * GROUP + k + 1))] for k in range(GROUP)], axis=1
        )

    names = wide(label_ref)
    grad_blank = wide(grads, 0)
    grad_emit = wide(grads, 1)
    spread = (grad_blank + grad_emit) * wide(lps_ref, 2)
    padded = exps_ref.shape[0]
    ids = row_ids((padded, WIDE))
    coeff = jnp.where(ids == names, grad_emit, 0.0)
    head = coeff[:8] + jnp.where(row_ids((8, WIDE)) == 0, grad_blank, 0.0)
    coeff = jnp.concatenate([head, coeff[8:]], axis=0)
    grad_logits = (coeff - exps_ref[:, here] * spread).astype(BF16)
    grad_hidden = jnp.dot(weights_ref[...], grad_logits, preferred_element_type=F32)
    hidden = hidden_ref[:, here]
    hidden_wide = hidden.astype(F32)
    grad_summed = grad_hidden * (1.0 - hidden_wide * hidden_wide)
    enc_term = balanced(jnp.add, [grad_summed[:, k * LANES : (k + 1) * LANES] for k in range(GROUP)])
    enc_sum[...] = enc_term if step == 0 else enc_sum[...] + enc_term
    starts = rows_to_lanes(starts_ref[...])
    base = starts + step * GROUP
    rows = jnp.concatenate([base + k for k in range(GROUP)], axis=1)
    wanted = rows + jnp.concatenate([per_lane(half, 0, label_rows)] * GROUP, axis=1)
    slot = row_ids((8 * PRED_SLOT, WIDE))
    match = (slot // PRED_SLOT * PRED_SHARE + slot % PRED_SLOT == wanted) & (slot % PRED_SLOT < PRED_SHARE)
    pred_term = lax.dot_general(
        match.astype(BF16), grad_summed.astype(BF16), NT_DIMS, preferred_element_type=F32
    )
    pred_sum[...] = pred_term if step == 0 else pred_sum[...] + pred_term
    weight_term = lax.dot_general(hidden, grad_logits, NT_DIMS, preferred_element_type=F32)
    weight_sum[...] = weight_term if step == 0 else weight_sum[...] + weight_term


def params():
    return pltpu.CompilerParams(dimension_semantics=("arbitrary",), vmem_limit_bytes=VMEM_BYTES)


def whole(shape):
    return pl.BlockSpec(shape, lambda i: (0,) * len(shape))


smem = pl.BlockSpec(memory_space=pltpu.SMEM)
vmem = pl.BlockSpec(memory_space=pltpu.VMEM)


def exchange(blocks, axes):
    return lax.all_to_all(blocks, axes, 0, 0, tiled=True)


def share_copies(block, axes):
    count = lax.axis_size(axes)
    return exchange(jnp.broadcast_to(block[None], (count, *block.shape)), axes)


def per_device(encoder, predictor, starts, frame_lengths, label_lengths, labels, w_out):
    utt_count, frame_count, width = encoder.shape
    own_rows, vocab = w_out.shape
    label_rows = predictor.shape[1]
    tm_index = lax.axis_index(TM)
    tm_count = lax.axis_size(TM)
    utt_size = lax.axis_size(UTT)
    piece = own_rows // tm_count
    padded = -(-vocab // LANES) * LANES
    fold = piece * padded // LANES
    share = width // tm_count
    rows = S * utt_count * frame_count
    shape = jax.ShapeDtypeStruct

    mine = lax.dynamic_slice_in_dim(w_out, tm_index * piece, piece, axis=0)
    mine = jnp.pad(mine, ((0, 0), (0, padded - vocab))).reshape(fold, LANES)
    held = share_copies(mine, UTT).reshape(share, padded)
    block = tm_index.reshape(1).astype(jnp.int32)

    hidden, label_ids = pl.pallas_call(
        functools.partial(hidden_kernel, own_rows),
        grid=(STEPS,),
        in_specs=[
            whole(starts.shape),
            whole(labels.shape),
            whole((utt_count * frame_count, width)),
            whole(predictor.shape),
        ],
        out_specs=[pl.BlockSpec((width, WIDE), lambda i: (0, i)), whole((S, LANES))],
        out_shape=[shape((width, rows), BF16), shape((S, LANES), jnp.int32)],
        scratch_shapes=[
            pltpu.VMEM((width, LANES), F32),
            pltpu.VMEM((width, 2 * PRED_PAD), BF16),
            pltpu.VMEM((2 * PRED_PAD, width), F32),
        ],
        compiler_params=params(),
        cost_estimate=pl.CostEstimate(
            flops=2 * 2 * PRED_PAD * width * rows, bytes_accessed=3 * 2**20, transcendentals=width * rows
        ),
    )(starts, labels, encoder.reshape(-1, width), predictor)

    held, hidden = lax.optimization_barrier((held, hidden))
    gathered = share_copies(held, TM).reshape(width, padded)
    levels = frame_count.bit_length() - 1
    exps, lps, tree, payload = pl.pallas_call(
        functools.partial(forward_kernel, vocab),
        in_specs=[vmem, smem, smem, smem] + [vmem] * 3,
        out_specs=[vmem] * 4,
        out_shape=[
            shape((padded, rows), F32),
            shape((3, S, LANES), F32),
            shape((levels, S, S, LANES), F32),
            shape((8, LANES), F32),
        ],
        scratch_shapes=[
            pltpu.VMEM((padded, width), BF16),
            pltpu.VMEM((S, S, LANES), F32),
        ],
        compiler_params=pltpu.CompilerParams(vmem_limit_bytes=VMEM_BYTES),
        cost_estimate=pl.CostEstimate(
            flops=2 * padded * width * rows, bytes_accessed=8 * 2**20, transcendentals=padded * rows
        ),
    )(starts, frame_lengths, label_lengths, block, label_ids, gathered, hidden)

    blocks = share_copies(payload, TM)

    losses, grad_encoder, send = pl.pallas_call(
        functools.partial(backward_kernel, own_rows, label_rows),
        in_specs=[vmem, smem, smem, smem] + [vmem] * 7,
        out_specs=[smem, vmem, vmem],
        out_shape=[
            shape((utt_count,), F32),
            shape((utt_count * frame_count, width), BF16),
            shape((tm_count, share + PRED_SLOT, padded), BF16),
        ],
        scratch_shapes=[
            pltpu.VMEM((S, S, LANES), F32),
            pltpu.VMEM((2, LANES, LANES), F32),
            pltpu.VMEM((S, LANES), F32),
            pltpu.VMEM((2, S, LANES), F32),
            pltpu.VMEM((width, LANES), F32),
            pltpu.VMEM((8 * PRED_SLOT, width), F32),
            pltpu.VMEM((width, padded), F32),
        ],
        compiler_params=pltpu.CompilerParams(vmem_limit_bytes=VMEM_BYTES),
        cost_estimate=pl.CostEstimate(
            flops=6 * padded * width * rows, bytes_accessed=8 * 2**20, transcendentals=2**16
        ),
    )(starts, frame_lengths, label_lengths, block, blocks, lps, tree, label_ids, gathered, hidden, exps)

    block_sum = jnp.sum(exchange(send, TM).astype(F32), axis=0)
    pred_rows = block_sum[share : share + PRED_SHARE]
    weight_rows = exchange(block_sum[:share].reshape(utt_size, fold, LANES), UTT)
    own_weight = jnp.sum(weight_rows, axis=0).reshape(piece, padded)
    final = share_copies(jnp.concatenate([pred_rows, own_weight], axis=0).astype(BF16), TM).astype(F32)
    grad_predictor = final[:, :PRED_SHARE].reshape(-1, width)[: utt_count * label_rows]
    grad_predictor = grad_predictor.reshape(utt_count, label_rows, width)
    grad_w_out = final[:, PRED_SHARE:, :vocab].reshape(own_rows, vocab)
    return (losses, grad_encoder.reshape(encoder.shape), grad_predictor, grad_w_out)


def solution(mesh):
    return jax.shard_map(
        per_device,
        mesh=mesh,
        in_specs=(
            P(UTT, TM, None),
            P(UTT, None, None),
            P(UTT, TM),
            P(UTT),
            P(UTT),
            P(UTT, None),
            P(UTT, None),
        ),
        out_specs=(P(UTT), P(UTT, TM, None), P(UTT, None, None), P(UTT, None)),
        check_vma=False,
    )
```

```python
import functools

import jax
import jax.numpy as jnp
from jax import lax
from jax.experimental import pallas as pl
from jax.experimental.pallas import tpu as pltpu
from jax.sharding import PartitionSpec as P

S = 16
LANES = 128
GROUP = 4
STEPS = S // GROUP
WIDE = GROUP * LANES
PRED_PAD = 80
VMEM_BYTES = 40 * 2**20

masked_log = -1e30

F32 = jnp.float32
BF16 = jnp.bfloat16

TM = "tm"
UTT = "utt"

NT_DIMS = (((1,), (1,)), ((), ()))


def lane_ids(shape=(1, LANES)):
    return lax.broadcasted_iota(jnp.int32, shape, 1)


def row_ids(shape):
    return lax.broadcasted_iota(jnp.int32, shape, 0)


def per_lane(half, low, high):
    return jnp.where(lane_ids() < half, low, high)


def rows_to_lanes(pair):
    return jnp.concatenate([pair[0:1, :], pair[1:2, :]], axis=1)


def balanced(combine, terms):
    while len(terms) > 1:
        terms = [combine(a, b) for a, b in zip(terms[0::2], terms[1::2])]
    return terms[0]


def rowwise_logsumexp(terms):
    top = balanced(jnp.maximum, terms)
    total = balanced(jnp.add, [jnp.exp(t - top) for t in terms])
    return top + jnp.log(total)


def vector_times(vector, matrix):
    return rowwise_logsumexp([vector[i : i + 1, :] + matrix[i] for i in range(S)])


def times_vector(matrix, vector, rows_ref):
    for i in range(S):
        terms = matrix[i] + vector
        top = jnp.max(terms, axis=0, keepdims=True)
        total = jnp.sum(jnp.exp(terms - top), axis=0, keepdims=True)
        rows_ref[i : i + 1, :] = top + jnp.log(total)
    return rows_ref[...]


def window_down(vector, distance):
    places = row_ids((S, LANES))
    for bit in (1, 2, 4, 8):
        moved = jnp.where(places < S - bit, pltpu.roll(vector, S - bit, 0), masked_log)
        vector = jnp.where((distance & bit) != 0, moved, vector)
    return vector


def window_up(vector, distance):
    places = row_ids((S, LANES))
    for bit in (1, 2, 4, 8):
        moved = jnp.where(places >= bit, pltpu.roll(vector, bit, 0), masked_log)
        vector = jnp.where((distance & bit) != 0, moved, vector)
    return vector


def slot_row(slot, core, own_rows, width):
    half, owned = width // 2, own_rows // 2
    inner = slot % half
    return inner // owned * own_rows + (slot // half + core) % 2 * owned + inner % owned


def frame_shifts(starts, half):
    lanes = lane_ids()
    first = (lanes == 0) | (lanes == half)
    return jnp.where(first, 0, starts - pltpu.roll(starts, 1, 1))


def span_rows(blank, emit):
    places = row_ids((S, LANES))
    spans = jnp.zeros((S, LANES), F32)
    rows = [None] * S
    for e in reversed(range(S)):
        spans = jnp.where(places > e, spans + emit[e : e + 1, :], 0.0)
        rows[e] = jnp.where(places >= e, spans + blank, masked_log)
    return rows


def reorder(core, own_rows, width):
    source = slot_row(row_ids((width, width)), core, own_rows, width)
    return (lane_ids((width, width)) == source).astype(BF16)


def hidden_kernel(
    own_rows, block_ref, starts_ref, labels_ref, enc_ref, pred_ref, hidden_ref, label_ref, enc_t, pred_t, stack
):
    step = pl.program_id(0)
    half = starts_ref.shape[1]
    starts = rows_to_lanes(starts_ref[...])

    @pl.when(step == 0)
    def _():
        turn = reorder(block_ref[0] % 2, own_rows, enc_ref.shape[1])
        enc_t[...] = lax.dot_general(turn, enc_ref[...], NT_DIMS, preferred_element_type=F32)
        stack[...] = jnp.zeros_like(stack)
        rows = pred_ref.shape[1]
        stack[0:rows, :] = pred_ref[0].astype(F32)
        stack[PRED_PAD : PRED_PAD + rows, :] = pred_ref[1].astype(F32)
        pred_t[...] = lax.dot_general(
            turn, stack[...].astype(BF16), NT_DIMS, preferred_element_type=F32
        ).astype(BF16)
        cap = labels_ref.shape[1]
        labels = labels_ref[...].astype(F32)
        table = [jnp.transpose(jnp.broadcast_to(labels[b : b + 1, :], (LANES, cap))) for b in range(2)]
        table = jnp.where(lane_ids((cap, LANES)) < half, table[0], table[1])
        places = row_ids((cap, LANES))
        for k in range(S):
            wanted = jnp.minimum(starts + k, cap - 1)
            label_ref[k : k + 1, :] = jnp.sum(
                jnp.where(places == wanted, table, 0.0), axis=0, keepdims=True
            ).astype(jnp.int32)

    base = starts + per_lane(half, 0, PRED_PAD) + step * GROUP
    wanted = jnp.concatenate([base + k for k in range(GROUP)], axis=1)
    match = (row_ids((2 * PRED_PAD, WIDE)) == wanted).astype(BF16)
    picked = jnp.dot(pred_t[...], match, preferred_element_type=F32)
    for k in range(GROUP):
        part = slice(k * LANES, (k + 1) * LANES)
        hidden_ref[:, part] = jnp.tanh(enc_t[...] + picked[:, part]).astype(BF16)


def forward_kernel(
    vocab,
    starts_ref,
    frames_ref,
    labels_len_ref,
    block_ref,
    label_ref,
    own_half_ref,
    far_half_ref,
    hidden_ref,
    exps_ref,
    lps_ref,
    tree_ref,
    payload_ref,
    weights_t,
    root,
):
    split = own_half_ref.shape[0]
    weights_t[:, :split] = jnp.transpose(own_half_ref[...])
    weights_t[:, split:] = jnp.transpose(far_half_ref[...])
    for step in range(STEPS):
        joiner_step(step, vocab, weights_t, label_ref, hidden_ref, exps_ref, lps_ref)
    lattice_products(starts_ref, frames_ref, labels_len_ref, block_ref, lps_ref, tree_ref, payload_ref, root)


def joiner_step(step, vocab, weights_t, label_ref, hidden_ref, exps_ref, lps_ref):
    here = slice(step * WIDE, (step + 1) * WIDE)
    logits = jnp.dot(weights_t[...], hidden_ref[:, here], preferred_element_type=F32)
    padded = logits.shape[0]
    edge = padded - 16
    tail = jnp.where(row_ids((16, WIDE)) < vocab - edge, logits[edge:], masked_log)
    logits = jnp.concatenate([logits[:edge], tail], axis=0)
    top = jnp.max(logits, axis=0, keepdims=True)
    exps = jnp.exp(logits - top)
    exps_ref[:, here] = exps
    total = jnp.sum(exps, axis=0, keepdims=True)
    norm = top + jnp.log(total)
    scale = 1.0 / total
    names = jnp.concatenate([label_ref[step * GROUP + k : step * GROUP + k + 1, :] for k in range(GROUP)], axis=1)
    emit = jnp.sum(jnp.where(row_ids((padded, WIDE)) == names, logits, 0.0), axis=0, keepdims=True) - norm
    blank = logits[0:1, :] - norm
    for k in range(GROUP):
        part = slice(k * LANES, (k + 1) * LANES)
        row = slice(step * GROUP + k, step * GROUP + k + 1)
        lps_ref[0, row, :] = blank[:, part]
        lps_ref[1, row, :] = emit[:, part]
        lps_ref[2, row, :] = scale[:, part]


def lattice_products(starts_ref, frames_ref, labels_len_ref, block_ref, lps_ref, tree_ref, payload_ref, root):
    half = starts_ref.shape[1]
    lanes = lane_ids()
    starts = rows_to_lanes(starts_ref[...])
    frame = block_ref[0] * half + lanes % half
    live = frame < per_lane(half, frames_ref[0], frames_ref[1])
    limit = per_lane(half, labels_len_ref[0], labels_len_ref[1])
    allowed = live & (row_ids((S, LANES)) + starts < limit)
    blank = jnp.where(live, lps_ref[0], 0.0)
    emit = jnp.where(allowed, lps_ref[1], masked_log)
    lps_ref[0] = blank
    lps_ref[1] = emit
    shift = frame_shifts(starts, half)
    rows = span_rows(blank, emit)
    for bit in (1, 2, 4, 8):
        moved = (shift & bit) != 0
        rows = [
            jnp.where(moved, rows[i - bit] if i >= bit else masked_log, rows[i]) for i in range(S)
        ]
    for i in range(S):
        tree_ref[0, i] = rows[i]
    levels = half.bit_length() - 1
    for level in range(levels):
        reach = 1 << level
        back = LANES - reach
        late = lanes % (2 * reach) == reach
        latter = [tree_ref[level, m] for m in range(S)]
        latter = [jnp.where(late, one, pltpu.roll(one, back, 1)) for one in latter]
        for i in range(S // 2):
            former = jnp.where(late, pltpu.roll(tree_ref[level, i + S // 2], reach, 1), tree_ref[level, i])
            row = rowwise_logsumexp([former[m : m + 1, :] + latter[m] for m in range(S)])
            moved = pltpu.roll(row, back, 1)
            if level + 1 < levels:
                tree_ref[level + 1, i] = row
                tree_ref[level + 1, i + S // 2] = moved
            else:
                root[i] = row
                root[i + S // 2] = moved
    flat = jnp.transpose(root[...].reshape(S * S, LANES))
    payload_ref[...] = jnp.zeros_like(payload_ref)
    for b in range(2):
        line = flat[b * half : b * half + 1, :]
        payload_ref[4 * b : 4 * b + 1, :] = line[:, :LANES]
        payload_ref[4 * b + 1 : 4 * b + 2, :] = line[:, LANES:]
        for end, at in ((2, half - 1), (3, 0)):
            edge_start = starts_ref[b : b + 1, at : at + 1].astype(F32)
            payload_ref[4 * b + end : 4 * b + end + 1, :] = jnp.broadcast_to(edge_start, (1, LANES))


def backward_kernel(
    own_rows,
    starts_ref,
    frames_ref,
    labels_len_ref,
    block_ref,
    blocks_ref,
    lps_ref,
    tree_ref,
    label_ref,
    own_half_ref,
    far_half_ref,
    hidden_ref,
    exps_ref,
    losses_ref,
    grad_enc_ref,
    weight_ref,
    pred_ref,
    send_ref,
    chain,
    line_up,
    rows_ref,
    grads,
    enc_sum,
    pred_sum,
    weight_sum,
):
    half = starts_ref.shape[1]
    width = hidden_ref.shape[0]
    core = block_ref[0] % 2
    count = blocks_ref.shape[0]
    lanes = lane_ids()

    places = row_ids((S, LANES))
    line_up[...] = jnp.zeros_like(line_up)
    ends = jnp.zeros((1, LANES), F32)
    begins = jnp.zeros((1, LANES), F32)
    for r in range(count):
        for b in range(2):
            at = 2 * r + b
            line_up[0, at : at + 1, :] = blocks_ref[r, 4 * b : 4 * b + 1, :]
            line_up[1, at : at + 1, :] = blocks_ref[r, 4 * b + 1 : 4 * b + 2, :]
            ends = jnp.where(lanes == at, blocks_ref[r, 4 * b + 2 : 4 * b + 3, :], ends)
            begins = jnp.where(lanes == at, blocks_ref[r, 4 * b + 3 : 4 * b + 4, :], begins)
    for h in range(2):
        chain[h * S // 2 : (h + 1) * S // 2] = jnp.transpose(line_up[h]).reshape(S // 2, S, LANES)
    odd = lanes % 2 == 1
    last_start = [blocks_ref[count - 1, 4 * b + 2 : 4 * b + 3, :].astype(jnp.int32) for b in range(2)]
    final_place = jnp.where(odd, labels_len_ref[1] - last_start[1], labels_len_ref[0] - last_start[0])
    gap = (begins - pltpu.roll(ends, 2, 1)).astype(jnp.int32)
    gap = jnp.where((lanes >= 2) & (lanes < 2 * count), gap, 0)
    forward = jnp.where(places == 0, 0.0, masked_log) + jnp.zeros((S, LANES), F32)
    closing = jnp.where(places == final_place, 0.0, masked_log)
    backward = closing
    owner = lanes // 2
    for turn in range(count - 1):
        ahead = window_down(pltpu.roll(vector_times(forward, chain), 2, 1), gap)
        forward = jnp.where(owner == turn + 1, ahead, forward)
        behind = pltpu.roll(window_up(times_vector(chain, backward, rows_ref), gap), LANES - 2, 1)
        backward = jnp.where(owner == count - 2 - turn, behind, backward)
    leaving = vector_times(forward, chain) + closing
    best = jnp.max(leaving, axis=0, keepdims=True)
    log_total = best + jnp.log(jnp.sum(jnp.exp(leaving - best), axis=0, keepdims=True))
    for b in range(2):
        own_total = jnp.sum(jnp.where(lanes == 2 * (count - 1) + b, log_total, 0.0))
        losses_ref[b] = -own_total / frames_ref[b].astype(F32)

    def own_boundary(vectors):
        columns = [
            jnp.sum(jnp.where(lanes == 2 * block_ref[0] + b, vectors, 0.0), axis=1, keepdims=True)
            for b in range(2)
        ]
        spread = jnp.where(lanes < half, columns[0], columns[1])
        return spread - jnp.max(spread, axis=0, keepdims=True)

    alpha = own_boundary(forward)
    beta = own_boundary(backward)
    levels = half.bit_length() - 1
    for level in reversed(range(levels)):
        reach = 1 << level
        later = lanes % (2 * reach) == reach
        ahead = pltpu.roll(vector_times(alpha, tree_ref.at[level]), reach, 1)
        alpha = jnp.where(later, ahead, alpha)
        beta_late = pltpu.roll(beta, reach, 1)
        behind = times_vector(tree_ref.at[level], beta_late, rows_ref)
        beta = jnp.where(later, beta_late, pltpu.roll(behind, LANES - reach, 1))
    starts = rows_to_lanes(starts_ref[...])
    alpha = window_down(alpha, frame_shifts(starts, half))
    spans = span_rows(lps_ref[0], lps_ref[1])
    scores = [spans[e] + alpha[e : e + 1, :] + beta for e in range(S)]
    best = jnp.max(functools.reduce(jnp.maximum, scores), axis=0, keepdims=True)
    weights = [jnp.exp(score - best) for score in scores]
    for e in range(1, S):
        weights[e] = weights[e] + weights[e - 1]
    total = jnp.sum(weights[S - 1], axis=0, keepdims=True)
    negative = -1.0 / total
    grads[0] = weights[S - 1] * negative
    for m in range(S):
        crossing = jnp.sum(jnp.where(places > m, weights[m], 0.0), axis=0, keepdims=True)
        grads[1, m : m + 1, :] = crossing * negative
    for step in range(STEPS):
        gradient_step(
            step, core, starts_ref, lps_ref, label_ref, own_half_ref, far_half_ref, hidden_ref, exps_ref, grads,
            enc_sum, pred_sum, weight_sum,
        )
    turn = reorder(core, own_rows, width)
    enc_rows = jnp.transpose(enc_sum[...]).astype(BF16)
    grad_enc_ref[...] = jnp.dot(enc_rows, turn, preferred_element_type=F32).astype(BF16)
    split = width // 2
    weight_ref[...] = weight_sum[:split, :]
    send_ref[:split, :] = weight_sum[split:, :].astype(BF16)
    upper = pred_sum[...].astype(BF16)
    lower = (pred_sum[:PRED_PAD, :] - upper[:PRED_PAD].astype(F32)).astype(BF16)
    turned = jnp.dot(upper, turn, preferred_element_type=F32)
    pred_ref[...] = turned[:PRED_PAD] + jnp.dot(lower, turn, preferred_element_type=F32)
    send_ref[split:, :] = turned[PRED_PAD:].astype(BF16)


def gradient_step(
    step, core, starts_ref, lps_ref, label_ref, own_half_ref, far_half_ref, hidden_ref, exps_ref, grads,
    enc_sum, pred_sum, weight_sum,
):
    half = starts_ref.shape[1]
    here = slice(step * WIDE, (step + 1) * WIDE)

    def wide(ref, *lead):
        return jnp.concatenate(
            [ref[(*lead, slice(step * GROUP + k, step * GROUP + k + 1))] for k in range(GROUP)], axis=1
        )

    names = wide(label_ref)
    grad_blank = wide(grads, 0)
    grad_emit = wide(grads, 1)
    spread = (grad_blank + grad_emit) * wide(lps_ref, 2)
    padded = exps_ref.shape[0]
    ids = row_ids((padded, WIDE))
    coeff = jnp.where(ids == names, grad_emit, 0.0)
    head = coeff[:8] + jnp.where(row_ids((8, WIDE)) == 0, grad_blank, 0.0)
    coeff = jnp.concatenate([head, coeff[8:]], axis=0)
    grad_logits = (coeff - exps_ref[:, here] * spread).astype(BF16)
    grad_hidden = jnp.concatenate(
        [jnp.dot(ref[...], grad_logits, preferred_element_type=F32) for ref in (own_half_ref, far_half_ref)], axis=0
    )
    hidden = hidden_ref[:, here]
    hidden_wide = hidden.astype(F32)
    grad_summed = grad_hidden * (1.0 - hidden_wide * hidden_wide)
    enc_term = balanced(jnp.add, [grad_summed[:, k * LANES : (k + 1) * LANES] for k in range(GROUP)])
    enc_sum[...] = enc_term if step == 0 else enc_sum[...] + enc_term
    starts = rows_to_lanes(starts_ref[...])
    base = starts + step * GROUP
    rows = jnp.concatenate([base + k for k in range(GROUP)], axis=1)
    second = jnp.concatenate([per_lane(half, 0, 1)] * GROUP, axis=1)
    slot = row_ids((2 * PRED_PAD, WIDE))
    match = (slot % PRED_PAD == rows) & ((slot // PRED_PAD + core) % 2 == second)
    pred_term = lax.dot_general(
        match.astype(BF16), grad_summed.astype(BF16), NT_DIMS, preferred_element_type=F32
    )
    pred_sum[...] = pred_term if step == 0 else pred_sum[...] + pred_term
    weight_term = lax.dot_general(hidden, grad_logits, NT_DIMS, preferred_element_type=F32)
    weight_sum[...] = weight_term if step == 0 else weight_sum[...] + weight_term


def params():
    return pltpu.CompilerParams(dimension_semantics=("arbitrary",), vmem_limit_bytes=VMEM_BYTES)


def whole(shape):
    return pl.BlockSpec(shape, lambda i: (0,) * len(shape))


smem = pl.BlockSpec(memory_space=pltpu.SMEM)
vmem = pl.BlockSpec(memory_space=pltpu.VMEM)


def exchange(blocks, axes):
    return lax.all_to_all(blocks, axes, 0, 0, tiled=True)


def share_copies(block, axes):
    count = lax.axis_size(axes)
    return exchange(jnp.broadcast_to(block[None], (count, *block.shape)), axes)


def tm_flip(block, turn):
    return lax.ppermute(block, TM, [(i ^ turn, i) for i in range(lax.axis_size(TM))])


def per_device(encoder, predictor, starts, frame_lengths, label_lengths, labels, w_out):
    utt_count, frame_count, width = encoder.shape
    own_rows, vocab = w_out.shape
    label_rows = predictor.shape[1]
    tm_index = lax.axis_index(TM)
    tm_count = lax.axis_size(TM)
    utt_size = lax.axis_size(UTT)
    core = tm_index & 1
    owned = own_rows // 2
    split = width // 2
    padded = -(-vocab // LANES) * LANES
    rows = S * utt_count * frame_count
    shape = jax.ShapeDtypeStruct

    mine = lax.dynamic_slice_in_dim(w_out, core * owned, owned, axis=0)
    mine = jnp.pad(mine, ((0, 0), (0, padded - vocab)))
    own_half = share_copies(mine, UTT).reshape(split, padded)
    block = tm_index.reshape(1).astype(jnp.int32)

    hidden, label_ids = pl.pallas_call(
        functools.partial(hidden_kernel, own_rows),
        grid=(STEPS,),
        in_specs=[
            smem,
            whole(starts.shape),
            whole(labels.shape),
            whole((utt_count * frame_count, width)),
            whole(predictor.shape),
        ],
        out_specs=[pl.BlockSpec((width, WIDE), lambda i: (0, i)), whole((S, LANES))],
        out_shape=[shape((width, rows), BF16), shape((S, LANES), jnp.int32)],
        scratch_shapes=[
            pltpu.VMEM((width, LANES), F32),
            pltpu.VMEM((width, 2 * PRED_PAD), BF16),
            pltpu.VMEM((2 * PRED_PAD, width), F32),
        ],
        compiler_params=params(),
        cost_estimate=pl.CostEstimate(
            flops=2 * 2 * PRED_PAD * width * rows, bytes_accessed=3 * 2**20, transcendentals=width * rows
        ),
    )(block, starts, labels, encoder.reshape(-1, width), predictor)

    own_half, hidden = lax.optimization_barrier((own_half, hidden))
    far_half = tm_flip(own_half, 1)
    levels = frame_count.bit_length() - 1
    exps, lps, tree, payload = pl.pallas_call(
        functools.partial(forward_kernel, vocab),
        in_specs=[vmem, smem, smem, smem] + [vmem] * 4,
        out_specs=[vmem] * 4,
        out_shape=[
            shape((padded, rows), F32),
            shape((3, S, LANES), F32),
            shape((levels, S, S, LANES), F32),
            shape((8, LANES), F32),
        ],
        scratch_shapes=[
            pltpu.VMEM((padded, width), BF16),
            pltpu.VMEM((S, S, LANES), F32),
        ],
        compiler_params=pltpu.CompilerParams(vmem_limit_bytes=VMEM_BYTES),
        cost_estimate=pl.CostEstimate(
            flops=2 * padded * width * rows, bytes_accessed=8 * 2**20, transcendentals=padded * rows
        ),
    )(starts, frame_lengths, label_lengths, block, label_ids, own_half, far_half, hidden)

    blocks = share_copies(payload, TM)

    losses, grad_encoder, weight_own, pred_own, send = pl.pallas_call(
        functools.partial(backward_kernel, own_rows),
        in_specs=[vmem, smem, smem, smem] + [vmem] * 8,
        out_specs=[smem] + [vmem] * 4,
        out_shape=[
            shape((utt_count,), F32),
            shape((utt_count * frame_count, width), BF16),
            shape((split, padded), F32),
            shape((PRED_PAD, width), F32),
            shape((split + PRED_PAD, padded), BF16),
        ],
        scratch_shapes=[
            pltpu.VMEM((S, S, LANES), F32),
            pltpu.VMEM((2, LANES, LANES), F32),
            pltpu.VMEM((S, LANES), F32),
            pltpu.VMEM((2, S, LANES), F32),
            pltpu.VMEM((width, LANES), F32),
            pltpu.VMEM((2 * PRED_PAD, width), F32),
            pltpu.VMEM((width, padded), F32),
        ],
        compiler_params=pltpu.CompilerParams(vmem_limit_bytes=VMEM_BYTES),
        cost_estimate=pl.CostEstimate(
            flops=6 * padded * width * rows, bytes_accessed=8 * 2**20, transcendentals=2**16
        ),
    )(starts, frame_lengths, label_lengths, block, blocks, lps, tree, label_ids, own_half, far_half, hidden, exps)

    came = tm_flip(send, 1)
    weight_half = (weight_own + came[:split].astype(F32)).astype(BF16).reshape(utt_size, owned, padded)
    weight_rows = jnp.sum(exchange(weight_half, UTT).astype(F32), axis=0)
    pred_own = pred_own + came[split:].astype(F32)
    for turn in (2, 4):
        pred_own = pred_own + tm_flip(pred_own.astype(BF16), turn).astype(F32)
    pred_own = pred_own[:label_rows]
    pred_far = tm_flip(pred_own, 1)
    grad_predictor = jnp.stack([jnp.where(core == 1, pred_far, pred_own), jnp.where(core == 1, pred_own, pred_far)])
    final = share_copies(weight_rows, TM).reshape(tm_count // 2, own_rows, padded)
    grad_w_out = jnp.sum(final, axis=0)[:, :vocab]
    return (losses, grad_encoder.reshape(encoder.shape), grad_predictor, grad_w_out)


def solution(mesh):
    return jax.shard_map(
        per_device,
        mesh=mesh,
        in_specs=(
            P(UTT, TM, None),
            P(UTT, None, None),
            P(UTT, TM),
            P(UTT),
            P(UTT),
            P(UTT, None),
            P(UTT, None),
        ),
        out_specs=(P(UTT), P(UTT, TM, None), P(UTT, None, None), P(UTT, None)),
        check_vma=False,
    )
```

```python
import functools

import jax
import jax.numpy as jnp
from jax import lax
from jax.experimental import pallas as pl
from jax.experimental.pallas import tpu as pltpu
from jax.sharding import PartitionSpec as P

S = 16
LANES = 128
GROUP = 4
STEPS = S // GROUP
WIDE = GROUP * LANES
PRED_PAD = 80
VMEM_BYTES = 40 * 2**20

masked_log = -1e30

F32 = jnp.float32
BF16 = jnp.bfloat16

TM = "tm"
UTT = "utt"

NT_DIMS = (((1,), (1,)), ((), ()))


def lane_ids(shape=(1, LANES)):
    return lax.broadcasted_iota(jnp.int32, shape, 1)


def row_ids(shape):
    return lax.broadcasted_iota(jnp.int32, shape, 0)


def per_lane(half, low, high):
    return jnp.where(lane_ids() < half, low, high)


def rows_to_lanes(pair):
    return jnp.concatenate([pair[0:1, :], pair[1:2, :]], axis=1)


def balanced(combine, terms):
    while len(terms) > 1:
        terms = [combine(a, b) for a, b in zip(terms[0::2], terms[1::2])]
    return terms[0]


def rowwise_logsumexp(terms):
    top = balanced(jnp.maximum, terms)
    total = balanced(jnp.add, [jnp.exp(t - top) for t in terms])
    return top + jnp.log(total)


def vector_times(vector, matrix):
    return rowwise_logsumexp([vector[i : i + 1, :] + matrix[i] for i in range(S)])


def times_vector(matrix, vector, rows_ref):
    for i in range(S):
        terms = matrix[i] + vector
        top = jnp.max(terms, axis=0, keepdims=True)
        total = jnp.sum(jnp.exp(terms - top), axis=0, keepdims=True)
        rows_ref[i : i + 1, :] = top + jnp.log(total)
    return rows_ref[...]


def window_down(vector, distance):
    places = row_ids((S, LANES))
    for bit in (1, 2, 4, 8):
        moved = jnp.where(places < S - bit, pltpu.roll(vector, S - bit, 0), masked_log)
        vector = jnp.where((distance & bit) != 0, moved, vector)
    return vector


def window_up(vector, distance):
    places = row_ids((S, LANES))
    for bit in (1, 2, 4, 8):
        moved = jnp.where(places >= bit, pltpu.roll(vector, bit, 0), masked_log)
        vector = jnp.where((distance & bit) != 0, moved, vector)
    return vector


def frame_shifts(starts, half):
    lanes = lane_ids()
    first = (lanes == 0) | (lanes == half)
    return jnp.where(first, 0, starts - pltpu.roll(starts, 1, 1))


def span_rows(blank, emit):
    places = row_ids((S, LANES))
    spans = jnp.zeros((S, LANES), F32)
    rows = [None] * S
    for e in reversed(range(S)):
        spans = jnp.where(places > e, spans + emit[e : e + 1, :], 0.0)
        rows[e] = jnp.where(places >= e, spans + blank, masked_log)
    return rows


def hidden_kernel(starts_ref, labels_ref, enc_ref, pred_ref, hidden_ref, label_ref, enc_t, pred_t, stack):
    step = pl.program_id(0)
    half = starts_ref.shape[1]
    starts = rows_to_lanes(starts_ref[...])

    @pl.when(step == 0)
    def _():
        enc_t[...] = jnp.transpose(enc_ref[...].astype(F32))
        stack[...] = jnp.zeros_like(stack)
        rows = pred_ref.shape[1]
        stack[0:rows, :] = pred_ref[0].astype(F32)
        stack[PRED_PAD : PRED_PAD + rows, :] = pred_ref[1].astype(F32)
        pred_t[...] = jnp.transpose(stack[...]).astype(BF16)
        cap = labels_ref.shape[1]
        labels = labels_ref[...].astype(F32)
        table = [jnp.transpose(jnp.broadcast_to(labels[b : b + 1, :], (LANES, cap))) for b in range(2)]
        table = jnp.where(lane_ids((cap, LANES)) < half, table[0], table[1])
        places = row_ids((cap, LANES))
        for k in range(S):
            wanted = jnp.minimum(starts + k, cap - 1)
            label_ref[k : k + 1, :] = jnp.sum(
                jnp.where(places == wanted, table, 0.0), axis=0, keepdims=True
            ).astype(jnp.int32)

    base = starts + per_lane(half, 0, PRED_PAD) + step * GROUP
    wanted = jnp.concatenate([base + k for k in range(GROUP)], axis=1)
    match = (row_ids((2 * PRED_PAD, WIDE)) == wanted).astype(BF16)
    picked = jnp.dot(pred_t[...], match, preferred_element_type=F32)
    for k in range(GROUP):
        part = slice(k * LANES, (k + 1) * LANES)
        hidden_ref[:, part] = jnp.tanh(enc_t[...] + picked[:, part]).astype(BF16)


def forward_kernel(
    vocab,
    starts_ref,
    meta_ref,
    label_ref,
    own_half_ref,
    far_half_ref,
    hidden_ref,
    exps_ref,
    lps_ref,
    tree_ref,
    payload_ref,
    weights_t,
    root,
):
    split = own_half_ref.shape[1]
    core = meta_ref[0] % 2
    weights_t[pl.ds(pl.multiple_of(core * split, split), split), :] = jnp.transpose(own_half_ref[...])
    weights_t[pl.ds(pl.multiple_of((1 - core) * split, split), split), :] = jnp.transpose(far_half_ref[...])
    for step in range(STEPS):
        joiner_step(step, vocab, weights_t, label_ref, hidden_ref, exps_ref, lps_ref)
    lattice_products(starts_ref, meta_ref, lps_ref, tree_ref, payload_ref, root)


def joiner_step(step, vocab, weights_t, label_ref, hidden_ref, exps_ref, lps_ref):
    here = slice(step * WIDE, (step + 1) * WIDE)
    logits = jnp.dot(weights_t[...], hidden_ref[:, here], preferred_element_type=F32)
    padded = logits.shape[0]
    edge = padded - 16
    tail = jnp.where(row_ids((16, WIDE)) < vocab - edge, logits[edge:], masked_log)
    logits = jnp.concatenate([logits[:edge], tail], axis=0)
    top = jnp.max(logits, axis=0, keepdims=True)
    exps = jnp.exp(logits - top)
    exps_ref[:, here] = exps
    total = jnp.sum(exps, axis=0, keepdims=True)
    norm = top + jnp.log(total)
    scale = 1.0 / total
    names = jnp.concatenate([label_ref[step * GROUP + k : step * GROUP + k + 1, :] for k in range(GROUP)], axis=1)
    emit = jnp.sum(jnp.where(row_ids((padded, WIDE)) == names, logits, 0.0), axis=0, keepdims=True) - norm
    blank = logits[0:1, :] - norm
    for k in range(GROUP):
        part = slice(k * LANES, (k + 1) * LANES)
        row = slice(step * GROUP + k, step * GROUP + k + 1)
        lps_ref[0, row, :] = blank[:, part]
        lps_ref[1, row, :] = emit[:, part]
        lps_ref[2, row, :] = scale[:, part]


def lattice_products(starts_ref, meta_ref, lps_ref, tree_ref, payload_ref, root):
    half = starts_ref.shape[1]
    lanes = lane_ids()
    starts = rows_to_lanes(starts_ref[...])
    frame = meta_ref[0] * half + lanes % half
    live = frame < per_lane(half, meta_ref[1], meta_ref[2])
    limit = per_lane(half, meta_ref[3], meta_ref[4])
    allowed = live & (row_ids((S, LANES)) + starts < limit)
    blank = jnp.where(live, lps_ref[0], 0.0)
    emit = jnp.where(allowed, lps_ref[1], masked_log)
    lps_ref[0] = blank
    lps_ref[1] = emit
    shift = frame_shifts(starts, half)
    rows = span_rows(blank, emit)
    for bit in (1, 2, 4, 8):
        moved = (shift & bit) != 0
        rows = [
            jnp.where(moved, rows[i - bit] if i >= bit else masked_log, rows[i]) for i in range(S)
        ]
    for i in range(S):
        tree_ref[0, i] = rows[i]
    levels = half.bit_length() - 1
    for level in range(levels):
        reach = 1 << level
        back = LANES - reach
        late = lanes % (2 * reach) == reach
        latter = [tree_ref[level, m] for m in range(S)]
        latter = [jnp.where(late, one, pltpu.roll(one, back, 1)) for one in latter]
        for i in range(S // 2):
            former = jnp.where(late, pltpu.roll(tree_ref[level, i + S // 2], reach, 1), tree_ref[level, i])
            row = rowwise_logsumexp([former[m : m + 1, :] + latter[m] for m in range(S)])
            moved = pltpu.roll(row, back, 1)
            if level + 1 < levels:
                tree_ref[level + 1, i] = row
                tree_ref[level + 1, i + S // 2] = moved
            else:
                root[i] = row
                root[i + S // 2] = moved
    flat = jnp.transpose(root[...].reshape(S * S, LANES))
    payload_ref[...] = jnp.zeros_like(payload_ref)
    for b in range(2):
        line = flat[b * half : b * half + 1, :]
        payload_ref[4 * b : 4 * b + 1, :] = line[:, :LANES]
        payload_ref[4 * b + 1 : 4 * b + 2, :] = line[:, LANES:]
        for end, at in ((2, half - 1), (3, 0)):
            edge_start = starts_ref[b : b + 1, at : at + 1].astype(F32)
            payload_ref[4 * b + end : 4 * b + end + 1, :] = jnp.broadcast_to(edge_start, (1, LANES))


def backward_kernel(
    starts_ref,
    meta_ref,
    blocks_ref,
    lps_ref,
    tree_ref,
    label_ref,
    own_half_ref,
    far_half_ref,
    hidden_ref,
    exps_ref,
    losses_ref,
    grad_enc_ref,
    weight_ref,
    pred_ref,
    send_ref,
    chain,
    line_up,
    rows_ref,
    grads,
    enc_sum,
    pred_sum,
    weight_sum,
    joined,
):
    half = starts_ref.shape[1]
    width = hidden_ref.shape[0]
    core = meta_ref[0] % 2
    count = blocks_ref.shape[0]
    lanes = lane_ids()

    places = row_ids((S, LANES))
    line_up[...] = jnp.zeros_like(line_up)
    ends = jnp.zeros((1, LANES), F32)
    begins = jnp.zeros((1, LANES), F32)
    for r in range(count):
        for b in range(2):
            at = 2 * r + b
            line_up[0, at : at + 1, :] = blocks_ref[r, 4 * b : 4 * b + 1, :]
            line_up[1, at : at + 1, :] = blocks_ref[r, 4 * b + 1 : 4 * b + 2, :]
            ends = jnp.where(lanes == at, blocks_ref[r, 4 * b + 2 : 4 * b + 3, :], ends)
            begins = jnp.where(lanes == at, blocks_ref[r, 4 * b + 3 : 4 * b + 4, :], begins)
    for h in range(2):
        chain[h * S // 2 : (h + 1) * S // 2] = jnp.transpose(line_up[h]).reshape(S // 2, S, LANES)
    odd = lanes % 2 == 1
    last_start = [blocks_ref[count - 1, 4 * b + 2 : 4 * b + 3, :].astype(jnp.int32) for b in range(2)]
    final_place = jnp.where(odd, meta_ref[4] - last_start[1], meta_ref[3] - last_start[0])
    gap = (begins - pltpu.roll(ends, 2, 1)).astype(jnp.int32)
    gap = jnp.where((lanes >= 2) & (lanes < 2 * count), gap, 0)
    forward = jnp.where(places == 0, 0.0, masked_log) + jnp.zeros((S, LANES), F32)
    closing = jnp.where(places == final_place, 0.0, masked_log)
    backward = closing
    owner = lanes // 2
    for turn in range(count - 1):
        ahead = window_down(pltpu.roll(vector_times(forward, chain), 2, 1), gap)
        forward = jnp.where(owner == turn + 1, ahead, forward)
        behind = pltpu.roll(window_up(times_vector(chain, backward, rows_ref), gap), LANES - 2, 1)
        backward = jnp.where(owner == count - 2 - turn, behind, backward)
    leaving = vector_times(forward, chain) + closing
    best = jnp.max(leaving, axis=0, keepdims=True)
    log_total = best + jnp.log(jnp.sum(jnp.exp(leaving - best), axis=0, keepdims=True))
    for b in range(2):
        own_total = jnp.sum(jnp.where(lanes == 2 * (count - 1) + b, log_total, 0.0))
        losses_ref[b] = -own_total / meta_ref[1 + b].astype(F32)

    def own_boundary(vectors):
        columns = [
            jnp.sum(jnp.where(lanes == 2 * meta_ref[0] + b, vectors, 0.0), axis=1, keepdims=True)
            for b in range(2)
        ]
        spread = jnp.where(lanes < half, columns[0], columns[1])
        return spread - jnp.max(spread, axis=0, keepdims=True)

    alpha = own_boundary(forward)
    beta = own_boundary(backward)
    levels = half.bit_length() - 1
    for level in reversed(range(levels)):
        reach = 1 << level
        later = lanes % (2 * reach) == reach
        ahead = pltpu.roll(vector_times(alpha, tree_ref.at[level]), reach, 1)
        alpha = jnp.where(later, ahead, alpha)
        beta_late = pltpu.roll(beta, reach, 1)
        behind = times_vector(tree_ref.at[level], beta_late, rows_ref)
        beta = jnp.where(later, beta_late, pltpu.roll(behind, LANES - reach, 1))
    starts = rows_to_lanes(starts_ref[...])
    alpha = window_down(alpha, frame_shifts(starts, half))
    spans = span_rows(lps_ref[0], lps_ref[1])
    scores = [spans[e] + alpha[e : e + 1, :] + beta for e in range(S)]
    best = jnp.max(functools.reduce(jnp.maximum, scores), axis=0, keepdims=True)
    weights = [jnp.exp(score - best) for score in scores]
    for e in range(1, S):
        weights[e] = weights[e] + weights[e - 1]
    total = jnp.sum(weights[S - 1], axis=0, keepdims=True)
    negative = -1.0 / total
    grads[0] = weights[S - 1] * negative
    for m in range(S):
        crossing = jnp.sum(jnp.where(places > m, weights[m], 0.0), axis=0, keepdims=True)
        grads[1, m : m + 1, :] = crossing * negative
    split = own_half_ref.shape[1]
    own_columns = pl.ds(pl.multiple_of(core * split, split), split)
    far_columns = pl.ds(pl.multiple_of((1 - core) * split, split), split)
    joined[:, own_columns] = own_half_ref[...]
    joined[:, far_columns] = far_half_ref[...]
    for step in range(STEPS):
        gradient_step(
            step, core, starts_ref, lps_ref, label_ref, joined, hidden_ref, exps_ref, grads,
            enc_sum, pred_sum, weight_sum,
        )
    grad_enc_ref[...] = jnp.transpose(enc_sum[...]).astype(BF16)
    weight_ref[...] = weight_sum[:, own_columns]
    send_ref[:width, :] = weight_sum[:, far_columns].astype(BF16)
    for i in range(2):
        rows, columns = slice(i * PRED_PAD, (i + 1) * PRED_PAD), slice(i * split, (i + 1) * split)
        pred_ref[rows, :] = pred_sum[:PRED_PAD, columns]
        send_ref[width + i * PRED_PAD : width + (i + 1) * PRED_PAD, :] = pred_sum[PRED_PAD:, columns].astype(BF16)


def gradient_step(
    step, core, starts_ref, lps_ref, label_ref, joined, hidden_ref, exps_ref, grads,
    enc_sum, pred_sum, weight_sum,
):
    half = starts_ref.shape[1]
    here = slice(step * WIDE, (step + 1) * WIDE)

    def wide(ref, *lead):
        return jnp.concatenate(
            [ref[(*lead, slice(step * GROUP + k, step * GROUP + k + 1))] for k in range(GROUP)], axis=1
        )

    names = wide(label_ref)
    grad_blank = wide(grads, 0)
    grad_emit = wide(grads, 1)
    spread = (grad_blank + grad_emit) * wide(lps_ref, 2)
    padded = exps_ref.shape[0]
    ids = row_ids((padded, WIDE))
    coeff = jnp.where(ids == names, grad_emit, 0.0)
    head = coeff[:8] + jnp.where(row_ids((8, WIDE)) == 0, grad_blank, 0.0)
    coeff = jnp.concatenate([head, coeff[8:]], axis=0)
    grad_logits = (coeff - exps_ref[:, here] * spread).astype(BF16)
    grad_hidden = jnp.dot(joined[...], grad_logits, preferred_element_type=F32)
    hidden = hidden_ref[:, here]
    hidden_wide = hidden.astype(F32)
    grad_summed = grad_hidden * (1.0 - hidden_wide * hidden_wide)
    enc_term = balanced(jnp.add, [grad_summed[:, k * LANES : (k + 1) * LANES] for k in range(GROUP)])
    enc_sum[...] = enc_term if step == 0 else enc_sum[...] + enc_term
    starts = rows_to_lanes(starts_ref[...])
    base = starts + step * GROUP
    rows = jnp.concatenate([base + k for k in range(GROUP)], axis=1)
    second = jnp.concatenate([per_lane(half, 0, 1)] * GROUP, axis=1)
    slot = row_ids((2 * PRED_PAD, WIDE))
    match = (slot % PRED_PAD == rows) & ((slot // PRED_PAD + core) % 2 == second)
    pred_term = lax.dot_general(
        match.astype(BF16), grad_summed.astype(BF16), NT_DIMS, preferred_element_type=F32
    )
    pred_sum[...] = pred_term if step == 0 else pred_sum[...] + pred_term
    weight_term = lax.dot_general(hidden, grad_logits, NT_DIMS, preferred_element_type=F32)
    weight_sum[...] = weight_term if step == 0 else weight_sum[...] + weight_term


def params():
    return pltpu.CompilerParams(dimension_semantics=("arbitrary",), vmem_limit_bytes=VMEM_BYTES)


def whole(shape):
    return pl.BlockSpec(shape, lambda i: (0,) * len(shape))


smem = pl.BlockSpec(memory_space=pltpu.SMEM)
vmem = pl.BlockSpec(memory_space=pltpu.VMEM)


def exchange(blocks, axes):
    return lax.all_to_all(blocks, axes, 0, 0, tiled=True)


def share_copies(block, axes):
    count = lax.axis_size(axes)
    return exchange(jnp.broadcast_to(block[None], (count, *block.shape)), axes)


def tm_flip(block, turn):
    return lax.ppermute(block, TM, [(i ^ turn, i) for i in range(lax.axis_size(TM))])


def per_device(encoder, predictor, starts, frame_lengths, label_lengths, labels, w_out):
    utt_count, frame_count, width = encoder.shape
    own_rows, vocab = w_out.shape
    label_rows = predictor.shape[1]
    tm_index = lax.axis_index(TM)
    tm_count = lax.axis_size(TM)
    utt_size = lax.axis_size(UTT)
    core = tm_index & 1
    padded = -(-vocab // 256) * 256
    split = padded // 2
    rows = S * utt_count * frame_count
    shape = jax.ShapeDtypeStruct

    mine = lax.dynamic_slice_in_dim(jnp.pad(w_out, ((0, 0), (0, padded - vocab))), core * split, split, axis=1)
    own_half = share_copies(mine, UTT).reshape(width, split)
    meta = jnp.concatenate([tm_index.reshape(1).astype(jnp.int32), frame_lengths, label_lengths])

    hidden, label_ids = pl.pallas_call(
        hidden_kernel,
        grid=(STEPS,),
        in_specs=[
            whole(starts.shape),
            whole(labels.shape),
            whole((utt_count * frame_count, width)),
            whole(predictor.shape),
        ],
        out_specs=[pl.BlockSpec((width, WIDE), lambda i: (0, i)), whole((S, LANES))],
        out_shape=[shape((width, rows), BF16), shape((S, LANES), jnp.int32)],
        scratch_shapes=[
            pltpu.VMEM((width, LANES), F32),
            pltpu.VMEM((width, 2 * PRED_PAD), BF16),
            pltpu.VMEM((2 * PRED_PAD, width), F32),
        ],
        compiler_params=params(),
        cost_estimate=pl.CostEstimate(
            flops=2 * 2 * PRED_PAD * width * rows, bytes_accessed=3 * 2**20, transcendentals=width * rows
        ),
    )(starts, labels, encoder.reshape(-1, width), predictor)

    own_half, hidden = lax.optimization_barrier((own_half, hidden))
    far_half = tm_flip(own_half, 1)
    levels = frame_count.bit_length() - 1
    exps, lps, tree, payload = pl.pallas_call(
        functools.partial(forward_kernel, vocab),
        in_specs=[vmem, smem] + [vmem] * 4,
        out_specs=[vmem] * 4,
        out_shape=[
            shape((padded, rows), F32),
            shape((3, S, LANES), F32),
            shape((levels, S, S, LANES), F32),
            shape((8, LANES), F32),
        ],
        scratch_shapes=[
            pltpu.VMEM((padded, width), BF16),
            pltpu.VMEM((S, S, LANES), F32),
        ],
        compiler_params=pltpu.CompilerParams(vmem_limit_bytes=VMEM_BYTES),
        cost_estimate=pl.CostEstimate(
            flops=2 * padded * width * rows, bytes_accessed=8 * 2**20, transcendentals=padded * rows
        ),
    )(starts, meta, label_ids, own_half, far_half, hidden)

    blocks = share_copies(payload, TM)

    losses, grad_encoder, weight_own, pred_own, send = pl.pallas_call(
        backward_kernel,
        in_specs=[vmem, smem] + [vmem] * 8,
        out_specs=[smem] + [vmem] * 4,
        out_shape=[
            shape((utt_count,), F32),
            shape((utt_count * frame_count, width), BF16),
            shape((width, split), F32),
            shape((2 * PRED_PAD, split), F32),
            shape((width + 2 * PRED_PAD, split), BF16),
        ],
        scratch_shapes=[
            pltpu.VMEM((S, S, LANES), F32),
            pltpu.VMEM((2, LANES, LANES), F32),
            pltpu.VMEM((S, LANES), F32),
            pltpu.VMEM((2, S, LANES), F32),
            pltpu.VMEM((width, LANES), F32),
            pltpu.VMEM((2 * PRED_PAD, width), F32),
            pltpu.VMEM((width, padded), F32),
            pltpu.VMEM((width, padded), BF16),
        ],
        compiler_params=pltpu.CompilerParams(vmem_limit_bytes=VMEM_BYTES),
        cost_estimate=pl.CostEstimate(
            flops=6 * padded * width * rows, bytes_accessed=8 * 2**20, transcendentals=2**16
        ),
    )(starts, meta, blocks, lps, tree, label_ids, own_half, far_half, hidden, exps)

    came = tm_flip(send, 1)
    weight_half = (weight_own + came[:width].astype(F32)).astype(BF16).reshape(utt_size, own_rows, split)
    weight_rows = jnp.sum(exchange(weight_half, UTT).astype(F32), axis=0)
    pred_own = pred_own + came[width:].astype(F32)
    for turn in (2, 4):
        pred_own = pred_own + tm_flip(pred_own.astype(BF16), turn).astype(F32)
    pred_far = tm_flip(pred_own, 1)
    pred_pair = jnp.stack([jnp.where(core == 1, pred_far, pred_own), jnp.where(core == 1, pred_own, pred_far)])
    pred_pair = pred_pair.reshape(utt_count, 2, PRED_PAD, split)[:, :, :label_rows]
    grad_predictor = jnp.concatenate([pred_pair[:, 0], pred_pair[:, 1]], axis=-1)
    final = share_copies(weight_rows, TM).reshape(tm_count // 2, 2, own_rows, split)
    final = jnp.sum(final, axis=0)
    grad_w_out = jnp.concatenate([final[0], final[1]], axis=-1)[:, :vocab]
    return (losses, grad_encoder.reshape(encoder.shape), grad_predictor, grad_w_out)


def solution(mesh):
    return jax.shard_map(
        per_device,
        mesh=mesh,
        in_specs=(
            P(UTT, TM, None),
            P(UTT, None, None),
            P(UTT, TM),
            P(UTT),
            P(UTT),
            P(UTT, None),
            P(UTT, None),
        ),
        out_specs=(P(UTT), P(UTT, TM, None), P(UTT, None, None), P(UTT, None)),
        check_vma=False,
    )
```

```python
import functools

import jax
import jax.numpy as jnp
from jax import lax
from jax.experimental import pallas as pl
from jax.experimental.pallas import tpu as pltpu
from jax.sharding import PartitionSpec as P

S = 16
LANES = 128
GROUP = 4
STEPS = S // GROUP
WIDE = GROUP * LANES
PRED_PAD = 80
VMEM_BYTES = 40 * 2**20

masked_log = -1e30

F32 = jnp.float32
BF16 = jnp.bfloat16

TM = "tm"
UTT = "utt"

NT_DIMS = (((1,), (1,)), ((), ()))


def lane_ids(shape=(1, LANES)):
    return lax.broadcasted_iota(jnp.int32, shape, 1)


def row_ids(shape):
    return lax.broadcasted_iota(jnp.int32, shape, 0)


def per_lane(half, low, high):
    return jnp.where(lane_ids() < half, low, high)


def rows_to_lanes(pair):
    return jnp.concatenate([pair[0:1, :], pair[1:2, :]], axis=1)


def balanced(combine, terms):
    while len(terms) > 1:
        terms = [combine(a, b) for a, b in zip(terms[0::2], terms[1::2])]
    return terms[0]


def rowwise_logsumexp(terms):
    top = balanced(jnp.maximum, terms)
    total = balanced(jnp.add, [jnp.exp(t - top) for t in terms])
    return top + jnp.log(total)


def vector_times(vector, matrix):
    return rowwise_logsumexp([vector[i : i + 1, :] + matrix[i] for i in range(S)])


def times_vector(matrix, vector, rows_ref):
    for i in range(S):
        terms = matrix[i] + vector
        top = jnp.max(terms, axis=0, keepdims=True)
        total = jnp.sum(jnp.exp(terms - top), axis=0, keepdims=True)
        rows_ref[i : i + 1, :] = top + jnp.log(total)
    return rows_ref[...]


def window_down(vector, distance):
    places = row_ids((S, LANES))
    for bit in (1, 2, 4, 8):
        moved = jnp.where(places < S - bit, pltpu.roll(vector, S - bit, 0), masked_log)
        vector = jnp.where((distance & bit) != 0, moved, vector)
    return vector


def window_up(vector, distance):
    places = row_ids((S, LANES))
    for bit in (1, 2, 4, 8):
        moved = jnp.where(places >= bit, pltpu.roll(vector, bit, 0), masked_log)
        vector = jnp.where((distance & bit) != 0, moved, vector)
    return vector


def frame_shifts(starts, half):
    lanes = lane_ids()
    first = (lanes == 0) | (lanes == half)
    return jnp.where(first, 0, starts - pltpu.roll(starts, 1, 1))


def span_rows(blank, emit):
    places = row_ids((S, LANES))
    spans = jnp.zeros((S, LANES), F32)
    rows = [None] * S
    for e in reversed(range(S)):
        spans = jnp.where(places > e, spans + emit[e : e + 1, :], 0.0)
        rows[e] = jnp.where(places >= e, spans + blank, masked_log)
    return rows


def hidden_kernel(meta_ref, starts_ref, labels_ref, enc_ref, pred_ref, hidden_ref, label_ref, enc_t, pred_t, stack):
    step = pl.program_id(0)
    half = starts_ref.shape[1]
    starts = rows_to_lanes(starts_ref[...])

    @pl.when(step == 0)
    def _():
        enc_t[...] = jnp.transpose(enc_ref[...].astype(F32))
        stack[...] = jnp.zeros_like(stack)
        rows = pred_ref.shape[1]
        stack[0:rows, :] = pred_ref[0].astype(F32)
        stack[PRED_PAD : PRED_PAD + rows, :] = pred_ref[1].astype(F32)
        pred_t[...] = jnp.transpose(stack[...]).astype(BF16)
        cap = labels_ref.shape[1]
        labels = labels_ref[...].astype(F32)
        table = [jnp.transpose(jnp.broadcast_to(labels[b : b + 1, :], (LANES, cap))) for b in range(2)]
        table = jnp.where(lane_ids((cap, LANES)) < half, table[0], table[1])
        places = row_ids((cap, LANES))
        for k in range(S):
            wanted = jnp.minimum(starts + k, cap - 1)
            label_ref[k : k + 1, :] = jnp.sum(
                jnp.where(places == wanted, table, 0.0), axis=0, keepdims=True
            ).astype(jnp.int32)

    base = starts + per_lane(half, 0, PRED_PAD) + step * GROUP
    wanted = jnp.concatenate([base + k for k in range(GROUP)], axis=1)
    match = (row_ids((2 * PRED_PAD, WIDE)) == wanted).astype(BF16)
    picked = jnp.dot(pred_t[...], match, preferred_element_type=F32)
    for k in range(GROUP):
        part = slice(k * LANES, (k + 1) * LANES)
        hidden_ref[:, part] = jnp.tanh(enc_t[...] + picked[:, part]).astype(BF16)


def forward_kernel(
    vocab,
    starts_ref,
    meta_ref,
    label_ref,
    own_half_ref,
    far_half_ref,
    hidden_ref,
    exps_ref,
    lps_ref,
    tree_ref,
    payload_ref,
    weights_t,
    root,
):
    split = own_half_ref.shape[1]
    core = meta_ref[0] % 2
    weights_t[pl.ds(pl.multiple_of(core * split, split), split), :] = jnp.transpose(own_half_ref[...])
    weights_t[pl.ds(pl.multiple_of((1 - core) * split, split), split), :] = jnp.transpose(far_half_ref[...])
    for step in range(STEPS):
        joiner_step(step, vocab, weights_t, label_ref, hidden_ref, exps_ref, lps_ref)
    lattice_products(starts_ref, meta_ref, lps_ref, tree_ref, payload_ref, root)


def joiner_step(step, vocab, weights_t, label_ref, hidden_ref, exps_ref, lps_ref):
    here = slice(step * WIDE, (step + 1) * WIDE)
    logits = jnp.dot(weights_t[...], hidden_ref[:, here], preferred_element_type=F32)
    padded = logits.shape[0]
    edge = padded - 16
    tail = jnp.where(row_ids((16, WIDE)) < vocab - edge, logits[edge:], masked_log)
    logits = jnp.concatenate([logits[:edge], tail], axis=0)
    top = jnp.max(logits, axis=0, keepdims=True)
    exps = jnp.exp(logits - top)
    exps_ref[:, here] = exps
    total = jnp.sum(exps, axis=0, keepdims=True)
    norm = top + jnp.log(total)
    scale = 1.0 / total
    names = jnp.concatenate([label_ref[step * GROUP + k : step * GROUP + k + 1, :] for k in range(GROUP)], axis=1)
    emit = jnp.sum(jnp.where(row_ids((padded, WIDE)) == names, logits, 0.0), axis=0, keepdims=True) - norm
    blank = logits[0:1, :] - norm
    for k in range(GROUP):
        part = slice(k * LANES, (k + 1) * LANES)
        row = slice(step * GROUP + k, step * GROUP + k + 1)
        lps_ref[0, row, :] = blank[:, part]
        lps_ref[1, row, :] = emit[:, part]
        lps_ref[2, row, :] = scale[:, part]


def lattice_products(starts_ref, meta_ref, lps_ref, tree_ref, payload_ref, root):
    half = starts_ref.shape[1]
    lanes = lane_ids()
    starts = rows_to_lanes(starts_ref[...])
    frame = meta_ref[0] * half + lanes % half
    live = frame < per_lane(half, meta_ref[1], meta_ref[2])
    limit = per_lane(half, meta_ref[3], meta_ref[4])
    allowed = live & (row_ids((S, LANES)) + starts < limit)
    blank = jnp.where(live, lps_ref[0], 0.0)
    emit = jnp.where(allowed, lps_ref[1], masked_log)
    lps_ref[0] = blank
    lps_ref[1] = emit
    shift = frame_shifts(starts, half)
    rows = span_rows(blank, emit)
    for bit in (1, 2, 4, 8):
        moved = (shift & bit) != 0
        rows = [
            jnp.where(moved, rows[i - bit] if i >= bit else masked_log, rows[i]) for i in range(S)
        ]
    for i in range(S):
        tree_ref[0, i] = rows[i]
    levels = half.bit_length() - 1
    for level in range(levels):
        reach = 1 << level
        back = LANES - reach
        late = lanes % (2 * reach) == reach
        latter = [tree_ref[level, m] for m in range(S)]
        latter = [jnp.where(late, one, pltpu.roll(one, back, 1)) for one in latter]
        for i in range(S // 2):
            former = jnp.where(late, pltpu.roll(tree_ref[level, i + S // 2], reach, 1), tree_ref[level, i])
            row = rowwise_logsumexp([former[m : m + 1, :] + latter[m] for m in range(S)])
            moved = pltpu.roll(row, back, 1)
            if level + 1 < levels:
                tree_ref[level + 1, i] = row
                tree_ref[level + 1, i + S // 2] = moved
            else:
                root[i] = row
                root[i + S // 2] = moved
    flat = jnp.transpose(root[...].reshape(S * S, LANES))
    payload_ref[...] = jnp.zeros_like(payload_ref)
    for b in range(2):
        line = flat[b * half : b * half + 1, :]
        payload_ref[4 * b : 4 * b + 1, :] = line[:, :LANES]
        payload_ref[4 * b + 1 : 4 * b + 2, :] = line[:, LANES:]
        for end, at in ((2, half - 1), (3, 0)):
            edge_start = starts_ref[b : b + 1, at : at + 1].astype(F32)
            payload_ref[4 * b + end : 4 * b + end + 1, :] = jnp.broadcast_to(edge_start, (1, LANES))


def backward_kernel(
    starts_ref,
    meta_ref,
    blocks_ref,
    lps_ref,
    tree_ref,
    label_ref,
    own_half_ref,
    far_half_ref,
    hidden_ref,
    exps_ref,
    losses_ref,
    grad_enc_ref,
    weight_ref,
    pred_ref,
    send_ref,
    chain,
    line_up,
    rows_ref,
    grads,
    enc_sum,
    pred_sum,
    weight_sum,
    joined,
):
    half = starts_ref.shape[1]
    width = hidden_ref.shape[0]
    core = meta_ref[0] % 2
    count = blocks_ref.shape[0]
    lanes = lane_ids()

    places = row_ids((S, LANES))
    line_up[...] = jnp.zeros_like(line_up)
    ends = jnp.zeros((1, LANES), F32)
    begins = jnp.zeros((1, LANES), F32)
    for r in range(count):
        for b in range(2):
            at = 2 * r + b
            line_up[0, at : at + 1, :] = blocks_ref[r, 4 * b : 4 * b + 1, :]
            line_up[1, at : at + 1, :] = blocks_ref[r, 4 * b + 1 : 4 * b + 2, :]
            ends = jnp.where(lanes == at, blocks_ref[r, 4 * b + 2 : 4 * b + 3, :], ends)
            begins = jnp.where(lanes == at, blocks_ref[r, 4 * b + 3 : 4 * b + 4, :], begins)
    for h in range(2):
        chain[h * S // 2 : (h + 1) * S // 2] = jnp.transpose(line_up[h]).reshape(S // 2, S, LANES)
    odd = lanes % 2 == 1
    last_start = [blocks_ref[count - 1, 4 * b + 2 : 4 * b + 3, :].astype(jnp.int32) for b in range(2)]
    final_place = jnp.where(odd, meta_ref[4] - last_start[1], meta_ref[3] - last_start[0])
    gap = (begins - pltpu.roll(ends, 2, 1)).astype(jnp.int32)
    gap = jnp.where((lanes >= 2) & (lanes < 2 * count), gap, 0)
    forward = jnp.where(places == 0, 0.0, masked_log) + jnp.zeros((S, LANES), F32)
    closing = jnp.where(places == final_place, 0.0, masked_log)
    backward = closing
    owner = lanes // 2
    for turn in range(count - 1):
        ahead = window_down(pltpu.roll(vector_times(forward, chain), 2, 1), gap)
        forward = jnp.where(owner == turn + 1, ahead, forward)
        behind = pltpu.roll(window_up(times_vector(chain, backward, rows_ref), gap), LANES - 2, 1)
        backward = jnp.where(owner == count - 2 - turn, behind, backward)
    leaving = vector_times(forward, chain) + closing
    best = jnp.max(leaving, axis=0, keepdims=True)
    log_total = best + jnp.log(jnp.sum(jnp.exp(leaving - best), axis=0, keepdims=True))
    for b in range(2):
        own_total = jnp.sum(jnp.where(lanes == 2 * (count - 1) + b, log_total, 0.0))
        losses_ref[b] = -own_total / meta_ref[1 + b].astype(F32)

    def own_boundary(vectors):
        columns = [
            jnp.sum(jnp.where(lanes == 2 * meta_ref[0] + b, vectors, 0.0), axis=1, keepdims=True)
            for b in range(2)
        ]
        spread = jnp.where(lanes < half, columns[0], columns[1])
        return spread - jnp.max(spread, axis=0, keepdims=True)

    alpha = own_boundary(forward)
    beta = own_boundary(backward)
    levels = half.bit_length() - 1
    for level in reversed(range(levels)):
        reach = 1 << level
        later = lanes % (2 * reach) == reach
        ahead = pltpu.roll(vector_times(alpha, tree_ref.at[level]), reach, 1)
        alpha = jnp.where(later, ahead, alpha)
        beta_late = pltpu.roll(beta, reach, 1)
        behind = times_vector(tree_ref.at[level], beta_late, rows_ref)
        beta = jnp.where(later, beta_late, pltpu.roll(behind, LANES - reach, 1))
    starts = rows_to_lanes(starts_ref[...])
    alpha = window_down(alpha, frame_shifts(starts, half))
    spans = span_rows(lps_ref[0], lps_ref[1])
    scores = [spans[e] + alpha[e : e + 1, :] + beta for e in range(S)]
    best = jnp.max(functools.reduce(jnp.maximum, scores), axis=0, keepdims=True)
    weights = [jnp.exp(score - best) for score in scores]
    for e in range(1, S):
        weights[e] = weights[e] + weights[e - 1]
    total = jnp.sum(weights[S - 1], axis=0, keepdims=True)
    negative = -1.0 / total
    grads[0] = weights[S - 1] * negative
    for m in range(S):
        crossing = jnp.sum(jnp.where(places > m, weights[m], 0.0), axis=0, keepdims=True)
        grads[1, m : m + 1, :] = crossing * negative
    split = own_half_ref.shape[1]
    own_columns = pl.ds(pl.multiple_of(core * split, split), split)
    far_columns = pl.ds(pl.multiple_of((1 - core) * split, split), split)
    joined[:, own_columns] = own_half_ref[...]
    joined[:, far_columns] = far_half_ref[...]
    for step in range(STEPS):
        gradient_step(
            step, core, starts_ref, lps_ref, label_ref, joined, hidden_ref, exps_ref, grads,
            enc_sum, pred_sum, weight_sum,
        )
    grad_enc_ref[...] = jnp.transpose(enc_sum[...]).astype(BF16)
    weight_ref[...] = weight_sum[:, own_columns]
    send_ref[:width, :] = weight_sum[:, far_columns].astype(BF16)
    for i in range(2):
        rows, columns = slice(i * PRED_PAD, (i + 1) * PRED_PAD), slice(i * split, (i + 1) * split)
        pred_ref[rows, :] = pred_sum[:PRED_PAD, columns]
        send_ref[width + i * PRED_PAD : width + (i + 1) * PRED_PAD, :] = pred_sum[PRED_PAD:, columns].astype(BF16)


def gradient_step(
    step, core, starts_ref, lps_ref, label_ref, joined, hidden_ref, exps_ref, grads,
    enc_sum, pred_sum, weight_sum,
):
    half = starts_ref.shape[1]
    here = slice(step * WIDE, (step + 1) * WIDE)

    def wide(ref, *lead):
        return jnp.concatenate(
            [ref[(*lead, slice(step * GROUP + k, step * GROUP + k + 1))] for k in range(GROUP)], axis=1
        )

    names = wide(label_ref)
    grad_blank = wide(grads, 0)
    grad_emit = wide(grads, 1)
    spread = (grad_blank + grad_emit) * wide(lps_ref, 2)
    padded = exps_ref.shape[0]
    ids = row_ids((padded, WIDE))
    coeff = jnp.where(ids == names, grad_emit, 0.0)
    head = coeff[:8] + jnp.where(row_ids((8, WIDE)) == 0, grad_blank, 0.0)
    coeff = jnp.concatenate([head, coeff[8:]], axis=0)
    grad_logits = (coeff - exps_ref[:, here] * spread).astype(BF16)
    grad_hidden = jnp.dot(joined[...], grad_logits, preferred_element_type=F32)
    hidden = hidden_ref[:, here]
    hidden_wide = hidden.astype(F32)
    grad_summed = grad_hidden * (1.0 - hidden_wide * hidden_wide)
    enc_term = balanced(jnp.add, [grad_summed[:, k * LANES : (k + 1) * LANES] for k in range(GROUP)])
    enc_sum[...] = enc_term if step == 0 else enc_sum[...] + enc_term
    starts = rows_to_lanes(starts_ref[...])
    base = starts + step * GROUP
    rows = jnp.concatenate([base + k for k in range(GROUP)], axis=1)
    second = jnp.concatenate([per_lane(half, 0, 1)] * GROUP, axis=1)
    slot = row_ids((2 * PRED_PAD, WIDE))
    match = (slot % PRED_PAD == rows) & ((slot // PRED_PAD + core) % 2 == second)
    pred_term = lax.dot_general(
        match.astype(BF16), grad_summed.astype(BF16), NT_DIMS, preferred_element_type=F32
    )
    pred_sum[...] = pred_term if step == 0 else pred_sum[...] + pred_term
    weight_term = lax.dot_general(hidden, grad_logits, NT_DIMS, preferred_element_type=F32)
    weight_sum[...] = weight_term if step == 0 else weight_sum[...] + weight_term


def params():
    return pltpu.CompilerParams(dimension_semantics=("arbitrary",), vmem_limit_bytes=VMEM_BYTES)


def whole(shape):
    return pl.BlockSpec(shape, lambda i: (0,) * len(shape))


smem = pl.BlockSpec(memory_space=pltpu.SMEM)
vmem = pl.BlockSpec(memory_space=pltpu.VMEM)


def exchange(blocks, axes):
    return lax.all_to_all(blocks, axes, 0, 0, tiled=True)


def share_copies(block, axes):
    count = lax.axis_size(axes)
    return exchange(jnp.broadcast_to(block[None], (count, *block.shape)), axes)


def tm_flip(block, turn):
    return lax.ppermute(block, TM, [(i ^ turn, i) for i in range(lax.axis_size(TM))])


def per_device(encoder, predictor, starts, frame_lengths, label_lengths, labels, w_out):
    utt_count, frame_count, width = encoder.shape
    own_rows, vocab = w_out.shape
    label_rows = predictor.shape[1]
    tm_index = lax.axis_index(TM)
    tm_count = lax.axis_size(TM)
    utt_size = lax.axis_size(UTT)
    core = tm_index & 1
    padded = -(-vocab // 256) * 256
    split = padded // 2
    rows = S * utt_count * frame_count
    shape = jax.ShapeDtypeStruct

    mine = lax.dynamic_slice_in_dim(jnp.pad(w_out, ((0, 0), (0, padded - vocab))), core * split, split, axis=1)
    own_half = share_copies(mine, UTT).reshape(width, split)
    meta = jnp.concatenate([tm_index.reshape(1).astype(jnp.int32), frame_lengths, label_lengths])

    hidden, label_ids = pl.pallas_call(
        hidden_kernel,
        grid=(STEPS,),
        in_specs=[
            smem,
            whole(starts.shape),
            whole(labels.shape),
            whole((utt_count * frame_count, width)),
            whole(predictor.shape),
        ],
        out_specs=[pl.BlockSpec((width, WIDE), lambda i: (0, i)), whole((S, LANES))],
        out_shape=[shape((width, rows), BF16), shape((S, LANES), jnp.int32)],
        scratch_shapes=[
            pltpu.VMEM((width, LANES), F32),
            pltpu.VMEM((width, 2 * PRED_PAD), BF16),
            pltpu.VMEM((2 * PRED_PAD, width), F32),
        ],
        compiler_params=params(),
        cost_estimate=pl.CostEstimate(
            flops=2 * 2 * PRED_PAD * width * rows, bytes_accessed=3 * 2**20, transcendentals=width * rows
        ),
    )(meta, starts, labels, encoder.reshape(-1, width), predictor)

    own_half, hidden = lax.optimization_barrier((own_half, hidden))
    far_half = tm_flip(own_half, 1)
    levels = frame_count.bit_length() - 1
    exps, lps, tree, payload = pl.pallas_call(
        functools.partial(forward_kernel, vocab),
        in_specs=[vmem, smem] + [vmem] * 4,
        out_specs=[vmem] * 4,
        out_shape=[
            shape((padded, rows), F32),
            shape((3, S, LANES), F32),
            shape((levels, S, S, LANES), F32),
            shape((8, LANES), F32),
        ],
        scratch_shapes=[
            pltpu.VMEM((padded, width), BF16),
            pltpu.VMEM((S, S, LANES), F32),
        ],
        compiler_params=pltpu.CompilerParams(vmem_limit_bytes=VMEM_BYTES),
        cost_estimate=pl.CostEstimate(
            flops=2 * padded * width * rows, bytes_accessed=8 * 2**20, transcendentals=padded * rows
        ),
    )(starts, meta, label_ids, own_half, far_half, hidden)

    blocks = share_copies(payload, TM)

    losses, grad_encoder, weight_own, pred_own, send = pl.pallas_call(
        backward_kernel,
        in_specs=[vmem, smem] + [vmem] * 8,
        out_specs=[smem] + [vmem] * 4,
        out_shape=[
            shape((utt_count,), F32),
            shape((utt_count * frame_count, width), BF16),
            shape((width, split), F32),
            shape((2 * PRED_PAD, split), F32),
            shape((width + 2 * PRED_PAD, split), BF16),
        ],
        scratch_shapes=[
            pltpu.VMEM((S, S, LANES), F32),
            pltpu.VMEM((2, LANES, LANES), F32),
            pltpu.VMEM((S, LANES), F32),
            pltpu.VMEM((2, S, LANES), F32),
            pltpu.VMEM((width, LANES), F32),
            pltpu.VMEM((2 * PRED_PAD, width), F32),
            pltpu.VMEM((width, padded), F32),
            pltpu.VMEM((width, padded), BF16),
        ],
        compiler_params=pltpu.CompilerParams(vmem_limit_bytes=VMEM_BYTES),
        cost_estimate=pl.CostEstimate(
            flops=6 * padded * width * rows, bytes_accessed=8 * 2**20, transcendentals=2**16
        ),
    )(starts, meta, blocks, lps, tree, label_ids, own_half, far_half, hidden, exps)

    came = tm_flip(send, 1)
    weight_half = (weight_own + came[:width].astype(F32)).astype(BF16).reshape(utt_size, own_rows, split)
    pred_own = pred_own + came[width:].astype(F32)
    weight_half, pred_own = lax.optimization_barrier((weight_half, pred_own))
    weight_rows = jnp.sum(exchange(weight_half, UTT).astype(F32), axis=0)
    for turn in (2, 4):
        pred_own = pred_own + tm_flip(pred_own.astype(BF16), turn).astype(F32)
    pred_far = tm_flip(pred_own, 1)
    pred_pair = jnp.stack([jnp.where(core == 1, pred_far, pred_own), jnp.where(core == 1, pred_own, pred_far)])
    pred_pair = pred_pair.reshape(utt_count, 2, PRED_PAD, split)[:, :, :label_rows]
    grad_predictor = jnp.concatenate([pred_pair[:, 0], pred_pair[:, 1]], axis=-1)
    final = share_copies(weight_rows, TM).reshape(tm_count // 2, 2, own_rows, split)
    final = jnp.sum(final, axis=0)
    grad_w_out = jnp.concatenate([final[0], final[1]], axis=-1)[:, :vocab]
    return (losses, grad_encoder.reshape(encoder.shape), grad_predictor, grad_w_out)


def solution(mesh):
    return jax.shard_map(
        per_device,
        mesh=mesh,
        in_specs=(
            P(UTT, TM, None),
            P(UTT, None, None),
            P(UTT, TM),
            P(UTT),
            P(UTT),
            P(UTT, None),
            P(UTT, None),
        ),
        out_specs=(P(UTT), P(UTT, TM, None), P(UTT, None, None), P(UTT, None)),
        check_vma=False,
    )
```
